32 devices in a mesh: utt: 4 (over y, core), seq: 8 (over z, x).
Axes of the slice: x: 2, y: 2, z: 4, core: 2. Of those that a mesh axis runs over, the one named last changes fastest.
Arguments:
- inputs: bfloat16 [5632, 1024], P(('utt', 'seq')), may hold values from -6 to 6
- skip_in: bfloat16 [5632, 1024], P(('utt', 'seq')), may hold values from -6 to 6
- lengths: int32 [4, 6], P('utt'), may hold values from 1 to 1320, as said below
- cotangent: bfloat16 [5632, 1024], P(('utt', 'seq')), may hold values from -6 to 6
- w_skip: bfloat16 [2048, 1024], replicated, may hold values from -0.125 to 0.125
- gain_one: float32 [1024], replicated, may hold values from 0.25 to 1.75
- w_qkv: bfloat16 [1024, 3072], replicated, may hold values from -0.1875 to 0.1875
- w_out: bfloat16 [1024, 1024], replicated, may hold values from -3 to 3
- gain_two: float32 [1024], replicated, may hold values from 0.25 to 1.75
- w_up: bfloat16 [1024, 4096], replicated, may hold values from -0.1875 to 0.1875
- b_up: float32 [4096], replicated, may hold values from -3 to 3
- w_down: bfloat16 [4096, 1024], replicated, may hold values from -0.09375 to 0.09375
- b_down: float32 [1024], replicated, may hold values from -3 to 3
Outputs:
- result: bfloat16 [5632, 1024], P(('utt', 'seq'))
- d_inputs: bfloat16 [5632, 1024], P(('utt', 'seq'))
- d_skip: bfloat16 [5632, 1024], P(('utt', 'seq'))
- g_w_skip: float32 [2048, 1024], P('seq')
- g_gain_one: float32 [1024], replicated
- g_w_qkv: float32 [1024, 3072], P('seq')
- g_w_out: float32 [1024, 1024], P('seq')
- g_gain_two: float32 [1024], replicated
- g_w_up: float32 [1024, 4096], P('seq')
- g_b_up: float32 [4096], replicated
- g_w_down: float32 [4096, 1024], P('seq')
- g_b_down: float32 [1024], replicated
The draws below stay inside these ranges and needn't reach their ends.
Inputs may be any that keep to these rules, and one draw needn't show every extreme that they name: In each group the lengths sum to 1408; exactly one of them, at a slot drawn from the seed, is 1320, and the others sum to 88.
All inputs are finite; a program needn't handle non-finite values.
Results may differ from the reference program's by a relative error of at most 0.02.
Values may be sent and summed in bfloat16 or wider, within the bound.
A program may use at most 192 MiB of HBM per device.

```python
import math
import jax
import jax.numpy as jnp
from jax import lax

D = 1024
FF = 4096
HEADS = 16
HEAD_DIM = 64
TOK_DEV = 176
UTTS = 6
TOKENS = 5632
N_UTT = 4
N_SEQ = 8


def draw_lengths(key, part):
    key = jax.random.fold_in(key, 11)
    remainder = TOK_DEV // 2
    longest = TOK_DEV * N_SEQ - remainder
    group_keys = jax.random.split(key, N_UTT)

    def one_group(group_key):
        cut_key, order_key = jax.random.split(group_key)
        cut_points = jnp.sort(jax.random.permutation(cut_key, remainder - 1)[:UTTS - 2] + 1).astype(jnp.int32)
        boundary = jnp.concatenate([jnp.zeros((1,), jnp.int32), cut_points, jnp.full((1,), remainder, jnp.int32)])
        short_ones = boundary[1:] - boundary[:-1]
        lengths_all = jnp.concatenate([jnp.full((1,), longest, jnp.int32), short_ones])
        return lengths_all[jax.random.permutation(order_key, UTTS)]
    return jax.vmap(one_group)(group_keys)


def level_of(key, extent, shards, smallest, largest):
    loudness = 1.0
    for position, parts in shards:
        steps = jax.random.uniform(jax.random.fold_in(jax.random.fold_in(key, 6), position), (parts,), jnp.float32, smallest / len(shards), largest / len(shards))
        loudness = loudness * jnp.repeat(jnp.exp(steps), extent[position] // parts).reshape((-1,) + (1,) * (len(extent) - 1 - position))
    return loudness


def noise(own_key, extent, width, most, shards=(), kind=jnp.bfloat16):
    entries = width * jax.random.normal(own_key, extent, jnp.float32)
    if shards:
        entries = entries * level_of(own_key, extent, shards, -0.22, 0.18)
    return jnp.clip(entries, -most, most).astype(kind)


def setup_inputs(seed: int = 0) -> dict:
    key_list = jax.random.split(jax.random.key(seed), 14)
    inputs = noise(key_list[0], (TOKENS, D), 1.0, 6.0, ((0, 32),))
    skip_in = noise(key_list[1], (TOKENS, D), 1.0, 6.0, ((0, 32),))
    lengths = draw_lengths(jax.random.fold_in(key_list[13], 71), 0)
    cotangent = noise(key_list[3], (TOKENS, D), 1.0, 6.0, ((0, 32),))
    w_skip = noise(key_list[4], (2 * D, D), (2 * D) ** -0.5, 0.125)
    gain_one = jnp.clip(1.0 + 0.15 * jax.random.normal(key_list[5], (D,), jnp.float32), 0.25, 1.75)
    w_qkv = noise(key_list[6], (D, 3 * D), D ** -0.5, 0.1875)
    w_out = noise(key_list[7], (D, D), (max(1, D // 256)) ** -0.5, 3.0)
    gain_two = jnp.clip(1.0 + 0.15 * jax.random.normal(key_list[8], (D,), jnp.float32), 0.25, 1.75)
    w_up = noise(key_list[9], (D, FF), D ** -0.5, 0.1875)
    b_up = noise(key_list[10], (FF,), 0.5, 3.0, (), jnp.float32)
    w_down = noise(key_list[11], (FF, D), FF ** -0.5, 0.09375)
    b_down = noise(key_list[12], (D,), 0.5, 3.0, (), jnp.float32)
    return {"inputs": inputs, "skip_in": skip_in, "lengths": lengths, "cotangent": cotangent, "w_skip": w_skip, "gain_one": gain_one, "w_qkv": w_qkv, "w_out": w_out, "gain_two": gain_two, "w_up": w_up, "b_up": b_up, "w_down": w_down, "b_down": b_down}


@jax.custom_vjp
def low(v):
    return lax.optimization_barrier(v.astype(jnp.bfloat16)).astype(jnp.float32)

@jax.custom_vjp
def low_back(v):
    return v

def low_keep(v):
    return (low(v), None)

def low_pass(kept, grad):
    return (grad,)

def back_keep(v):
    return (v, None)

def back_low(kept, grad):
    return (low(grad),)
low.defvjp(low_keep, low_pass)
low_back.defvjp(back_keep, back_low)
EPSILON = 1e-06
HIGHEST = lax.Precision.HIGHEST

def rms_scale(hidden, gain_vec):
    return hidden * lax.rsqrt(lax.optimization_barrier(jnp.mean(hidden * hidden, axis=-1, keepdims=True)) + EPSILON) * gain_vec

def gelu_exact(values_in):
    return 0.5 * values_in * (1.0 + jax.scipy.special.erf(values_in * 0.7071067811865476))

def rotate(values_in, cosine_table, sine_table):
    half_size = values_in.shape[-1] // 2
    front_half = values_in[..., :half_size]
    back_half = values_in[..., half_size:]
    return jnp.concatenate([front_half * cosine_table - back_half * sine_table, back_half * cosine_table + front_half * sine_table], axis=-1)

def frame_segments(own_lengths, positions):
    ends_at = jnp.cumsum(own_lengths).astype(jnp.int32)
    starts_at = (ends_at - own_lengths).astype(jnp.int32)
    segment = lax.optimization_barrier(jnp.sum((positions[:, None] >= ends_at[None, :]).astype(jnp.int32), axis=1)).astype(jnp.int32)
    slots = jnp.arange(own_lengths.shape[0], dtype=jnp.int32)
    offset = lax.optimization_barrier(jnp.sum(jnp.where(segment[:, None] == slots[None, :], starts_at[None, :], 0), axis=1)).astype(jnp.int32)
    return (segment, (positions - offset).astype(jnp.int32))

def rotary_tables(places, head_size):
    freqs = jnp.exp(jnp.arange(head_size // 2, dtype=jnp.float32) * (-2.0 * math.log(10000.0) / head_size))
    angles = places.astype(jnp.float32)[:, None] * freqs[None, :]
    return (jnp.cos(angles)[:, None, :], jnp.sin(angles)[:, None, :])

def block_attention(query_block, keys_all, values_all, segment_query, segment_keys):
    scale = query_block.shape[-1] ** (-0.5)
    scores = jnp.einsum('qhd,khd->hqk', query_block, keys_all, precision=HIGHEST) * scale
    scores = low_back(scores)
    same = segment_query[:, None] == segment_keys[None, :]
    scores = jnp.where(same[None], scores, -1e+30)
    top_score = lax.optimization_barrier(jnp.max(scores, axis=-1, keepdims=True))
    expos = jnp.exp(scores - top_score)
    probs = low(expos / lax.optimization_barrier(jnp.sum(expos, axis=-1, keepdims=True)))
    mixed = jnp.einsum('hqk,khd->qhd', probs, values_all, precision=HIGHEST)
    return low(low_back(mixed))

def group_layer(inputs_group, skip_group, segment, cosine_table, sine_table, params):
    w_skip, gain_one, w_qkv, w_out, gain_two, w_up, b_up, w_down, b_down = params
    frames = inputs_group.shape[0]
    joined = jnp.concatenate([inputs_group, skip_group], axis=1)
    entry = low_back(jnp.dot(joined, w_skip, precision=HIGHEST))
    normed_one = low(rms_scale(entry, gain_one))
    qkv = low_back(jnp.dot(normed_one, w_qkv, precision=HIGHEST))
    query = qkv[:, :D].reshape(frames, HEADS, HEAD_DIM)
    keys_all = qkv[:, D:2 * D].reshape(frames, HEADS, HEAD_DIM)
    values_all = low(low_back(qkv[:, 2 * D:].reshape(frames, HEADS, HEAD_DIM)))
    query = low(low_back(rotate(query, cosine_table, sine_table)))
    keys_all = low(low_back(rotate(keys_all, cosine_table, sine_table)))
    block_rows = math.gcd(frames, 512)
    block_count = frames // block_rows

    def one_block(item):
        return block_attention(item[0], keys_all, values_all, item[1], segment)
    mixed = lax.map(jax.checkpoint(one_block), (query.reshape(block_count, block_rows, HEADS, HEAD_DIM), segment.reshape(block_count, block_rows)))
    mixed = mixed.reshape(frames, D)
    middle = entry + low_back(jnp.dot(mixed, w_out, precision=HIGHEST))
    normed_two = low(rms_scale(middle, gain_two))
    up_values = low_back(jnp.dot(normed_two, w_up, precision=HIGHEST) + b_up)
    active = low(gelu_exact(up_values))
    return middle + low_back(jnp.dot(active, w_down, precision=HIGHEST) + b_down)

def reference(inputs, skip_in, lengths, cotangent, w_skip, gain_one, w_qkv, w_out, gain_two, w_up, b_up, w_down, b_down):
    group_count = lengths.shape[0]
    frames = inputs.shape[0] // group_count
    positions = jnp.arange(frames, dtype=jnp.int32)

    def tables(own_lengths):
        segment, places = frame_segments(own_lengths, positions)
        cosine_table, sine_table = rotary_tables(places, HEAD_DIM)
        return (segment, cosine_table, sine_table)
    segments, cosines, sines = jax.vmap(tables)(lengths)
    floats = tuple((item.astype(jnp.float32) for item in (inputs, skip_in, w_skip, gain_one, w_qkv, w_out, gain_two, w_up, b_up, w_down, b_down)))

    def forward(inputs_all, skip_all, *params):

        def per_group(item):
            return group_layer(item[0], item[1], item[2], item[3], item[4], params)
        outputs = lax.map(per_group, (inputs_all.reshape(group_count, frames, D), skip_all.reshape(group_count, frames, D), segments, cosines, sines))
        return outputs.reshape(group_count * frames, D)
    output, pullback = jax.vjp(forward, *floats)
    grads = pullback(cotangent.astype(jnp.float32))
    return (output.astype(jnp.bfloat16), grads[0].astype(jnp.bfloat16), grads[1].astype(jnp.bfloat16), grads[2], grads[3], grads[4], grads[5], grads[6], grads[7], grads[8], grads[9], grads[10])
```

```python
import functools
import math

import jax
import jax.numpy as jnp
from jax import lax
from jax.experimental import pallas as pl
from jax.experimental.pallas import tpu as pltpu
from jax.sharding import Mesh, PartitionSpec as P

HEAD_DIM = 64
EPSILON = 1e-06
BF = jnp.bfloat16
F32 = jnp.float32
AXES = ("u", "z", "x")
PLANE = ("u", "x")


def dot_nn(a, b):
    return lax.dot_general(a, b, (((1,), (0,)), ((), ())), preferred_element_type=F32)


def dot_nt(a, b):
    return lax.dot_general(a, b, (((1,), (1,)), ((), ())), preferred_element_type=F32)


def dot_tn(a, b):
    return lax.dot_general(a, b, (((0,), (0,)), ((), ())), preferred_element_type=F32)


def attention_forward(q_ref, k_ref, v_ref, col_ref, row_ref, o_ref, lse_ref, acc, out_t):
    frames, width = q_ref.shape
    heads = width // HEAD_DIM
    block = frames // (frames // 352)
    lane = lax.broadcasted_iota(jnp.int32, (1, width), 1)
    segment_row = row_ref[...]
    for h in range(heads):
        own = (lane // HEAD_DIM == h).astype(BF)
        query = q_ref[...] * own
        acc[...] = jnp.zeros_like(acc)

        def step(j, carry):
            top, total = carry
            rows = pl.ds(pl.multiple_of(j * block, block), block)
            scores = dot_nt(k_ref[rows, :], query)
            scores = jnp.where(col_ref[rows, :] == segment_row, scores, -1e30)
            peak = jnp.maximum(top, jnp.max(scores, axis=0, keepdims=True))
            expos = jnp.exp(scores - peak)
            shrink = jnp.exp(top - peak)
            acc[...] = acc[...] * shrink + dot_tn(v_ref[rows, :], expos.astype(BF))
            return peak, total * shrink + jnp.sum(expos, axis=0, keepdims=True)

        top, total = lax.fori_loop(
            0,
            frames // block,
            step,
            (jnp.full((1, frames), -1e30, F32), jnp.zeros((1, frames), F32)),
        )
        part = slice(h * HEAD_DIM, (h + 1) * HEAD_DIM)
        out_t[part, :] = acc[part, :] / total
        lse_ref[h : h + 1, :] = top + jnp.log(total)
    o_ref[...] = out_t[...].T.astype(BF)


def attention_backward(
    q_ref, k_ref, v_ref, o_ref, do_ref, col_ref, row_ref, lse_ref, dq_ref, dk_ref, dv_ref, acc
):
    frames, width = q_ref.shape
    heads = width // HEAD_DIM
    block = frames // (frames // 352)
    lane = lax.broadcasted_iota(jnp.int32, (1, width), 1)
    segment_row = row_ref[...]
    product_t = (o_ref[...].astype(F32) * do_ref[...].astype(F32)).T
    for h in range(heads):
        own = (lane // HEAD_DIM == h).astype(BF)
        query = q_ref[...] * own
        grad = do_ref[...] * own
        part = slice(h * HEAD_DIM, (h + 1) * HEAD_DIM)
        delta = jnp.sum(product_t[part, :], axis=0, keepdims=True)
        log_total = lse_ref[h : h + 1, :]

        def step(j, _):
            rows = pl.ds(pl.multiple_of(j * block, block), block)
            keys = k_ref[rows, :]
            scores = dot_nt(keys, query)
            same = col_ref[rows, :] == segment_row
            probs = jnp.where(same, jnp.exp(scores - log_total), 0.0)
            d_probs = dot_nt(v_ref[rows, :], grad)
            d_scores = (probs * (d_probs - delta)).astype(BF)
            value_part = dot_nn(probs.astype(BF), grad)
            key_part = dot_nn(d_scores, query)
            if h == 0:
                dv_ref[rows, :] = value_part
                dk_ref[rows, :] = key_part
            else:
                dv_ref[rows, :] += value_part
                dk_ref[rows, :] += key_part
            query_part = dot_tn(keys * own, d_scores)

            if h == 0:

                @pl.when(j == 0)
                def _():
                    acc[...] = query_part

                @pl.when(j > 0)
                def _():
                    acc[...] += query_part

            else:
                acc[...] += query_part
            return 0

        lax.fori_loop(0, frames // block, step, 0)
    dq_ref[...] = acc[...].T * (HEAD_DIM**-0.5)


def call_forward(query, keys, values, col, row):
    frames, width = query.shape
    return pl.pallas_call(
        attention_forward,
        out_shape=(
            jax.ShapeDtypeStruct((frames, width), BF),
            jax.ShapeDtypeStruct((width // HEAD_DIM, frames), F32),
        ),
        scratch_shapes=[pltpu.VMEM((width, frames), F32), pltpu.VMEM((width, frames), F32)],
        compiler_params=pltpu.CompilerParams(vmem_limit_bytes=56 * 2**20),
        cost_estimate=pl.CostEstimate(
            flops=16 * frames * frames * width, bytes_accessed=10 * frames * width, transcendentals=0
        ),
        name="attention_forward",
    )(query, keys, values, col, row)


def call_backward(query, keys, values, mixed, grad, col, row, lse):
    frames, width = query.shape
    shape = jax.ShapeDtypeStruct((frames, width), F32)
    return pl.pallas_call(
        attention_backward,
        out_shape=(shape, shape, shape),
        scratch_shapes=[pltpu.VMEM((width, frames), F32)],
        compiler_params=pltpu.CompilerParams(vmem_limit_bytes=56 * 2**20),
        cost_estimate=pl.CostEstimate(
            flops=32 * frames * frames * width, bytes_accessed=20 * frames * width, transcendentals=0
        ),
        name="attention_backward",
    )(query, keys, values, mixed, grad, col, row, lse)


def frame_segments(own_lengths, positions):
    slots = own_lengths.shape[0]
    upto = jnp.arange(slots)[:, None] >= jnp.arange(slots)[None, :]
    ends_at = jnp.sum(jnp.where(upto, own_lengths[None, :], 0), axis=1)
    starts_at = ends_at - own_lengths
    segment = jnp.sum((positions[:, None] >= ends_at[None, :]).astype(jnp.int32), axis=1)
    index = jnp.arange(slots, dtype=jnp.int32)
    offset = jnp.sum(jnp.where(segment[:, None] == index[None, :], starts_at[None, :], 0), axis=1)
    return segment, positions - offset


def rotary_tables(places):
    freqs = jnp.exp(
        jnp.arange(HEAD_DIM // 2, dtype=F32) * (-2.0 * math.log(10000.0) / HEAD_DIM)
    )
    angles = places.astype(F32)[:, None] * freqs[None, :]
    cosine, sine = jnp.cos(angles), jnp.sin(angles)
    return (
        jnp.concatenate([cosine, cosine], axis=1)[:, None, :],
        jnp.concatenate([-sine, sine], axis=1)[:, None, :],
    )


def rotate(v, tables, sign):
    frames, width = v.shape
    shaped = v.reshape(frames, width // HEAD_DIM, HEAD_DIM)
    half = HEAD_DIM // 2
    swapped = jnp.concatenate([shaped[..., half:], shaped[..., :half]], axis=-1)
    return (shaped * tables[0] + swapped * (sign * tables[1])).reshape(frames, width)


def rms_parts(hidden):
    return lax.rsqrt(jnp.mean(hidden * hidden, axis=-1, keepdims=True) + EPSILON)


def rms_back(hidden, inverse, gain, grad):
    scaled = hidden * inverse
    weighted = grad * gain
    inner = jnp.mean(weighted * scaled, axis=-1, keepdims=True)
    return inverse * (weighted - scaled * inner), jnp.sum(grad * scaled, axis=0)


def gelu_both(t):
    bell = 0.5 * (1.0 + lax.erf(t * 0.7071067811865476))
    return t * bell, bell + t * (0.3989422804014327 * jnp.exp(-0.5 * t * t))


def local(
    sizes,
    inputs,
    skip_in,
    lengths,
    cotangent,
    w_skip,
    gain_one,
    w_qkv,
    w_out,
    gain_two,
    w_up,
    b_up,
    w_down,
    b_down,
):
    n_u, n_z, n_x = sizes
    frames, d = inputs.shape
    hidden = w_up.shape[1]
    parts = n_u * n_x
    group = frames * parts
    u, z, x = (lax.axis_index(a) for a in AXES)
    me = u * n_x + x
    width = d // parts

    def line(a, b, c):
        return (a * n_z + b) * n_x + c

    def permute(v, to):
        pairs = [
            (line(a, b, c), line(*to(a, b, c)))
            for a in range(n_u)
            for b in range(n_z)
            for c in range(n_x)
        ]
        return lax.ppermute(v, AXES, pairs)

    def plane_of(a):
        return (a % 2) * (n_u // 2) + a // 2

    group_of = {plane_of(a): a for a in range(n_u)}

    def away(v):
        return permute(v, lambda a, b, c: (b, plane_of(a), c))

    def home(v):
        return permute(v, lambda a, b, c: (group_of[b], a, c))

    def swap_plane(v, bit):
        def to(a, b, c):
            other = (a * n_x + c) ^ bit
            return other // n_x, b, other % n_x

        return permute(v, to)

    plane_bits = [1 << i for i in range(parts.bit_length() - 1)]
    if n_x == 2 and n_u == 4:
        orders = ([1, 4, 2], [4, 1, 2])
    else:
        orders = (plane_bits, plane_bits)
    cut = frames // 32 * 16

    def gather_plane(v):
        pieces = []
        for piece, order in zip((v[:cut], v[cut:]), orders):
            for bit in order:
                piece = jnp.concatenate([piece, swap_plane(piece, bit)], axis=0)
            pieces.append(piece)
        return jnp.concatenate(pieces, axis=0)

    def gather_order(v):
        pieces = []
        for start, size, order in ((0, cut, orders[0]), (cut, frames - cut, orders[1])):
            offsets = [0]
            for bit in order:
                offsets = offsets + [o ^ bit for o in offsets]
            for o in offsets:
                pieces.append(
                    lax.dynamic_slice_in_dim(v, (me ^ o) * frames + start, size, axis=0)
                )
        return jnp.concatenate(pieces, axis=0)

    z_bits = n_z.bit_length() - 1

    def reduce_z(v):
        rest = v.shape[1:]
        v = v.reshape((2,) * z_bits + (v.shape[0] // n_z,) + rest)
        for bit in range(z_bits):
            axis = z_bits - 1 - bit
            own = (z >> bit) & 1
            keep = lax.dynamic_index_in_dim(v, own, axis, keepdims=False)
            give = lax.dynamic_index_in_dim(v, 1 - own, axis, keepdims=False)
            got = permute(
                give.astype(BF), lambda a, b, c, bit=bit: (a, b ^ (1 << bit), c)
            )
            v = keep.astype(F32) + got.astype(F32)
            if bit < z_bits - 1:
                v = v.astype(BF)
        return v.astype(BF)

    def finish_columns(v):
        if n_x == 2:
            v = v.reshape((2, v.shape[0] // 2) + v.shape[1:])
            keep = lax.dynamic_index_in_dim(v, x, 0, keepdims=False)
            give = lax.dynamic_index_in_dim(v, 1 - x, 0, keepdims=False)
            got = permute(give, lambda a, b, c: (a, b, 1 - c))
            both = jnp.where(x == 0, jnp.stack([keep, got]), jnp.stack([got, keep]))
        else:
            both = v[None]
        every = lax.all_gather(both, "u", axis=0)
        return every.reshape((parts,) + both.shape[1:])

    def sum_all(v):
        total = n_u * n_z * n_x
        for i in range(total.bit_length() - 1):
            bit = 1 << i
            pairs = [(n, n ^ bit) for n in range(total)]
            v = v + lax.ppermute(v, AXES, pairs)
        return v

    entry_home = dot_nn(inputs, w_skip[:d]) + dot_nn(skip_in, w_skip[d:])
    entry = away(entry_home.astype(BF)).astype(F32)
    group_lengths = away(lengths)[0]
    grad_low = away(cotangent)
    inputs_away = away(inputs)
    skip_away = away(skip_in)

    segment, places = frame_segments(group_lengths, jnp.arange(group, dtype=jnp.int32))
    own_places = lax.dynamic_slice_in_dim(places, me * frames, frames)
    tables = rotary_tables(own_places)
    col, row = segment[:, None], segment[None, :]

    inverse_one = rms_parts(entry)
    normed_one = (entry * inverse_one * gain_one).astype(BF)
    qkv = dot_nn(normed_one, w_qkv)
    query = (rotate(qkv[:, :d], tables, 1.0)).astype(BF) * BF(HEAD_DIM**-0.5)
    keys = rotate(qkv[:, d : 2 * d], tables, 1.0).astype(BF)
    values = qkv[:, 2 * d :].astype(BF)

    def to_heads(*arrays):
        n = len(arrays)
        v = jnp.stack([a.reshape(frames, parts, width) for a in arrays], axis=2)
        v = lax.all_to_all(
            v.reshape(frames, parts * n * width), PLANE, split_axis=1, concat_axis=0, tiled=True
        )
        return [v[:, i * width : (i + 1) * width] for i in range(n)]

    def to_frames(*arrays):
        n = len(arrays)
        v = jnp.concatenate(arrays, axis=1)
        v = lax.all_to_all(v, PLANE, split_axis=0, concat_axis=1, tiled=True)
        v = v.reshape(frames, parts, n, width)
        return [v[:, :, i].reshape(frames, d) for i in range(n)]

    head_query, head_keys, head_values = to_heads(query, keys, values)
    head_mixed, lse = call_forward(head_query, head_keys, head_values, col, row)
    (mixed,) = to_frames(head_mixed)

    middle = entry + dot_nn(mixed, w_out)
    inverse_two = rms_parts(middle)
    normed_two = (middle * inverse_two * gain_two).astype(BF)
    up = dot_nn(normed_two, w_up) + b_up
    d_active = dot_nt(grad_low, w_down)
    active, slope = gelu_both(up)
    d_up = (d_active * slope).astype(BF)
    result_away = (middle + dot_nn(active.astype(BF), w_down) + b_down).astype(BF)
    result = home(result_away)
    d_normed_two = dot_nt(d_up, w_up)
    middle_part, g_gain_two = rms_back(middle, inverse_two, gain_two, d_normed_two)
    d_middle = grad_low.astype(F32) + middle_part
    d_branch = d_middle.astype(BF)
    d_mixed = dot_nt(d_branch, w_out).astype(BF)
    (head_grad,) = to_heads(d_mixed)
    dq, dk, dv = call_backward(
        head_query, head_keys, head_values, head_mixed, head_grad, col, row, lse
    )

    chunk = hidden // (n_z * parts)
    w_up_own = lax.dynamic_slice(
        w_up.reshape(d, n_z, n_x, n_u, chunk), (0, 0, x, u, 0), (d, n_z, 1, 1, chunk)
    ).reshape(d, n_z * chunk)
    w_down_own = lax.dynamic_slice(
        w_down.reshape(n_z, n_x, n_u, chunk, d), (0, x, u, 0, 0), (n_z, 1, 1, chunk, d)
    ).reshape(n_z * chunk, d)
    b_up_own = lax.dynamic_slice(
        b_up.reshape(n_z, n_x, n_u, chunk), (0, x, u, 0), (n_z, 1, 1, chunk)
    ).reshape(n_z * chunk)
    plane_grad = gather_plane(grad_low)
    plane_normed = gather_plane(normed_two)
    up_own = dot_nn(plane_normed, w_up_own) + b_up_own
    active_own, slope_own = gelu_both(up_own)
    d_up_own = (dot_nt(plane_grad, w_down_own) * slope_own).astype(BF)
    g_down = dot_tn(active_own.astype(BF), plane_grad)
    g_up = dot_tn(plane_normed, d_up_own)
    down_z = reduce_z(g_down.astype(BF))
    up_z = reduce_z(g_up.astype(BF))
    out_down = lax.all_gather(down_z, "u", axis=0, tiled=True).astype(F32)
    out_up = finish_columns(up_z)
    out_up = (
        out_up.reshape(n_u, n_x, -1, n_z, chunk).transpose(2, 3, 1, 0, 4).reshape(-1, hidden)
    ).astype(F32)

    plane_mixed = gather_plane(mixed)
    own_branch = gather_order(
        lax.all_to_all(d_branch, PLANE, split_axis=1, concat_axis=0, tiled=True)
    )
    g_out = dot_tn(plane_mixed, own_branch)
    out_out = (
        finish_columns(reduce_z(g_out.astype(BF))).transpose(1, 0, 2).reshape(-1, d).astype(F32)
    )

    low = [a.astype(BF) for a in (dq, dk, dv)]
    frame_query, frame_keys, frame_values = to_frames(*low)
    d_qkv = jnp.concatenate(
        [
            rotate(frame_query.astype(F32), tables, -1.0).astype(BF),
            rotate(frame_keys.astype(F32), tables, -1.0).astype(BF),
            frame_values,
        ],
        axis=1,
    )
    d_normed_one = dot_nt(d_qkv, w_qkv)
    entry_part, g_gain_one = rms_back(entry, inverse_one, gain_one, d_normed_one)
    d_entry = (d_middle + entry_part).astype(BF)
    d_entry_home = home(d_entry)
    d_joined = dot_nt(d_entry_home, w_skip)
    d_inputs = d_joined[:, :d].astype(BF)
    d_skip = d_joined[:, d:].astype(BF)

    group_tables = rotary_tables(places)
    head_d_qkv = jnp.concatenate(
        [
            rotate(low[0].astype(F32), group_tables, -1.0).astype(BF),
            rotate(low[1].astype(F32), group_tables, -1.0).astype(BF),
            low[2],
        ],
        axis=1,
    )
    plane_first = gather_plane(normed_one)
    g_qkv = dot_tn(plane_first, gather_order(head_d_qkv))
    plane_inputs = gather_plane(inputs_away)
    plane_skip = gather_plane(skip_away)
    own_entry = gather_order(
        lax.all_to_all(d_entry, PLANE, split_axis=1, concat_axis=0, tiled=True)
    )
    g_skip = jnp.concatenate([dot_tn(plane_inputs, own_entry), dot_tn(plane_skip, own_entry)])
    out_qkv = finish_columns(reduce_z(g_qkv.astype(BF)))
    out_qkv = (
        out_qkv.reshape(parts, -1, 3, width).transpose(1, 2, 0, 3).reshape(-1, 3 * d).astype(F32)
    )
    out_skip = (
        finish_columns(reduce_z(g_skip.astype(BF))).transpose(1, 0, 2).reshape(-1, d).astype(F32)
    )

    early = sum_all(
        jnp.concatenate(
            [
                g_gain_two,
                jnp.sum(d_up.astype(F32), axis=0),
                jnp.sum(cotangent.astype(F32), axis=0),
            ]
        )
    )
    total_gain_one = sum_all(g_gain_one)
    return (
        result,
        d_inputs,
        d_skip,
        out_skip,
        total_gain_one,
        out_qkv,
        out_out,
        early[:d],
        out_up,
        early[d : d + hidden],
        out_down,
        early[d + hidden :],
    )


def solution(mesh):
    n_u, n_s = mesh.shape["utt"], mesh.shape["seq"]
    sizes = (n_u, n_u, n_s // n_u)
    inner = Mesh(mesh.devices.reshape(sizes), AXES)
    rows, seq = P(AXES, None), P(("z", "x"), None)
    in_specs = (rows, rows, P("u", None), rows) + (P(),) * 9
    out_specs = (rows, rows, rows, seq, P(), seq, seq, P(), seq, P(), seq, P())
    return jax.shard_map(
        functools.partial(local, sizes),
        mesh=inner,
        in_specs=in_specs,
        out_specs=out_specs,
        check_vma=False,
    )
```

```python
import functools
import math

import jax
import jax.numpy as jnp
from jax import lax
from jax.experimental import pallas as pl
from jax.experimental.pallas import tpu as pltpu
from jax.sharding import Mesh, PartitionSpec as P

HEAD_DIM = 64
EPSILON = 1e-06
BF = jnp.bfloat16
F32 = jnp.float32
AXES = ("u", "z", "x")
PLANE = ("u", "x")


def dot_nn(a, b):
    return lax.dot_general(a, b, (((1,), (0,)), ((), ())), preferred_element_type=F32)


def dot_nt(a, b):
    return lax.dot_general(a, b, (((1,), (1,)), ((), ())), preferred_element_type=F32)


def dot_tn(a, b):
    return lax.dot_general(a, b, (((0,), (0,)), ((), ())), preferred_element_type=F32)


def attention_forward(q_ref, k_ref, v_ref, col_ref, row_ref, o_ref, lse_ref, acc, out_t):
    forward_heads(q_ref, k_ref, v_ref, col_ref, row_ref[...], o_ref, lse_ref, acc, out_t)


def forward_heads(q_ref, k_ref, v_ref, col_ref, segment_row, o_ref, lse_ref, acc, out_t):
    frames, width = q_ref.shape
    heads = width // HEAD_DIM
    block = frames // (frames // 352)
    lane = lax.broadcasted_iota(jnp.int32, (1, width), 1)
    for h in range(heads):
        own = (lane // HEAD_DIM == h).astype(BF)
        query = q_ref[...] * own
        acc[...] = jnp.zeros_like(acc)

        def step(j, carry):
            top, total = carry
            rows = pl.ds(pl.multiple_of(j * block, block), block)
            scores = dot_nt(k_ref[rows, :], query)
            scores = jnp.where(col_ref[rows, 0:1] == segment_row, scores, -1e30)
            peak = jnp.maximum(top, jnp.max(scores, axis=0, keepdims=True))
            expos = jnp.exp(scores - peak)
            shrink = jnp.exp(top - peak)
            acc[...] = acc[...] * shrink + dot_tn(v_ref[rows, :], expos.astype(BF))
            return peak, total * shrink + jnp.sum(expos, axis=0, keepdims=True)

        top, total = lax.fori_loop(
            0,
            frames // block,
            step,
            (jnp.full((1, frames), -1e30, F32), jnp.zeros((1, frames), F32)),
        )
        part = slice(h * HEAD_DIM, (h + 1) * HEAD_DIM)
        out_t[part, :] = acc[part, :] / total
        lse_ref[h : h + 1, :] = top + jnp.log(total)
    o_ref[...] = out_t[...].T.astype(BF)


def attention_backward(
    q_ref, k_ref, v_ref, o_ref, do_ref, col_ref, row_ref, lse_ref, dq_ref, dk_ref, dv_ref, acc
):
    backward_heads(
        q_ref, k_ref, v_ref, o_ref, do_ref, col_ref, row_ref[...], lse_ref, dq_ref, dk_ref, dv_ref, acc
    )


def backward_heads(
    q_ref, k_ref, v_ref, o_ref, do_ref, col_ref, segment_row, lse_ref, dq_ref, dk_ref, dv_ref, acc
):
    frames, width = q_ref.shape
    heads = width // HEAD_DIM
    block = frames // (frames // 352)
    lane = lax.broadcasted_iota(jnp.int32, (1, width), 1)
    product_t = (o_ref[...].astype(F32) * do_ref[...].astype(F32)).T
    for h in range(heads):
        own = (lane // HEAD_DIM == h).astype(BF)
        query = q_ref[...] * own
        grad = do_ref[...] * own
        part = slice(h * HEAD_DIM, (h + 1) * HEAD_DIM)
        delta = jnp.sum(product_t[part, :], axis=0, keepdims=True)
        log_total = lse_ref[h : h + 1, :]

        def step(j, _):
            rows = pl.ds(pl.multiple_of(j * block, block), block)
            keys = k_ref[rows, :]
            scores = dot_nt(keys, query)
            same = col_ref[rows, 0:1] == segment_row
            probs = jnp.where(same, jnp.exp(scores - log_total), 0.0)
            d_probs = dot_nt(v_ref[rows, :], grad)
            d_scores = (probs * (d_probs - delta)).astype(BF)
            value_part = dot_nn(probs.astype(BF), grad)
            key_part = dot_nn(d_scores, query)
            if h == 0:
                dv_ref[rows, :] = value_part
                dk_ref[rows, :] = key_part
            else:
                dv_ref[rows, :] += value_part
                dk_ref[rows, :] += key_part
            query_part = dot_tn(keys * own, d_scores)

            if h == 0:

                @pl.when(j == 0)
                def _():
                    acc[...] = query_part

                @pl.when(j > 0)
                def _():
                    acc[...] += query_part

            else:
                acc[...] += query_part
            return 0

        lax.fori_loop(0, frames // block, step, 0)
    dq_ref[...] = acc[...].T * (HEAD_DIM**-0.5)


def call_forward(query, keys, values, col, row):
    frames, width = query.shape
    return pl.pallas_call(
        attention_forward,
        out_shape=(
            jax.ShapeDtypeStruct((frames, width), BF),
            jax.ShapeDtypeStruct((width // HEAD_DIM, frames), F32),
        ),
        scratch_shapes=[pltpu.VMEM((width, frames), F32), pltpu.VMEM((width, frames), F32)],
        compiler_params=pltpu.CompilerParams(vmem_limit_bytes=56 * 2**20),
        cost_estimate=pl.CostEstimate(
            flops=16 * frames * frames * width, bytes_accessed=10 * frames * width, transcendentals=0
        ),
        name="attention_forward",
    )(query, keys, values, col, row)


def call_backward(query, keys, values, mixed, grad, col, row, lse):
    frames, width = query.shape
    shape = jax.ShapeDtypeStruct((frames, width), F32)
    return pl.pallas_call(
        attention_backward,
        out_shape=(shape, shape, shape),
        scratch_shapes=[pltpu.VMEM((width, frames), F32)],
        compiler_params=pltpu.CompilerParams(vmem_limit_bytes=56 * 2**20),
        cost_estimate=pl.CostEstimate(
            flops=32 * frames * frames * width, bytes_accessed=20 * frames * width, transcendentals=0
        ),
        name="attention_backward",
    )(query, keys, values, mixed, grad, col, row, lse)


def frame_segments(own_lengths, positions):
    slots = own_lengths.shape[0]
    upto = jnp.arange(slots)[:, None] >= jnp.arange(slots)[None, :]
    ends_at = jnp.sum(jnp.where(upto, own_lengths[None, :], 0), axis=1)
    starts_at = ends_at - own_lengths
    segment = jnp.sum((positions[:, None] >= ends_at[None, :]).astype(jnp.int32), axis=1)
    index = jnp.arange(slots, dtype=jnp.int32)
    offset = jnp.sum(jnp.where(segment[:, None] == index[None, :], starts_at[None, :], 0), axis=1)
    return segment, positions - offset


def rotary_tables(places):
    freqs = jnp.exp(
        jnp.arange(HEAD_DIM // 2, dtype=F32) * (-2.0 * math.log(10000.0) / HEAD_DIM)
    )
    angles = places.astype(F32)[:, None] * freqs[None, :]
    cosine, sine = jnp.cos(angles), jnp.sin(angles)
    return (
        jnp.concatenate([cosine, cosine], axis=1)[:, None, :],
        jnp.concatenate([-sine, sine], axis=1)[:, None, :],
    )


def rotate(v, tables, sign):
    frames, width = v.shape
    shaped = v.reshape(frames, width // HEAD_DIM, HEAD_DIM)
    half = HEAD_DIM // 2
    swapped = jnp.concatenate([shaped[..., half:], shaped[..., :half]], axis=-1)
    return (shaped * tables[0] + swapped * (sign * tables[1])).reshape(frames, width)


def rms_parts(hidden):
    return lax.rsqrt(jnp.mean(hidden * hidden, axis=-1, keepdims=True) + EPSILON)


def rms_back(hidden, inverse, gain, grad):
    scaled = hidden * inverse
    weighted = grad * gain
    inner = jnp.mean(weighted * scaled, axis=-1, keepdims=True)
    return inverse * (weighted - scaled * inner), jnp.sum(grad * scaled, axis=0)


def gelu_both(t):
    bell = 0.5 * (1.0 + lax.erf(t * 0.7071067811865476))
    return t * bell, bell + t * (0.3989422804014327 * jnp.exp(-0.5 * t * t))


TOK = 176
MESH_ID = pl.DeviceIdType.MESH


def flip_low(u):
    return u + 1 - 2 * lax.rem(u, 2)


def flip_high(u):
    return u + 2 - 4 * lax.div(u, 2)


def swap_bits(u):
    return 2 * lax.rem(u, 2) + lax.div(u, 2)


class Sender:
    def __init__(self, send, recv, load):
        self.send, self.recv, self.load = send, recv, load
        self.n = self.m = 0
        self.sent, self.kept = [], []

    def remote(self, src, dst, device, arrival=None):
        copy = pltpu.make_async_remote_copy(
            src_ref=src,
            dst_ref=dst,
            send_sem=self.send.at[self.n],
            recv_sem=self.recv.at[self.n] if arrival is None else arrival,
            device_id=device,
            device_id_type=MESH_ID,
        )
        self.n += 1
        return copy

    def push(self, src, dst, device):
        copy = self.remote(src, dst, device)
        copy.start()
        self.sent.append(copy)
        return copy

    def push_or_keep(self, src, dst, device, own, arrival=None):
        arrival = self.recv.at[self.n] if arrival is None else arrival
        inside = pltpu.make_async_copy(src, dst, arrival)
        copy = self.remote(src, dst, device, arrival)

        @pl.when(own)
        def _():
            inside.start()

        @pl.when(jnp.logical_not(own))
        def _():
            copy.start()

        self.kept.append((copy, own))
        return copy

    def local(self, src, dst):
        copy = pltpu.make_async_copy(src, dst, self.load.at[self.m])
        self.m += 1
        copy.start()
        return copy

    def finish(self):
        for copy in self.sent:
            copy.wait_send()
        for copy, own in self.kept:

            @pl.when(jnp.logical_not(own))
            def _(copy=copy):
                copy.wait_send()

        self.sent, self.kept = [], []


def plane_peers(u, z, x):
    peers = []
    for k in range(8):
        a = flip_low(u) if k & 2 else u
        a = flip_high(a) if k & 4 else a
        b = 1 - x if k & 1 else x
        peers.append(((a, z, b), 2 * a + b))
    return peers


def rows_of(p, start=0, size=TOK):
    return pl.ds(pl.multiple_of(p * TOK + start, 16), size)


def gather_blocks(sender, buffer, peers, use):
    me = peers[0][1]
    low, high = 80, 96

    def block(k, start=0, size=TOK):
        return buffer.at[rows_of(peers[k][1], start, size)]

    own_c = sender.push(block(0), block(0), peers[2][0])
    own_x = sender.push(block(0), block(0), peers[1][0])
    own_y = sender.push(block(0), block(0), peers[4][0])
    use(0)
    own_c.wait_recv()
    use(2)
    own_x.wait_recv()
    over_y = sender.push(block(1, low, high), block(1, low, high), peers[4][0])
    core_x = sender.push(block(1), block(1), peers[2][0])
    own_y.wait_recv()
    over_x = sender.push(block(4, 0, low), block(4, 0, low), peers[1][0])
    core_y = sender.push(block(4), block(4), peers[2][0])
    use(1)
    use(4)
    core_x.wait_recv()
    use(3)
    core_y.wait_recv()
    use(6)
    over_x.wait_recv()
    over_y.wait_recv()
    core_xy = sender.push(block(5), block(5), peers[2][0])
    use(5)
    core_xy.wait_recv()
    use(7)


def first_kernel(
    lens_ref,
    inputs_ref,
    skip_ref,
    cot_ref,
    w_skip_ref,
    w_qkv_ref,
    gain_ref,
    entry_out,
    cot_out,
    joined_out,
    normed_out,
    q_out,
    k_out,
    v_out,
    o_out,
    lse_out,
    cos_out,
    sin_out,
    seg_out,
    mixed_out,
    xin,
    xskip,
    wskip,
    wqkv,
    ent_send,
    jperm,
    cot_r,
    joined_r,
    lens_r,
    ent_r,
    n1,
    q,
    k,
    v,
    o,
    lse,
    cos_t,
    sin_t,
    seg_col,
    mixed,
    acc,
    out_t,
    send,
    recv,
    load,
    spread_recv,
):
    u, z, x = (lax.axis_index(a) for a in AXES)
    me = 2 * u + x
    peers = plane_peers(u, z, x)
    d = xin.shape[1]
    frames = n1.shape[0]
    plane = swap_bits(u)
    away = (z, plane, x)
    stays = jnp.logical_and(u == z, plane == z)
    sender = Sender(send, recv, load)

    got_x = sender.local(inputs_ref, xin)
    got_s = sender.local(skip_ref, xskip)
    got_w = sender.local(w_skip_ref, wskip)
    got_q = [
        sender.local(
            w_qkv_ref.at[:, pl.ds(pl.multiple_of(c * d + me * 128, 128), 128)],
            wqkv.at[:, pl.ds(c * 128, 128)],
        )
        for c in range(3)
    ]
    sent_lens = sender.push_or_keep(lens_ref, lens_r, away, stays)
    got_x.wait()
    got_s.wait()
    got_w.wait()
    sent_entry = []
    for n in range(2):
        part = slice(n * d // 2, (n + 1) * d // 2)
        value = dot_nn(xin[...], wskip[:d, part]) + dot_nn(xskip[...], wskip[d:, part])
        ent_send[:, part] = value.astype(BF)
        sent_entry.append(
            sender.push_or_keep(ent_send.at[:, part], ent_r.at[:, part], away, stays)
        )

    lane = lax.broadcasted_iota(jnp.int32, (TOK, 128), 1)
    for a in range(4):
        for b in range(2):
            for pair in range(2):
                halves = []
                for s in range(2):
                    block = 4 * (2 * pair + s) + 2 * b + a // 2
                    source = xin if block < d // 128 else xskip
                    first = block % (d // 128) * 128
                    piece = source[:, first : first + 128].astype(F32)
                    if a % 2 != s:
                        piece = pltpu.roll(piece, 64, 1)
                    halves.append(piece)
                place = (2 * a + b) * 256 + pair * 128
                jperm[:, place : place + 128] = jnp.where(lane < 64, halves[0], halves[1]).astype(BF)

    sent_lens.wait_recv()
    spread = lax.broadcasted_iota(jnp.int32, (TOK, 128), 1)
    freqs = jnp.exp(
        lax.rem(spread, 32).astype(F32) * (-2.0 * math.log(10000.0) / HEAD_DIM)
    )
    sign = jnp.where(lax.rem(spread, 64) < 32, -1.0, 1.0)
    slots = 6

    def table(i, _):
        rows = rows_of(i)
        at = (lax.broadcasted_iota(jnp.int32, (TOK, 128), 0) + i * TOK).astype(F32)
        place, segment, end = at, jnp.zeros_like(at), jnp.zeros((1, 128), F32)
        for s in range(slots):
            length = lens_r[s : s + 1, :]
            end = end + length
            past = at >= end
            segment = segment + jnp.where(past, 1.0, 0.0)
            place = place - jnp.where(past, length, 0.0)
        angle = place * freqs
        cos_t[rows, :] = jnp.cos(angle)
        sin_t[rows, :] = jnp.sin(angle) * sign
        seg_col[rows, :] = segment
        return 0

    lax.fori_loop(0, frames // TOK, table, 0)
    at = lax.broadcasted_iota(jnp.int32, (1, frames), 1).astype(F32)
    segment_row, end = jnp.zeros((1, frames), F32), jnp.zeros((1, 1), F32)
    for s in range(slots):
        end = end + lens_r[s : s + 1, 0:1]
        segment_row = segment_row + jnp.where(at >= end, 1.0, 0.0)

    for copy in sent_entry:
        copy.wait_recv()
    entry = ent_r[...].astype(F32)
    n1[rows_of(me), :] = (entry * rms_parts(entry) * gain_ref[...]).astype(BF)
    outs = [sender.local(ent_r, entry_out)]
    for copy in got_q:
        copy.wait()

    later = []

    def use(i):
        rows = rows_of(peers[i][1])
        value = dot_nn(n1[rows, :], wqkv[...])
        cosine, sine = cos_t[rows, :], sin_t[rows, :]
        front = lax.rem(lax.broadcasted_iota(jnp.int32, (TOK, 128), 1), 64) < 32

        def turn(t):
            swapped = jnp.where(front, pltpu.roll(t, 96, 1), pltpu.roll(t, 32, 1))
            return t * cosine + swapped * sine

        q[rows, :] = (turn(value[:, :128]).astype(BF).astype(F32) * HEAD_DIM**-0.5).astype(BF)
        k[rows, :] = turn(value[:, 128:256]).astype(BF)
        v[rows, :] = value[:, 256:].astype(BF)
        if i == 0:
            later.append(sender.push_or_keep(cot_ref, cot_r, away, stays))

    gather_blocks(sender, n1, peers, use)
    outs.append(sender.local(n1, normed_out))
    for a in range(4):
        for b in range(2):
            own = jnp.logical_and(jnp.logical_and(u == a, x == b), plane == z)
            sender.push_or_keep(
                jperm.at[:, pl.ds((2 * a + b) * 256, 256)],
                joined_r.at[rows_of(2 * z + x)],
                (a, plane, b),
                own,
                spread_recv.at[2 * z + x],
            )

    forward_heads(q, k, v, seg_col, segment_row, o, lse, acc, out_t)
    for src, dst in ((q, q_out), (k, k_out), (v, v_out), (o, o_out), (lse, lse_out)):
        outs.append(sender.local(src, dst))
    for src, dst in ((cos_t, cos_out), (sin_t, sin_out), (seg_col, seg_out)):
        outs.append(sender.local(src, dst))
    arrivals = [
        sender.push(
            o.at[rows_of(peers[i][1])],
            mixed.at[:, pl.ds(pl.multiple_of(me * 128, 128), 128)],
            peers[i][0],
        )
        for i in range(1, 8)
    ]
    own = sender.local(
        o.at[rows_of(me)], mixed.at[:, pl.ds(pl.multiple_of(me * 128, 128), 128)]
    )
    own.wait()
    for copy in arrivals:
        copy.wait_recv()
    outs.append(sender.local(mixed, mixed_out))
    for copy in later:
        copy.wait_recv()
    for s in range(8):
        rows = pl.ds(s * TOK, TOK)
        pltpu.make_async_copy(joined_r.at[rows], joined_r.at[rows], spread_recv.at[s]).wait()
    outs.append(sender.local(cot_r, cot_out))
    outs.append(sender.local(joined_r, joined_out))
    for copy in outs:
        copy.wait()
    sender.finish()


def call_first(lens, inputs, skip_in, cotangent, w_skip, w_qkv, gain_one):
    d = inputs.shape[1]
    group = 8 * TOK
    any_space = pl.BlockSpec(memory_space=pl.ANY)
    vmem = pl.BlockSpec(memory_space=pltpu.VMEM)
    wide, head, table = (group, d), ((group, 128), BF), ((group, 128), F32)
    outs = [
        ((TOK, d), BF),
        ((TOK, d), BF),
        ((group, 256), BF),
        (wide, BF),
        head,
        head,
        head,
        head,
        ((8, group), F32),
        table,
        table,
        table,
        ((TOK, d), BF),
    ]
    scratch = [
        ((TOK, d), BF),
        ((TOK, d), BF),
        ((2 * d, d), BF),
        ((d, 384), BF),
        ((TOK, d), BF),
        ((TOK, 2 * d), BF),
        ((TOK, d), BF),
        ((group, 256), BF),
        ((8, 128), F32),
        ((TOK, d), BF),
        (wide, BF),
        head,
        head,
        head,
        head,
        ((8, group), F32),
        table,
        table,
        table,
        ((TOK, d), BF),
        ((128, group), F32),
        ((128, group), F32),
    ]
    return pl.pallas_call(
        first_kernel,
        in_specs=[vmem] + [any_space] * 5 + [vmem],
        out_specs=[any_space] * len(outs),
        out_shape=[jax.ShapeDtypeStruct(*o) for o in outs],
        scratch_shapes=[pltpu.VMEM(*s) for s in scratch]
        + [pltpu.SemaphoreType.DMA((40,))] * 3
        + [pltpu.SemaphoreType.DMA((8,))],
        compiler_params=pltpu.CompilerParams(
            vmem_limit_bytes=56 * 2**20, has_side_effects=True
        ),
        name="entry_to_mixed",
    )(lens, inputs, skip_in, cotangent, w_skip, w_qkv, gain_one)


def local(
    sizes,
    inputs,
    skip_in,
    lengths,
    cotangent,
    w_skip,
    gain_one,
    w_qkv,
    w_out,
    gain_two,
    w_up,
    b_up,
    w_down,
    b_down,
):
    n_u, n_z, n_x = sizes
    frames, d = inputs.shape
    hidden = w_up.shape[1]
    parts = n_u * n_x
    group = frames * parts
    u, z, x = (lax.axis_index(a) for a in AXES)
    me = u * n_x + x
    width = d // parts

    def line(a, b, c):
        return (a * n_z + b) * n_x + c

    def permute(v, to):
        pairs = [
            (line(a, b, c), line(*to(a, b, c)))
            for a in range(n_u)
            for b in range(n_z)
            for c in range(n_x)
        ]
        return lax.ppermute(v, AXES, pairs)

    def plane_of(a):
        return (a % 2) * (n_u // 2) + a // 2

    group_of = {plane_of(a): a for a in range(n_u)}

    def away(v):
        return permute(v, lambda a, b, c: (b, plane_of(a), c))

    def home(v):
        return permute(v, lambda a, b, c: (group_of[b], a, c))

    def swap_plane(v, bit):
        def to(a, b, c):
            other = (a * n_x + c) ^ bit
            return other // n_x, b, other % n_x

        return permute(v, to)

    plane_bits = [1 << i for i in range(parts.bit_length() - 1)]
    if n_x == 2 and n_u == 4:
        orders = ([1, 4, 2], [4, 1, 2])
    else:
        orders = (plane_bits, plane_bits)
    cut = frames // 32 * 16

    def gather_plane(v):
        pieces = []
        for piece, order in zip((v[:cut], v[cut:]), orders):
            for bit in order:
                piece = jnp.concatenate([piece, swap_plane(piece, bit)], axis=0)
            pieces.append(piece)
        return jnp.concatenate(pieces, axis=0)

    def gather_order(v):
        pieces = []
        for start, size, order in ((0, cut, orders[0]), (cut, frames - cut, orders[1])):
            offsets = [0]
            for bit in order:
                offsets = offsets + [o ^ bit for o in offsets]
            for o in offsets:
                pieces.append(
                    lax.dynamic_slice_in_dim(v, (me ^ o) * frames + start, size, axis=0)
                )
        return jnp.concatenate(pieces, axis=0)

    z_bits = n_z.bit_length() - 1

    def reduce_z(v):
        rest = v.shape[1:]
        v = v.reshape((2,) * z_bits + (v.shape[0] // n_z,) + rest)
        for bit in range(z_bits):
            axis = z_bits - 1 - bit
            own = (z >> bit) & 1
            keep = lax.dynamic_index_in_dim(v, own, axis, keepdims=False)
            give = lax.dynamic_index_in_dim(v, 1 - own, axis, keepdims=False)
            got = permute(
                give.astype(BF), lambda a, b, c, bit=bit: (a, b ^ (1 << bit), c)
            )
            v = keep.astype(F32) + got.astype(F32)
            if bit < z_bits - 1:
                v = v.astype(BF)
        return v.astype(BF)

    def finish_columns(v):
        if n_x == 2:
            v = v.reshape((2, v.shape[0] // 2) + v.shape[1:])
            keep = lax.dynamic_index_in_dim(v, x, 0, keepdims=False)
            give = lax.dynamic_index_in_dim(v, 1 - x, 0, keepdims=False)
            got = permute(give, lambda a, b, c: (a, b, 1 - c))
            both = jnp.where(x == 0, jnp.stack([keep, got]), jnp.stack([got, keep]))
        else:
            both = v[None]
        every = lax.all_gather(both, "u", axis=0)
        return every.reshape((parts,) + both.shape[1:])

    def sum_all(v):
        total = n_u * n_z * n_x
        for i in range(total.bit_length() - 1):
            bit = 1 << i
            pairs = [(n, n ^ bit) for n in range(total)]
            v = v + lax.ppermute(v, AXES, pairs)
        return v

    entry_home = dot_nn(inputs, w_skip[:d]) + dot_nn(skip_in, w_skip[d:])
    entry = away(entry_home.astype(BF)).astype(F32)
    group_lengths = away(lengths)[0]
    grad_low = away(cotangent)
    inputs_away = away(inputs)
    skip_away = away(skip_in)

    segment, places = frame_segments(group_lengths, jnp.arange(group, dtype=jnp.int32))
    own_places = lax.dynamic_slice_in_dim(places, me * frames, frames)
    tables = rotary_tables(own_places)
    col, row = segment[:, None], segment[None, :]

    inverse_one = rms_parts(entry)
    normed_one = (entry * inverse_one * gain_one).astype(BF)
    qkv = dot_nn(normed_one, w_qkv)
    query = (rotate(qkv[:, :d], tables, 1.0)).astype(BF) * BF(HEAD_DIM**-0.5)
    keys = rotate(qkv[:, d : 2 * d], tables, 1.0).astype(BF)
    values = qkv[:, 2 * d :].astype(BF)

    def to_heads(*arrays):
        n = len(arrays)
        v = jnp.stack([a.reshape(frames, parts, width) for a in arrays], axis=2)
        v = lax.all_to_all(
            v.reshape(frames, parts * n * width), PLANE, split_axis=1, concat_axis=0, tiled=True
        )
        return [v[:, i * width : (i + 1) * width] for i in range(n)]

    def to_frames(*arrays):
        n = len(arrays)
        v = jnp.concatenate(arrays, axis=1)
        v = lax.all_to_all(v, PLANE, split_axis=0, concat_axis=1, tiled=True)
        v = v.reshape(frames, parts, n, width)
        return [v[:, :, i].reshape(frames, d) for i in range(n)]

    head_query, head_keys, head_values = to_heads(query, keys, values)
    head_mixed, lse = call_forward(head_query, head_keys, head_values, col, row)
    (mixed,) = to_frames(head_mixed)

    middle = entry + dot_nn(mixed, w_out)
    inverse_two = rms_parts(middle)
    normed_two = (middle * inverse_two * gain_two).astype(BF)
    up = dot_nn(normed_two, w_up) + b_up
    d_active = dot_nt(grad_low, w_down)
    active, slope = gelu_both(up)
    d_up = (d_active * slope).astype(BF)
    result_away = (middle + dot_nn(active.astype(BF), w_down) + b_down).astype(BF)
    result = home(result_away)
    d_normed_two = dot_nt(d_up, w_up)
    middle_part, g_gain_two = rms_back(middle, inverse_two, gain_two, d_normed_two)
    d_middle = grad_low.astype(F32) + middle_part
    d_branch = d_middle.astype(BF)
    d_mixed = dot_nt(d_branch, w_out).astype(BF)
    (head_grad,) = to_heads(d_mixed)
    dq, dk, dv = call_backward(
        head_query, head_keys, head_values, head_mixed, head_grad, col, row, lse
    )

    chunk = hidden // (n_z * parts)
    w_up_own = lax.dynamic_slice(
        w_up.reshape(d, n_z, n_x, n_u, chunk), (0, 0, x, u, 0), (d, n_z, 1, 1, chunk)
    ).reshape(d, n_z * chunk)
    w_down_own = lax.dynamic_slice(
        w_down.reshape(n_z, n_x, n_u, chunk, d), (0, x, u, 0, 0), (n_z, 1, 1, chunk, d)
    ).reshape(n_z * chunk, d)
    b_up_own = lax.dynamic_slice(
        b_up.reshape(n_z, n_x, n_u, chunk), (0, x, u, 0), (n_z, 1, 1, chunk)
    ).reshape(n_z * chunk)
    plane_grad = gather_plane(grad_low)
    plane_normed = gather_plane(normed_two)
    up_own = dot_nn(plane_normed, w_up_own) + b_up_own
    active_own, slope_own = gelu_both(up_own)
    d_up_own = (dot_nt(plane_grad, w_down_own) * slope_own).astype(BF)
    g_down = dot_tn(active_own.astype(BF), plane_grad)
    g_up = dot_tn(plane_normed, d_up_own)
    down_z = reduce_z(g_down.astype(BF))
    up_z = reduce_z(g_up.astype(BF))
    out_down = lax.all_gather(down_z, "u", axis=0, tiled=True).astype(F32)
    out_up = finish_columns(up_z)
    out_up = (
        out_up.reshape(n_u, n_x, -1, n_z, chunk).transpose(2, 3, 1, 0, 4).reshape(-1, hidden)
    ).astype(F32)

    plane_mixed = gather_plane(mixed)
    own_branch = gather_order(
        lax.all_to_all(d_branch, PLANE, split_axis=1, concat_axis=0, tiled=True)
    )
    g_out = dot_tn(plane_mixed, own_branch)
    out_out = (
        finish_columns(reduce_z(g_out.astype(BF))).transpose(1, 0, 2).reshape(-1, d).astype(F32)
    )

    low = [a.astype(BF) for a in (dq, dk, dv)]
    frame_query, frame_keys, frame_values = to_frames(*low)
    d_qkv = jnp.concatenate(
        [
            rotate(frame_query.astype(F32), tables, -1.0).astype(BF),
            rotate(frame_keys.astype(F32), tables, -1.0).astype(BF),
            frame_values,
        ],
        axis=1,
    )
    d_normed_one = dot_nt(d_qkv, w_qkv)
    entry_part, g_gain_one = rms_back(entry, inverse_one, gain_one, d_normed_one)
    d_entry = (d_middle + entry_part).astype(BF)
    d_entry_home = home(d_entry)
    d_joined = dot_nt(d_entry_home, w_skip)
    d_inputs = d_joined[:, :d].astype(BF)
    d_skip = d_joined[:, d:].astype(BF)

    group_tables = rotary_tables(places)
    head_d_qkv = jnp.concatenate(
        [
            rotate(low[0].astype(F32), group_tables, -1.0).astype(BF),
            rotate(low[1].astype(F32), group_tables, -1.0).astype(BF),
            low[2],
        ],
        axis=1,
    )
    plane_first = gather_plane(normed_one)
    g_qkv = dot_tn(plane_first, gather_order(head_d_qkv))
    plane_inputs = gather_plane(inputs_away)
    plane_skip = gather_plane(skip_away)
    own_entry = gather_order(
        lax.all_to_all(d_entry, PLANE, split_axis=1, concat_axis=0, tiled=True)
    )
    g_skip = jnp.concatenate([dot_tn(plane_inputs, own_entry), dot_tn(plane_skip, own_entry)])
    out_qkv = finish_columns(reduce_z(g_qkv.astype(BF)))
    out_qkv = (
        out_qkv.reshape(parts, -1, 3, width).transpose(1, 2, 0, 3).reshape(-1, 3 * d).astype(F32)
    )
    out_skip = (
        finish_columns(reduce_z(g_skip.astype(BF))).transpose(1, 0, 2).reshape(-1, d).astype(F32)
    )

    early = sum_all(
        jnp.concatenate(
            [
                g_gain_two,
                jnp.sum(d_up.astype(F32), axis=0),
                jnp.sum(cotangent.astype(F32), axis=0),
            ]
        )
    )
    total_gain_one = sum_all(g_gain_one)
    return (
        result,
        d_inputs,
        d_skip,
        out_skip,
        total_gain_one,
        out_qkv,
        out_out,
        early[:d],
        out_up,
        early[d : d + hidden],
        out_down,
        early[d + hidden :],
    )


def local_fast(
    sizes,
    inputs,
    skip_in,
    lengths,
    cotangent,
    w_skip,
    gain_one,
    w_qkv,
    w_out,
    gain_two,
    w_up,
    b_up,
    w_down,
    b_down,
):
    n_u, n_z, n_x = sizes
    frames, d = inputs.shape
    hidden = w_up.shape[1]
    parts = n_u * n_x
    group = frames * parts
    u, z, x = (lax.axis_index(a) for a in AXES)
    me = u * n_x + x
    width = d // parts

    def line(a, b, c):
        return (a * n_z + b) * n_x + c

    def permute(v, to):
        pairs = [
            (line(a, b, c), line(*to(a, b, c)))
            for a in range(n_u)
            for b in range(n_z)
            for c in range(n_x)
        ]
        return lax.ppermute(v, AXES, pairs)

    def plane_of(a):
        return (a % 2) * (n_u // 2) + a // 2

    group_of = {plane_of(a): a for a in range(n_u)}

    def away(v):
        return permute(v, lambda a, b, c: (b, plane_of(a), c))

    def home(v):
        return permute(v, lambda a, b, c: (group_of[b], a, c))

    def swap_plane(v, bit):
        def to(a, b, c):
            other = (a * n_x + c) ^ bit
            return other // n_x, b, other % n_x

        return permute(v, to)

    plane_bits = [1 << i for i in range(parts.bit_length() - 1)]
    if n_x == 2 and n_u == 4:
        orders = ([1, 4, 2], [4, 1, 2])
    else:
        orders = (plane_bits, plane_bits)
    cut = frames // 32 * 16

    def gather_plane(v):
        pieces = []
        for piece, order in zip((v[:cut], v[cut:]), orders):
            for bit in order:
                piece = jnp.concatenate([piece, swap_plane(piece, bit)], axis=0)
            pieces.append(piece)
        return jnp.concatenate(pieces, axis=0)

    def gather_order(v):
        pieces = []
        for start, size, order in ((0, cut, orders[0]), (cut, frames - cut, orders[1])):
            offsets = [0]
            for bit in order:
                offsets = offsets + [o ^ bit for o in offsets]
            for o in offsets:
                pieces.append(
                    lax.dynamic_slice_in_dim(v, (me ^ o) * frames + start, size, axis=0)
                )
        return jnp.concatenate(pieces, axis=0)

    z_bits = n_z.bit_length() - 1

    def reduce_z(v):
        rest = v.shape[1:]
        v = v.reshape((2,) * z_bits + (v.shape[0] // n_z,) + rest)
        for bit in range(z_bits):
            axis = z_bits - 1 - bit
            own = (z >> bit) & 1
            keep = lax.dynamic_index_in_dim(v, own, axis, keepdims=False)
            give = lax.dynamic_index_in_dim(v, 1 - own, axis, keepdims=False)
            got = permute(
                give.astype(BF), lambda a, b, c, bit=bit: (a, b ^ (1 << bit), c)
            )
            v = keep.astype(F32) + got.astype(F32)
            if bit < z_bits - 1:
                v = v.astype(BF)
        return v.astype(BF)

    def finish_columns(v):
        if n_x == 2:
            v = v.reshape((2, v.shape[0] // 2) + v.shape[1:])
            keep = lax.dynamic_index_in_dim(v, x, 0, keepdims=False)
            give = lax.dynamic_index_in_dim(v, 1 - x, 0, keepdims=False)
            got = permute(give, lambda a, b, c: (a, b, 1 - c))
            both = jnp.where(x == 0, jnp.stack([keep, got]), jnp.stack([got, keep]))
        else:
            both = v[None]
        every = lax.all_gather(both, "u", axis=0)
        return every.reshape((parts,) + both.shape[1:])

    def sum_all(v):
        total = n_u * n_z * n_x
        for i in range(total.bit_length() - 1):
            bit = 1 << i
            pairs = [(n, n ^ bit) for n in range(total)]
            v = v + lax.ppermute(v, AXES, pairs)
        return v

    lens = jnp.broadcast_to(
        jnp.pad(lengths[0].astype(F32), (0, 8 - lengths.shape[1]))[:, None], (8, 128)
    )
    (
        entry_low,
        grad_low,
        joined_own,
        plane_first,
        head_query,
        head_keys,
        head_values,
        head_mixed,
        lse8,
        cos_t,
        sin_t,
        seg_t,
        mixed,
    ) = call_first(lens, inputs, skip_in, cotangent, w_skip, w_qkv, gain_one[None])
    entry = entry_low.astype(F32)
    inverse_one = rms_parts(entry)
    lse = lse8[:2]
    col = seg_t[:, :1]
    row = col.reshape(1, group)
    own_cos = lax.dynamic_slice_in_dim(cos_t, me * frames, frames)[:, None, :64]
    own_sin = lax.dynamic_slice_in_dim(sin_t, me * frames, frames)[:, None, :64]
    tables = (own_cos, own_sin)
    group_tables = (cos_t[:, None, :64], sin_t[:, None, :64])
    def to_heads(*arrays):
        n = len(arrays)
        v = jnp.stack([a.reshape(frames, parts, width) for a in arrays], axis=2)
        v = lax.all_to_all(
            v.reshape(frames, parts * n * width), PLANE, split_axis=1, concat_axis=0, tiled=True
        )
        return [v[:, i * width : (i + 1) * width] for i in range(n)]

    def to_frames(*arrays):
        n = len(arrays)
        v = jnp.concatenate(arrays, axis=1)
        v = lax.all_to_all(v, PLANE, split_axis=0, concat_axis=1, tiled=True)
        v = v.reshape(frames, parts, n, width)
        return [v[:, :, i].reshape(frames, d) for i in range(n)]

    middle = entry + dot_nn(mixed, w_out)
    inverse_two = rms_parts(middle)
    normed_two = (middle * inverse_two * gain_two).astype(BF)
    up = dot_nn(normed_two, w_up) + b_up
    d_active = dot_nt(grad_low, w_down)
    active, slope = gelu_both(up)
    d_up = (d_active * slope).astype(BF)
    result_away = (middle + dot_nn(active.astype(BF), w_down) + b_down).astype(BF)
    result = home(result_away)
    d_normed_two = dot_nt(d_up, w_up)
    middle_part, g_gain_two = rms_back(middle, inverse_two, gain_two, d_normed_two)
    d_middle = grad_low.astype(F32) + middle_part
    d_branch = d_middle.astype(BF)
    d_mixed = dot_nt(d_branch, w_out).astype(BF)
    (head_grad,) = to_heads(d_mixed)
    dq, dk, dv = call_backward(
        head_query, head_keys, head_values, head_mixed, head_grad, col, row, lse
    )

    chunk = hidden // (n_z * parts)
    w_up_own = lax.dynamic_slice(
        w_up.reshape(d, n_z, n_x, n_u, chunk), (0, 0, x, u, 0), (d, n_z, 1, 1, chunk)
    ).reshape(d, n_z * chunk)
    w_down_own = lax.dynamic_slice(
        w_down.reshape(n_z, n_x, n_u, chunk, d), (0, x, u, 0, 0), (n_z, 1, 1, chunk, d)
    ).reshape(n_z * chunk, d)
    b_up_own = lax.dynamic_slice(
        b_up.reshape(n_z, n_x, n_u, chunk), (0, x, u, 0), (n_z, 1, 1, chunk)
    ).reshape(n_z * chunk)
    plane_grad = gather_plane(grad_low)
    plane_normed = gather_plane(normed_two)
    up_own = dot_nn(plane_normed, w_up_own) + b_up_own
    active_own, slope_own = gelu_both(up_own)
    d_up_own = (dot_nt(plane_grad, w_down_own) * slope_own).astype(BF)
    g_down = dot_tn(active_own.astype(BF), plane_grad)
    g_up = dot_tn(plane_normed, d_up_own)
    down_z = reduce_z(g_down.astype(BF))
    up_z = reduce_z(g_up.astype(BF))
    out_down = lax.all_gather(down_z, "u", axis=0, tiled=True).astype(F32)
    out_up = finish_columns(up_z)
    out_up = (
        out_up.reshape(n_u, n_x, -1, n_z, chunk).transpose(2, 3, 1, 0, 4).reshape(-1, hidden)
    ).astype(F32)

    plane_mixed = gather_plane(mixed)
    own_branch = gather_order(
        lax.all_to_all(d_branch, PLANE, split_axis=1, concat_axis=0, tiled=True)
    )
    g_out = dot_tn(plane_mixed, own_branch)
    out_out = (
        finish_columns(reduce_z(g_out.astype(BF))).transpose(1, 0, 2).reshape(-1, d).astype(F32)
    )

    low = [a.astype(BF) for a in (dq, dk, dv)]
    frame_query, frame_keys, frame_values = to_frames(*low)
    d_qkv = jnp.concatenate(
        [
            rotate(frame_query.astype(F32), tables, -1.0).astype(BF),
            rotate(frame_keys.astype(F32), tables, -1.0).astype(BF),
            frame_values,
        ],
        axis=1,
    )
    d_normed_one = dot_nt(d_qkv, w_qkv)
    entry_part, g_gain_one = rms_back(entry, inverse_one, gain_one, d_normed_one)
    d_entry = (d_middle + entry_part).astype(BF)
    d_entry_home = home(d_entry)
    d_joined = dot_nt(d_entry_home, w_skip)
    d_inputs = d_joined[:, :d].astype(BF)
    d_skip = d_joined[:, d:].astype(BF)

    head_d_qkv = jnp.concatenate(
        [
            rotate(low[0].astype(F32), group_tables, -1.0).astype(BF),
            rotate(low[1].astype(F32), group_tables, -1.0).astype(BF),
            low[2],
        ],
        axis=1,
    )
    g_qkv = dot_tn(plane_first, head_d_qkv)
    g_skip = dot_tn(joined_own, lax.all_gather(d_entry, PLANE, axis=0, tiled=True))
    out_qkv = finish_columns(reduce_z(g_qkv.astype(BF)))
    out_qkv = (
        out_qkv.reshape(parts, -1, 3, width).transpose(1, 2, 0, 3).reshape(-1, 3 * d).astype(F32)
    )
    out_skip = lax.all_gather(
        reduce_z(g_skip.astype(BF)), "u", axis=0, tiled=True
    ).astype(F32)

    early = sum_all(
        jnp.concatenate(
            [
                g_gain_two,
                jnp.sum(d_up.astype(F32), axis=0),
                jnp.sum(cotangent.astype(F32), axis=0),
            ]
        )
    )
    total_gain_one = sum_all(g_gain_one)
    return (
        result,
        d_inputs,
        d_skip,
        out_skip,
        total_gain_one,
        out_qkv,
        out_out,
        early[:d],
        out_up,
        early[d : d + hidden],
        out_down,
        early[d + hidden :],
    )


def solution(mesh):
    n_u, n_s = mesh.shape["utt"], mesh.shape["seq"]
    sizes = (n_u, n_u, n_s // n_u)
    program = local_fast if sizes == (4, 4, 2) else local
    inner = Mesh(mesh.devices.reshape(sizes), AXES)
    rows, seq = P(AXES, None), P(("z", "x"), None)
    in_specs = (rows, rows, P("u", None), rows) + (P(),) * 9
    out_specs = (rows, rows, rows, seq, P(), seq, seq, P(), seq, P(), seq, P())
    return jax.shard_map(
        functools.partial(program, sizes),
        mesh=inner,
        in_specs=in_specs,
        out_specs=out_specs,
        check_vma=False,
    )
```

```python
import functools
import math

import jax
import jax.numpy as jnp
from jax import lax
from jax.experimental import pallas as pl
from jax.experimental.pallas import tpu as pltpu
from jax.sharding import Mesh, PartitionSpec as P

HEAD_DIM = 64
EPSILON = 1e-06
BF = jnp.bfloat16
F32 = jnp.float32
AXES = ("u", "z", "x")
PLANE = ("u", "x")


def dot_nn(a, b):
    return lax.dot_general(a, b, (((1,), (0,)), ((), ())), preferred_element_type=F32)


def dot_nt(a, b):
    return lax.dot_general(a, b, (((1,), (1,)), ((), ())), preferred_element_type=F32)


def dot_tn(a, b):
    return lax.dot_general(a, b, (((0,), (0,)), ((), ())), preferred_element_type=F32)


def attention_forward(q_ref, k_ref, v_ref, col_ref, row_ref, o_ref, lse_ref, acc, out_t):
    forward_heads(q_ref, k_ref, v_ref, col_ref, row_ref[...], o_ref, lse_ref, acc, out_t)


def forward_heads(q_ref, k_ref, v_ref, col_ref, segment_row, o_ref, lse_ref, acc, out_t):
    frames, width = q_ref.shape
    heads = width // HEAD_DIM
    block = frames // (frames // 352)
    lane = lax.broadcasted_iota(jnp.int32, (1, width), 1)
    for h in range(heads):
        own = (lane // HEAD_DIM == h).astype(BF)
        query = q_ref[...] * own
        acc[...] = jnp.zeros_like(acc)

        def step(j, carry):
            top, total = carry
            rows = pl.ds(pl.multiple_of(j * block, block), block)
            scores = dot_nt(k_ref[rows, :], query)
            scores = jnp.where(col_ref[rows, 0:1] == segment_row, scores, -1e30)
            peak = jnp.maximum(top, jnp.max(scores, axis=0, keepdims=True))
            expos = jnp.exp(scores - peak)
            shrink = jnp.exp(top - peak)
            acc[...] = acc[...] * shrink + dot_tn(v_ref[rows, :], expos.astype(BF))
            return peak, total * shrink + jnp.sum(expos, axis=0, keepdims=True)

        top, total = lax.fori_loop(
            0,
            frames // block,
            step,
            (jnp.full((1, frames), -1e30, F32), jnp.zeros((1, frames), F32)),
        )
        part = slice(h * HEAD_DIM, (h + 1) * HEAD_DIM)
        out_t[part, :] = acc[part, :] / total
        lse_ref[h : h + 1, :] = top + jnp.log(total)
    o_ref[...] = out_t[...].T.astype(BF)


def attention_backward(
    q_ref, k_ref, v_ref, o_ref, do_ref, col_ref, row_ref, lse_ref, dq_ref, dk_ref, dv_ref, acc
):
    backward_heads(
        q_ref, k_ref, v_ref, o_ref, do_ref, col_ref, row_ref[...], lse_ref, dq_ref, dk_ref, dv_ref, acc
    )


def backward_heads(
    q_ref, k_ref, v_ref, o_ref, do_ref, col_ref, segment_row, lse_ref, dq_ref, dk_ref, dv_ref, acc
):
    frames, width = q_ref.shape
    heads = width // HEAD_DIM
    block = frames // (frames // 352)
    lane = lax.broadcasted_iota(jnp.int32, (1, width), 1)
    product_t = (o_ref[...].astype(F32) * do_ref[...].astype(F32)).T
    for h in range(heads):
        own = (lane // HEAD_DIM == h).astype(BF)
        query = q_ref[...] * own
        grad = do_ref[...] * own
        part = slice(h * HEAD_DIM, (h + 1) * HEAD_DIM)
        delta = jnp.sum(product_t[part, :], axis=0, keepdims=True)
        log_total = lse_ref[h : h + 1, :]

        def step(j, _):
            rows = pl.ds(pl.multiple_of(j * block, block), block)
            keys = k_ref[rows, :]
            scores = dot_nt(keys, query)
            same = col_ref[rows, 0:1] == segment_row
            probs = jnp.where(same, jnp.exp(scores - log_total), 0.0)
            d_probs = dot_nt(v_ref[rows, :], grad)
            d_scores = (probs * (d_probs - delta)).astype(BF)
            value_part = dot_nn(probs.astype(BF), grad)
            key_part = dot_nn(d_scores, query)
            if h == 0:
                dv_ref[rows, :] = value_part
                dk_ref[rows, :] = key_part
            else:
                dv_ref[rows, :] += value_part
                dk_ref[rows, :] += key_part
            query_part = dot_tn(keys * own, d_scores)

            if h == 0:

                @pl.when(j == 0)
                def _():
                    acc[...] = query_part

                @pl.when(j > 0)
                def _():
                    acc[...] += query_part

            else:
                acc[...] += query_part
            return 0

        lax.fori_loop(0, frames // block, step, 0)
    dq_ref[...] = acc[...].T * (HEAD_DIM**-0.5)


def call_forward(query, keys, values, col, row):
    frames, width = query.shape
    return pl.pallas_call(
        attention_forward,
        out_shape=(
            jax.ShapeDtypeStruct((frames, width), BF),
            jax.ShapeDtypeStruct((width // HEAD_DIM, frames), F32),
        ),
        scratch_shapes=[pltpu.VMEM((width, frames), F32), pltpu.VMEM((width, frames), F32)],
        compiler_params=pltpu.CompilerParams(vmem_limit_bytes=56 * 2**20),
        cost_estimate=pl.CostEstimate(
            flops=16 * frames * frames * width, bytes_accessed=10 * frames * width, transcendentals=0
        ),
        name="attention_forward",
    )(query, keys, values, col, row)


def call_backward(query, keys, values, mixed, grad, col, row, lse):
    frames, width = query.shape
    shape = jax.ShapeDtypeStruct((frames, width), F32)
    return pl.pallas_call(
        attention_backward,
        out_shape=(shape, shape, shape),
        scratch_shapes=[pltpu.VMEM((width, frames), F32)],
        compiler_params=pltpu.CompilerParams(vmem_limit_bytes=56 * 2**20),
        cost_estimate=pl.CostEstimate(
            flops=32 * frames * frames * width, bytes_accessed=20 * frames * width, transcendentals=0
        ),
        name="attention_backward",
    )(query, keys, values, mixed, grad, col, row, lse)


def frame_segments(own_lengths, positions):
    slots = own_lengths.shape[0]
    upto = jnp.arange(slots)[:, None] >= jnp.arange(slots)[None, :]
    ends_at = jnp.sum(jnp.where(upto, own_lengths[None, :], 0), axis=1)
    starts_at = ends_at - own_lengths
    segment = jnp.sum((positions[:, None] >= ends_at[None, :]).astype(jnp.int32), axis=1)
    index = jnp.arange(slots, dtype=jnp.int32)
    offset = jnp.sum(jnp.where(segment[:, None] == index[None, :], starts_at[None, :], 0), axis=1)
    return segment, positions - offset


def rotary_tables(places):
    freqs = jnp.exp(
        jnp.arange(HEAD_DIM // 2, dtype=F32) * (-2.0 * math.log(10000.0) / HEAD_DIM)
    )
    angles = places.astype(F32)[:, None] * freqs[None, :]
    cosine, sine = jnp.cos(angles), jnp.sin(angles)
    return (
        jnp.concatenate([cosine, cosine], axis=1)[:, None, :],
        jnp.concatenate([-sine, sine], axis=1)[:, None, :],
    )


def rotate(v, tables, sign):
    frames, width = v.shape
    shaped = v.reshape(frames, width // HEAD_DIM, HEAD_DIM)
    half = HEAD_DIM // 2
    swapped = jnp.concatenate([shaped[..., half:], shaped[..., :half]], axis=-1)
    return (shaped * tables[0] + swapped * (sign * tables[1])).reshape(frames, width)


def rms_parts(hidden):
    return lax.rsqrt(jnp.mean(hidden * hidden, axis=-1, keepdims=True) + EPSILON)


def rms_back(hidden, inverse, gain, grad):
    scaled = hidden * inverse
    weighted = grad * gain
    inner = jnp.mean(weighted * scaled, axis=-1, keepdims=True)
    return inverse * (weighted - scaled * inner), jnp.sum(grad * scaled, axis=0)


def gelu_both(t):
    bell = 0.5 * (1.0 + lax.erf(t * 0.7071067811865476))
    return t * bell, bell + t * (0.3989422804014327 * jnp.exp(-0.5 * t * t))


TOK = 176
MESH_ID = pl.DeviceIdType.MESH


def flip_low(u):
    return u + 1 - 2 * lax.rem(u, 2)


def flip_high(u):
    return u + 2 - 4 * lax.div(u, 2)


def swap_bits(u):
    return 2 * lax.rem(u, 2) + lax.div(u, 2)


class Sender:
    def __init__(self, send, recv, load):
        self.send, self.recv, self.load = send, recv, load
        self.n = self.m = 0
        self.sent, self.kept = [], []

    def remote(self, src, dst, device, arrival=None):
        copy = pltpu.make_async_remote_copy(
            src_ref=src,
            dst_ref=dst,
            send_sem=self.send.at[self.n],
            recv_sem=self.recv.at[self.n] if arrival is None else arrival,
            device_id=device,
            device_id_type=MESH_ID,
        )
        self.n += 1
        return copy

    def push(self, src, dst, device):
        copy = self.remote(src, dst, device)
        copy.start()
        self.sent.append(copy)
        return copy

    def push_or_keep(self, src, dst, device, own, arrival=None):
        arrival = self.recv.at[self.n] if arrival is None else arrival
        inside = pltpu.make_async_copy(src, dst, arrival)
        copy = self.remote(src, dst, device, arrival)

        @pl.when(own)
        def _():
            inside.start()

        @pl.when(jnp.logical_not(own))
        def _():
            copy.start()

        self.kept.append((copy, own))
        return copy

    def local(self, src, dst):
        copy = pltpu.make_async_copy(src, dst, self.load.at[self.m])
        self.m += 1
        copy.start()
        return copy

    def finish(self):
        for copy in self.sent:
            copy.wait_send()
        for copy, own in self.kept:

            @pl.when(jnp.logical_not(own))
            def _(copy=copy):
                copy.wait_send()

        self.sent, self.kept = [], []


def plane_peers(u, z, x):
    peers = []
    for k in range(8):
        a = flip_low(u) if k & 2 else u
        a = flip_high(a) if k & 4 else a
        b = 1 - x if k & 1 else x
        peers.append(((a, z, b), 2 * a + b))
    return peers


def rows_of(p, start=0, size=TOK):
    return pl.ds(pl.multiple_of(p * TOK + start, 16), size)


def gather_blocks(sender, buffer, peers, use):
    me = peers[0][1]
    low, high = 80, 96

    def block(k, start=0, size=TOK):
        return buffer.at[rows_of(peers[k][1], start, size)]

    own_c = sender.push(block(0), block(0), peers[2][0])
    own_x = sender.push(block(0), block(0), peers[1][0])
    own_y = sender.push(block(0), block(0), peers[4][0])
    use(0)
    own_c.wait_recv()
    use(2)
    own_x.wait_recv()
    over_y = sender.push(block(1, low, high), block(1, low, high), peers[4][0])
    core_x = sender.push(block(1), block(1), peers[2][0])
    own_y.wait_recv()
    over_x = sender.push(block(4, 0, low), block(4, 0, low), peers[1][0])
    core_y = sender.push(block(4), block(4), peers[2][0])
    use(1)
    use(4)
    core_x.wait_recv()
    use(3)
    core_y.wait_recv()
    use(6)
    over_x.wait_recv()
    over_y.wait_recv()
    core_xy = sender.push(block(5), block(5), peers[2][0])
    use(5)
    core_xy.wait_recv()
    use(7)


def first_kernel(
    lens_ref,
    inputs_ref,
    skip_ref,
    cot_ref,
    w_skip_ref,
    w_qkv_ref,
    gain_ref,
    entry_out,
    cot_out,
    joined_out,
    normed_out,
    q_out,
    k_out,
    v_out,
    o_out,
    lse_out,
    cos_out,
    sin_out,
    seg_out,
    mixed_out,
    xin,
    xskip,
    wskip,
    wqkv,
    ent_send,
    jperm,
    cot_r,
    joined_r,
    lens_r,
    ent_r,
    n1,
    q,
    k,
    v,
    o,
    lse,
    cos_t,
    sin_t,
    seg_col,
    mixed,
    acc,
    out_t,
    send,
    recv,
    load,
    spread_recv,
):
    u, z, x = (lax.axis_index(a) for a in AXES)
    me = 2 * u + x
    peers = plane_peers(u, z, x)
    d = xin.shape[1]
    frames = n1.shape[0]
    plane = swap_bits(u)
    away = (z, plane, x)
    stays = jnp.logical_and(u == z, plane == z)
    sender = Sender(send, recv, load)

    got_x = sender.local(inputs_ref, xin)
    got_s = sender.local(skip_ref, xskip)
    got_w = sender.local(w_skip_ref, wskip)
    got_q = [
        sender.local(
            w_qkv_ref.at[:, pl.ds(pl.multiple_of(c * d + me * 128, 128), 128)],
            wqkv.at[:, pl.ds(c * 128, 128)],
        )
        for c in range(3)
    ]
    sent_lens = sender.push_or_keep(lens_ref, lens_r, away, stays)
    got_x.wait()
    got_s.wait()
    got_w.wait()
    sent_entry = []
    for n in range(2):
        part = slice(n * d // 2, (n + 1) * d // 2)
        value = dot_nn(xin[...], wskip[:d, part]) + dot_nn(xskip[...], wskip[d:, part])
        ent_send[:, part] = value.astype(BF)
        sent_entry.append(
            sender.push_or_keep(ent_send.at[:, part], ent_r.at[:, part], away, stays)
        )

    lane = lax.broadcasted_iota(jnp.int32, (TOK, 128), 1)
    for a in range(4):
        for b in range(2):
            for pair in range(2):
                halves = []
                for s in range(2):
                    block = 4 * (2 * pair + s) + 2 * b + a // 2
                    source = xin if block < d // 128 else xskip
                    first = block % (d // 128) * 128
                    piece = source[:, first : first + 128].astype(F32)
                    if a % 2 != s:
                        piece = pltpu.roll(piece, 64, 1)
                    halves.append(piece)
                place = (2 * a + b) * 256 + pair * 128
                jperm[:, place : place + 128] = jnp.where(lane < 64, halves[0], halves[1]).astype(BF)

    sent_lens.wait_recv()
    spread = lax.broadcasted_iota(jnp.int32, (TOK, 128), 1)
    freqs = jnp.exp(
        lax.rem(spread, 32).astype(F32) * (-2.0 * math.log(10000.0) / HEAD_DIM)
    )
    sign = jnp.where(lax.rem(spread, 64) < 32, -1.0, 1.0)
    slots = 6

    def table(i, _):
        rows = rows_of(i)
        at = (lax.broadcasted_iota(jnp.int32, (TOK, 128), 0) + i * TOK).astype(F32)
        place, segment, end = at, jnp.zeros_like(at), jnp.zeros((1, 128), F32)
        for s in range(slots):
            length = lens_r[s : s + 1, :]
            end = end + length
            past = at >= end
            segment = segment + jnp.where(past, 1.0, 0.0)
            place = place - jnp.where(past, length, 0.0)
        angle = place * freqs
        cos_t[rows, :] = jnp.cos(angle)
        sin_t[rows, :] = jnp.sin(angle) * sign
        seg_col[rows, :] = segment
        return 0

    lax.fori_loop(0, frames // TOK, table, 0)
    at = lax.broadcasted_iota(jnp.int32, (1, frames), 1).astype(F32)
    segment_row, end = jnp.zeros((1, frames), F32), jnp.zeros((1, 1), F32)
    for s in range(slots):
        end = end + lens_r[s : s + 1, 0:1]
        segment_row = segment_row + jnp.where(at >= end, 1.0, 0.0)

    lse[2:3, :] = segment_row
    for copy in sent_entry:
        copy.wait_recv()
    entry = ent_r[...].astype(F32)
    n1[rows_of(me), :] = (entry * rms_parts(entry) * gain_ref[...]).astype(BF)
    outs = [sender.local(ent_r, entry_out)]
    for copy in got_q:
        copy.wait()

    later = []

    def use(i):
        rows = rows_of(peers[i][1])
        value = dot_nn(n1[rows, :], wqkv[...])
        cosine, sine = cos_t[rows, :], sin_t[rows, :]
        front = lax.rem(lax.broadcasted_iota(jnp.int32, (TOK, 128), 1), 64) < 32

        def turn(t):
            swapped = jnp.where(front, pltpu.roll(t, 96, 1), pltpu.roll(t, 32, 1))
            return t * cosine + swapped * sine

        q[rows, :] = (turn(value[:, :128]).astype(BF).astype(F32) * HEAD_DIM**-0.5).astype(BF)
        k[rows, :] = turn(value[:, 128:256]).astype(BF)
        v[rows, :] = value[:, 256:].astype(BF)
        if i == 0:
            later.append(sender.push_or_keep(cot_ref, cot_r, away, stays))

    gather_blocks(sender, n1, peers, use)
    outs.append(sender.local(n1, normed_out))
    for a in range(4):
        for b in range(2):
            own = jnp.logical_and(jnp.logical_and(u == a, x == b), plane == z)
            sender.push_or_keep(
                jperm.at[:, pl.ds((2 * a + b) * 256, 256)],
                joined_r.at[rows_of(2 * z + x)],
                (a, plane, b),
                own,
                spread_recv.at[2 * z + x],
            )

    forward_heads(q, k, v, seg_col, segment_row, o, lse, acc, out_t)
    for src, dst in ((q, q_out), (k, k_out), (v, v_out), (o, o_out), (lse, lse_out)):
        outs.append(sender.local(src, dst))
    for src, dst in ((cos_t, cos_out), (sin_t, sin_out), (seg_col, seg_out)):
        outs.append(sender.local(src, dst))
    arrivals = [
        sender.push(
            o.at[rows_of(peers[i][1])],
            mixed.at[:, pl.ds(pl.multiple_of(me * 128, 128), 128)],
            peers[i][0],
        )
        for i in range(1, 8)
    ]
    own = sender.local(
        o.at[rows_of(me)], mixed.at[:, pl.ds(pl.multiple_of(me * 128, 128), 128)]
    )
    own.wait()
    for copy in arrivals:
        copy.wait_recv()
    outs.append(sender.local(mixed, mixed_out))
    for copy in later:
        copy.wait_recv()
    for s in range(8):
        rows = pl.ds(s * TOK, TOK)
        pltpu.make_async_copy(joined_r.at[rows], joined_r.at[rows], spread_recv.at[s]).wait()
    outs.append(sender.local(cot_r, cot_out))
    outs.append(sender.local(joined_r, joined_out))
    for copy in outs:
        copy.wait()
    sender.finish()


def call_first(lens, inputs, skip_in, cotangent, w_skip, w_qkv, gain_one):
    d = inputs.shape[1]
    group = 8 * TOK
    any_space = pl.BlockSpec(memory_space=pl.ANY)
    vmem = pl.BlockSpec(memory_space=pltpu.VMEM)
    wide, head, table = (group, d), ((group, 128), BF), ((group, 128), F32)
    outs = [
        ((TOK, d), BF),
        ((TOK, d), BF),
        ((group, 256), BF),
        (wide, BF),
        head,
        head,
        head,
        head,
        ((8, group), F32),
        table,
        table,
        table,
        ((TOK, d), BF),
    ]
    scratch = [
        ((TOK, d), BF),
        ((TOK, d), BF),
        ((2 * d, d), BF),
        ((d, 384), BF),
        ((TOK, d), BF),
        ((TOK, 2 * d), BF),
        ((TOK, d), BF),
        ((group, 256), BF),
        ((8, 128), F32),
        ((TOK, d), BF),
        (wide, BF),
        head,
        head,
        head,
        head,
        ((8, group), F32),
        table,
        table,
        table,
        ((TOK, d), BF),
        ((128, group), F32),
        ((128, group), F32),
    ]
    return pl.pallas_call(
        first_kernel,
        in_specs=[vmem] + [any_space] * 5 + [vmem],
        out_specs=[any_space] * len(outs),
        out_shape=[jax.ShapeDtypeStruct(*o) for o in outs],
        scratch_shapes=[pltpu.VMEM(*s) for s in scratch]
        + [pltpu.SemaphoreType.DMA((40,))] * 3
        + [pltpu.SemaphoreType.DMA((8,))],
        compiler_params=pltpu.CompilerParams(
            vmem_limit_bytes=56 * 2**20, has_side_effects=True
        ),
        name="entry_to_mixed",
    )(lens, inputs, skip_in, cotangent, w_skip, w_qkv, gain_one)


def rms_back_rows(hidden, inverse, gain, grad):
    scaled = hidden * inverse
    weighted = grad * gain
    inner = jnp.mean(weighted * scaled, axis=-1, keepdims=True)
    return inverse * (weighted - scaled * inner), jnp.sum(grad * scaled, axis=0, keepdims=True)


class PlaneGather:
    LOW, HIGH = 80, 96

    def __init__(self, sender, buffer, peers):
        self.sender, self.buffer, self.peers = sender, buffer, peers

    def block(self, k, start=0, size=TOK):
        return self.buffer.at[rows_of(self.peers[k][1], start, size)]

    def pass_on(self, k, to, start=0, size=TOK):
        block = self.block(k, start, size)
        copy = self.sender.remote(block, block, self.peers[to][0])
        copy.start()
        self.copies.append(copy)
        return copy

    def start(self):
        self.copies = []
        self.x = self.pass_on(0, 1)
        self.y = self.pass_on(0, 4)
        self.waits = [self.pass_on(0, 2)]

    def forward(self):
        self.x.wait_recv()
        self.over_y = self.pass_on(1, 4, self.LOW, self.HIGH)
        self.waits.append(self.pass_on(1, 2))
        self.y.wait_recv()
        self.over_x = self.pass_on(4, 1, 0, self.LOW)
        self.waits.append(self.pass_on(4, 2))

    def corner(self):
        self.over_x.wait_recv()
        self.over_y.wait_recv()
        self.waits.append(self.pass_on(5, 2))

    def done(self):
        for copy in self.waits:
            copy.wait_recv()
        for copy in self.copies:
            copy.wait_send()


class PlaneSum:
    def __init__(self, sender, terms, first, second, third, place):
        self.sender, self.terms = sender, terms
        self.first, self.second, self.third = first, second, third
        u, z, x = place
        self.low, self.high = lax.rem(z, 2), lax.div(z, 2)
        self.near, self.far = (u, flip_low(z), x), (u, flip_high(z), x)
        self.rows = third.shape[0]

    def chunk(self, j, low):
        return pl.ds(pl.multiple_of((2 * j + low) * self.rows, self.rows), self.rows)

    def start(self):
        self.waits = [
            self.sender.push(
                self.terms.at[self.chunk(j, 1 - self.low)], self.first.at[j], self.near
            )
            for j in range(2)
        ]

    def middle(self):
        for copy in self.waits:
            copy.wait_recv()
        for j in range(2):
            own = self.terms[self.chunk(j, self.low), :].astype(F32)
            self.second[j] = (own + self.first[j].astype(F32)).astype(BF)
        self.wait = self.sender.push(self.second.at[1 - self.high], self.third, self.far)

    def end(self, out):
        self.wait.wait_recv()
        out[...] = (self.second[self.high].astype(F32) + self.third[...].astype(F32)).astype(BF)


def second_kernel(
    entry_ref,
    cot_ref,
    joined_ref,
    normed_ref,
    q_ref,
    k_ref,
    v_ref,
    o_ref,
    lse_ref,
    cos_ref,
    sin_ref,
    seg_ref,
    mixed_ref,
    w_out_ref,
    w_up_ref,
    w_down_ref,
    w_qkv_ref,
    w_skip_ref,
    gain_one_ref,
    gain_two_ref,
    b_up_ref,
    b_up_own_ref,
    b_down_ref,
    result_out,
    inputs_out,
    skip_out,
    g_skip_out,
    g_qkv_out,
    g_out_out,
    g_up_out,
    g_down_out,
    vector_out,
    wide_a,
    wide_b,
    w_out,
    n2,
    ct,
    db,
    joined,
    q,
    k,
    v,
    o,
    grad,
    lse,
    cos_t,
    sin_t,
    seg,
    entry,
    mixed,
    middle,
    down_sum,
    normed_sum,
    result,
    result_r,
    d_mixed,
    d_heads,
    d_frames,
    entry_r,
    gd,
    gu,
    gq,
    gs,
    go,
    d1,
    d2,
    d3,
    dz,
    u1,
    u2,
    u3,
    uz,
    q1,
    q2,
    q3,
    qz,
    s1,
    s2,
    s3,
    sz,
    o1,
    o2,
    fin_d,
    fin_u,
    fin_q,
    fin_s,
    fin_o,
    vec,
    vec_plane,
    vec_sum,
    vec_z,
    acc,
    send,
    recv,
    load,
    spread,
):
    u, z, x = (lax.axis_index(a) for a in AXES)
    me = 2 * u + x
    peers = plane_peers(u, z, x)
    place = (u, z, x)
    d = entry.shape[1]
    group = n2.shape[0]
    hidden = wide_a.shape[1]
    own_home = swap_bits(z)
    home = (own_home, u, x)
    stays = jnp.logical_and(own_home == u, u == z)
    sender = Sender(send, recv, load)
    mine = rows_of(me)

    got_cot = sender.local(cot_ref, ct.at[mine])
    got_entry = sender.local(entry_ref, entry)
    got_mixed = sender.local(mixed_ref, mixed)
    got_out = sender.local(w_out_ref, w_out)
    got_up = sender.local(w_up_ref, wide_a)
    got_down = sender.local(w_down_ref, wide_b)
    got_heads = [
        sender.local(a, b)
        for a, b in (
            (q_ref, q),
            (k_ref, k),
            (v_ref, v),
            (o_ref, o),
            (lse_ref, lse),
            (cos_ref, cos_t),
            (sin_ref, sin_t),
            (seg_ref, seg),
            (joined_ref, joined),
        )
    ]
    got_cot.wait()
    gather_cot = PlaneGather(sender, ct, peers)
    gather_cot.start()

    got_entry.wait()
    got_mixed.wait()
    got_out.wait()
    value = entry[...].astype(F32) + dot_nn(mixed[...], w_out[...])
    middle[...] = value
    n2[mine, :] = (value * rms_parts(value) * gain_two_ref[...]).astype(BF)
    gather_normed = PlaneGather(sender, n2, peers)
    gather_normed.start()

    down_sum[...] = jnp.zeros_like(down_sum)
    normed_sum[...] = jnp.zeros_like(normed_sum)
    got_up.wait()
    got_down.wait()
    step = 512

    def feed(c, _):
        cols = pl.ds(pl.multiple_of(c * step, step), step)
        up = dot_nn(n2[mine, :], wide_a[:, cols]) + b_up_ref[pl.ds(c, 1), :]
        active, slope = gelu_both(up)
        d_up = (dot_nt(ct[mine, :], wide_b[cols, :]) * slope).astype(BF)
        down_sum[...] += dot_nn(active.astype(BF), wide_b[cols, :])
        normed_sum[...] += dot_nt(d_up, wide_a[:, cols])
        vec[pl.ds(8 + c, 1), :] = jnp.sum(d_up.astype(F32), axis=0, keepdims=True)
        return 0

    half = hidden // step // 2
    lax.fori_loop(0, half, feed, 0)
    gather_cot.forward()
    lax.fori_loop(half, 2 * half, feed, 0)
    gather_cot.corner()

    value = middle[...]
    result[...] = (value + down_sum[...] + b_down_ref[...]).astype(BF)
    sent_result = sender.push_or_keep(result, result_r, home, stays)
    inverse = rms_parts(value)
    back, g_gain_two = rms_back_rows(value, inverse, gain_two_ref[...], normed_sum[...])
    grad_out = ct[mine, :].astype(F32)
    d_middle = grad_out + back
    middle[...] = d_middle
    g_b_down = jnp.sum(grad_out, axis=0, keepdims=True)
    for i in range(2):
        part = slice(i * d // 2, (i + 1) * d // 2)
        vec[2 + i : 3 + i, :] = g_gain_two[:, part]
        vec[4 + i : 5 + i, :] = g_b_down[:, part]
    vec[6:8, :] = jnp.zeros((2, step), F32)
    db[mine, :] = d_middle.astype(BF)
    d_mixed[...] = dot_nt(db[mine, :], w_out[...]).astype(BF)
    own_grad = sender.local(
        d_mixed.at[:, pl.ds(pl.multiple_of(me * 128, 128), 128)], grad.at[mine]
    )
    got_grad = [
        sender.push(
            d_mixed.at[:, pl.ds(pl.multiple_of(peers[i][1] * 128, 128), 128)],
            grad.at[mine],
            peers[i][0],
        )
        for i in range(1, 8)
    ]
    gather_normed.forward()
    gather_branch = PlaneGather(sender, db, peers)
    gather_branch.start()
    gather_normed.corner()
    gather_cot.done()
    gather_normed.done()

    chunk = hidden // 32

    def own_units(w_up_own, w_down_own, active, d_up):
        copies = []
        for s in range(4):
            first = pl.multiple_of((2 * s + x) * (4 * chunk) + u * chunk, chunk)
            copies.append(
                sender.local(w_up_ref.at[:, pl.ds(first, chunk)], w_up_own.at[:, pl.ds(s * chunk, chunk)])
            )
            copies.append(
                sender.local(w_down_ref.at[pl.ds(first, chunk)], w_down_own.at[pl.ds(s * chunk, chunk)])
            )
        for copy in copies:
            copy.wait()

        def units(i, _):
            rows = rows_of(i)
            up = dot_nn(n2[rows, :], w_up_own[...]) + b_up_own_ref[...]
            act, slope = gelu_both(up)
            active[rows, :] = act.astype(BF)
            d_up[rows, :] = (dot_nt(ct[rows, :], w_down_own[...]) * slope).astype(BF)
            return 0

        lax.fori_loop(0, group // TOK, units, 0)

        def down_terms(i, _):
            cols = pl.ds(pl.multiple_of(i * 256, 256), 256)
            gd[cols, :] = dot_tn(active[:, cols], ct[...]).astype(BF)
            return 0

        lax.fori_loop(0, 4 * chunk // 256, down_terms, 0)

        def up_terms(i, _):
            cols = pl.ds(pl.multiple_of(i * 256, 256), 256)
            gu[cols, :] = dot_tn(n2[:, cols], d_up[...]).astype(BF)
            return 0

        lax.fori_loop(0, d // 256, up_terms, 0)

    pl.run_scoped(
        own_units,
        pltpu.VMEM((d, 4 * chunk), BF),
        pltpu.VMEM((4 * chunk, d), BF),
        pltpu.VMEM((group, 4 * chunk), BF),
        pltpu.VMEM((group, 4 * chunk), BF),
    )
    sum_down = PlaneSum(sender, gd, d1, d2, d3, place)
    sum_up = PlaneSum(sender, gu, u1, u2, u3, place)
    sum_down.start()
    sum_up.start()
    gather_branch.forward()
    got_normed = sender.local(normed_ref, ct)
    got_qkv = sender.local(w_qkv_ref, wide_a.at[:, pl.ds(0, 3 * d)])
    got_skip = sender.local(w_skip_ref, wide_b.at[pl.ds(0, 2 * d)])
    for copy in got_heads:
        copy.wait()
    own_grad.wait()
    for copy in got_grad:
        copy.wait_recv()

    def heads(dq, dk, dv):
        backward_heads(
            q, k, v, o, grad, seg, lse[2:3, :], lse, dq, dk, dv, acc
        )

        def turn_back(i, _):
            rows = rows_of(i)
            cosine, sine = cos_t[rows, :], sin_t[rows, :]
            front = lax.rem(lax.broadcasted_iota(jnp.int32, (TOK, 128), 1), 64) < 32
            for c, ref in ((0, dq), (1, dk)):
                t = ref[rows, :].astype(BF).astype(F32)
                swapped = jnp.where(front, pltpu.roll(t, 96, 1), pltpu.roll(t, 32, 1))
                d_heads[c, rows, :] = (t * cosine - swapped * sine).astype(BF)
            d_heads[2, rows, :] = dv[rows, :].astype(BF)
            return 0

        lax.fori_loop(0, group // TOK, turn_back, 0)

    pl.run_scoped(heads, *[pltpu.VMEM((group, 128), F32)] * 3)
    own_frames = sender.local(
        d_heads.at[:, mine], d_frames.at[:, :, pl.ds(pl.multiple_of(me * 128, 128), 128)]
    )
    got_frames = [
        sender.push(
            d_heads.at[:, rows_of(peers[i][1])],
            d_frames.at[:, :, pl.ds(pl.multiple_of(me * 128, 128), 128)],
            peers[i][0],
        )
        for i in range(1, 8)
    ]
    gather_branch.corner()
    sum_down.middle()
    sum_up.middle()
    got_normed.wait()

    def qkv_terms(i, _):
        cols = pl.ds(pl.multiple_of(i * 256, 256), 256)
        turned = ct[:, cols].T
        for c in range(3):
            gq[cols, c * 128 : (c + 1) * 128] = dot_nn(turned, d_heads[c]).astype(BF)
        return 0

    lax.fori_loop(0, d // 256, qkv_terms, 0)
    sum_qkv = PlaneSum(sender, gq, q1, q2, q3, place)
    sum_qkv.start()
    gather_branch.done()
    go[...] = dot_tn(o[...], db[...]).astype(BF)

    same_high = lax.div(z, 2) == lax.div(u, 2)
    same_low = lax.rem(z, 2) == lax.rem(u, 2)
    owner = z == u
    to_far = sender.remote(go, o1, (u, flip_high(z), x))
    to_near = sender.remote(go, o2, (u, flip_low(z), x))

    @pl.when(jnp.logical_not(same_high))
    def _():
        to_far.start()

    own_frames.wait()
    for copy in got_frames:
        copy.wait_recv()
    got_qkv.wait()
    d_normed = dot_nt(d_frames[0], wide_a[:, :d])
    d_normed += dot_nt(d_frames[1], wide_a[:, d : 2 * d])
    d_normed += dot_nt(d_frames[2], wide_a[:, 2 * d : 3 * d])
    value = entry[...].astype(F32)
    back, g_gain_one = rms_back_rows(value, rms_parts(value), gain_one_ref[...], d_normed)
    for i in range(2):
        vec[i : i + 1, :] = g_gain_one[:, i * d // 2 : (i + 1) * d // 2]
    n2[mine, :] = (middle[...] + back).astype(BF)
    gather_entry = PlaneGather(sender, n2, peers)
    gather_entry.start()
    sent_entry = sender.push_or_keep(n2.at[mine], entry_r, home, stays)

    got_vec = [
        sender.push(vec, vec_plane.at[pl.ds(pl.multiple_of(me * 16, 16), 16)], peers[i][0])
        for i in range(1, 8)
    ]
    vec_plane[pl.ds(pl.multiple_of(me * 16, 16), 16), :] = vec[...]

    @pl.when(same_high)
    def _():
        to_far.wait_recv()
        go[...] = (go[...].astype(F32) + o1[...].astype(F32)).astype(BF)

    sum_qkv.middle()
    sum_down.end(dz)
    sum_up.end(uz)

    final_d = [
        sender.push(dz, fin_d.at[pl.ds(pl.multiple_of(u * 128, 128), 128)], peers[i][0])
        for i in (2, 4, 6)
    ]
    fin_d[pl.ds(pl.multiple_of(u * 128, 128), 128), :] = dz[...]

    def rows_for(device, rows):
        return pl.ds(pl.multiple_of(device[2] * rows, rows), rows)

    def to_columns(source, fin):
        copies = [
            sender.push(source.at[rows_for(peers[i][0], 128)], fin.at[me], peers[i][0])
            for i in range(1, 8)
        ]
        fin[me] = source[rows_for(place, 128), :]
        return copies

    final_u = to_columns(uz, fin_u)

    @pl.when(jnp.logical_and(same_high, jnp.logical_not(same_low)))
    def _():
        to_near.start()

    @pl.when(owner)
    def _():
        to_near.wait_recv()
        fin_o[...] = (go[...].astype(F32) + o2[...].astype(F32)).astype(BF)

    tell = [
        pltpu.make_async_remote_copy(
            src_ref=fin_o,
            dst_ref=fin_o,
            send_sem=spread.at[i],
            recv_sem=spread.at[3],
            device_id=peers[2 * (i + 1)][0],
            device_id_type=MESH_ID,
        )
        for i in range(3)
    ]

    @pl.when(owner)
    def _():
        for copy in tell:
            copy.start()

    def skip_terms(i):
        rows = rows_of(peers[i][1])
        return dot_tn(joined[rows, :], n2[rows, :])

    total = skip_terms(0)
    gather_entry.forward()
    total += skip_terms(1)
    total += skip_terms(4)
    gather_entry.corner()
    total += skip_terms(5)
    gather_entry.done()
    for i in (2, 3, 6, 7):
        total += skip_terms(i)
    gs[...] = total.astype(BF)
    sum_skip = PlaneSum(sender, gs, s1, s2, s3, place)
    sum_skip.start()

    for copy in got_vec:
        copy.wait_recv()
    value = vec_plane[0:16, :]
    for i in range(1, 8):
        value += vec_plane[16 * i : 16 * (i + 1), :]
    vec_sum[...] = value
    z_devices = (
        (u, flip_low(z), x),
        (u, flip_high(z), x),
        (u, flip_low(flip_high(z)), x),
    )
    got_vec = [
        sender.push(vec_sum, vec_z.at[pl.ds(pl.multiple_of(z * 16, 16), 16)], device)
        for device in z_devices
    ]
    vec_z[pl.ds(pl.multiple_of(z * 16, 16), 16), :] = vec_sum[...]

    sum_qkv.end(qz)
    final_q = to_columns(qz, fin_q)

    sent_entry.wait_recv()
    got_skip.wait()
    outs = []
    for i, (staged, out) in enumerate(((mixed, inputs_out), (entry, skip_out))):
        staged[...] = dot_nt(entry_r[...], wide_b[i * d : (i + 1) * d, :]).astype(BF)
        outs.append(sender.local(staged, out))
    sum_skip.middle()
    for copy in got_vec:
        copy.wait_recv()
    vec_sum_out = vec_z[0:16, :] + vec_z[16:32, :] + vec_z[32:48, :] + vec_z[48:64, :]
    vec_plane[0:16, :] = vec_sum_out
    outs.append(sender.local(vec_plane.at[pl.ds(0, 16)], vector_out))
    sent_result.wait_recv()
    outs.append(sender.local(result_r, result_out))
    for copy in final_d + final_u + final_q:
        copy.wait_recv()
    outs.append(sender.local(fin_d, g_down_out))
    for p in range(8):
        for s in range(4):
            first = (2 * s + p % 2) * 4 * chunk + p // 2 * chunk
            outs.append(
                sender.local(
                    fin_u.at[p, :, pl.ds(s * chunk, chunk)], g_up_out.at[:, pl.ds(first, chunk)]
                )
            )
        for c in range(3):
            outs.append(
                sender.local(
                    fin_q.at[p, :, pl.ds(c * 128, 128)],
                    g_qkv_out.at[:, pl.ds(c * d + p * 128, 128)],
                )
            )

    @pl.when(owner)
    def _():
        for copy in tell:
            copy.wait_send()

    @pl.when(jnp.logical_not(same_high))
    def _():
        to_far.wait_send()

    @pl.when(jnp.logical_and(same_high, jnp.logical_not(same_low)))
    def _():
        to_near.wait_send()

    @pl.when(jnp.logical_not(owner))
    def _():
        tell[0].wait_recv()

    outs.append(sender.local(fin_o, g_out_out))
    sum_skip.end(sz)
    final_s = [
        sender.push(sz, fin_s.at[pl.ds(pl.multiple_of(u * 64, 64), 64)], peers[i][0])
        for i in (2, 4, 6)
    ]
    fin_s[pl.ds(pl.multiple_of(u * 64, 64), 64), :] = sz[...]
    for copy in final_s:
        copy.wait_recv()
    outs.append(sender.local(fin_s, g_skip_out))
    for copy in outs:
        copy.wait()
    sender.finish()


def call_second(own, weights, vectors):
    d = weights[0].shape[0]
    group = 8 * TOK
    hidden = weights[1].shape[1]
    any_space = pl.BlockSpec(memory_space=pl.ANY)
    vmem = pl.BlockSpec(memory_space=pltpu.VMEM)
    block, wide = ((TOK, d), BF), ((group, d), BF)
    head, table, total = ((group, 128), BF), ((group, 128), F32), ((TOK, d), F32)
    unit = hidden // 8

    def sums(rows, columns):
        return [
            ((2, rows, columns), BF),
            ((2, rows, columns), BF),
            ((rows, columns), BF),
            ((rows, columns), BF),
        ]

    outs = [
        block,
        block,
        block,
        ((2 * d // 8, d), BF),
        ((d // 8, 3 * d), BF),
        ((d // 8, d), BF),
        ((d // 8, hidden), BF),
        ((unit, d), BF),
        ((16, 512), F32),
    ]
    scratch = [
        ((d, hidden), BF),
        ((hidden, d), BF),
        ((d, d), BF),
        wide,
        wide,
        wide,
        ((group, 256), BF),
        head,
        head,
        head,
        head,
        head,
        ((8, group), F32),
        table,
        table,
        table,
        block,
        block,
        total,
        total,
        total,
        block,
        block,
        block,
        ((3, group, 128), BF),
        ((3, TOK, d), BF),
        block,
        ((unit, d), BF),
        ((d, unit), BF),
        ((d, 384), BF),
        ((256, d), BF),
        ((128, d), BF),
        *sums(unit // 4, d),
        *sums(d // 4, unit),
        *sums(d // 4, 384),
        *sums(64, d),
        ((128, d), BF),
        ((128, d), BF),
        ((unit, d), BF),
        ((8, d // 8, unit), BF),
        ((8, d // 8, 384), BF),
        ((256, d), BF),
        ((128, d), BF),
        ((16, 512), F32),
        ((128, 512), F32),
        ((16, 512), F32),
        ((64, 512), F32),
        ((128, group), F32),
    ]
    return pl.pallas_call(
        second_kernel,
        in_specs=[any_space] * (len(own) + len(weights)) + [vmem] * len(vectors),
        out_specs=[any_space] * len(outs),
        out_shape=[jax.ShapeDtypeStruct(*o) for o in outs],
        scratch_shapes=[pltpu.VMEM(*s) for s in scratch]
        + [pltpu.SemaphoreType.DMA((128,))] * 2
        + [pltpu.SemaphoreType.DMA((128,)), pltpu.SemaphoreType.DMA((4,))],
        compiler_params=pltpu.CompilerParams(
            vmem_limit_bytes=60 * 2**20, has_side_effects=True
        ),
        name="mixed_to_gradients",
    )(*own, *weights, *vectors)


def local(
    sizes,
    inputs,
    skip_in,
    lengths,
    cotangent,
    w_skip,
    gain_one,
    w_qkv,
    w_out,
    gain_two,
    w_up,
    b_up,
    w_down,
    b_down,
):
    n_u, n_z, n_x = sizes
    frames, d = inputs.shape
    hidden = w_up.shape[1]
    parts = n_u * n_x
    group = frames * parts
    u, z, x = (lax.axis_index(a) for a in AXES)
    me = u * n_x + x
    width = d // parts

    def line(a, b, c):
        return (a * n_z + b) * n_x + c

    def permute(v, to):
        pairs = [
            (line(a, b, c), line(*to(a, b, c)))
            for a in range(n_u)
            for b in range(n_z)
            for c in range(n_x)
        ]
        return lax.ppermute(v, AXES, pairs)

    def plane_of(a):
        return (a % 2) * (n_u // 2) + a // 2

    group_of = {plane_of(a): a for a in range(n_u)}

    def away(v):
        return permute(v, lambda a, b, c: (b, plane_of(a), c))

    def home(v):
        return permute(v, lambda a, b, c: (group_of[b], a, c))

    def swap_plane(v, bit):
        def to(a, b, c):
            other = (a * n_x + c) ^ bit
            return other // n_x, b, other % n_x

        return permute(v, to)

    plane_bits = [1 << i for i in range(parts.bit_length() - 1)]
    if n_x == 2 and n_u == 4:
        orders = ([1, 4, 2], [4, 1, 2])
    else:
        orders = (plane_bits, plane_bits)
    cut = frames // 32 * 16

    def gather_plane(v):
        pieces = []
        for piece, order in zip((v[:cut], v[cut:]), orders):
            for bit in order:
                piece = jnp.concatenate([piece, swap_plane(piece, bit)], axis=0)
            pieces.append(piece)
        return jnp.concatenate(pieces, axis=0)

    def gather_order(v):
        pieces = []
        for start, size, order in ((0, cut, orders[0]), (cut, frames - cut, orders[1])):
            offsets = [0]
            for bit in order:
                offsets = offsets + [o ^ bit for o in offsets]
            for o in offsets:
                pieces.append(
                    lax.dynamic_slice_in_dim(v, (me ^ o) * frames + start, size, axis=0)
                )
        return jnp.concatenate(pieces, axis=0)

    z_bits = n_z.bit_length() - 1

    def reduce_z(v):
        rest = v.shape[1:]
        v = v.reshape((2,) * z_bits + (v.shape[0] // n_z,) + rest)
        for bit in range(z_bits):
            axis = z_bits - 1 - bit
            own = (z >> bit) & 1
            keep = lax.dynamic_index_in_dim(v, own, axis, keepdims=False)
            give = lax.dynamic_index_in_dim(v, 1 - own, axis, keepdims=False)
            got = permute(
                give.astype(BF), lambda a, b, c, bit=bit: (a, b ^ (1 << bit), c)
            )
            v = keep.astype(F32) + got.astype(F32)
            if bit < z_bits - 1:
                v = v.astype(BF)
        return v.astype(BF)

    def finish_columns(v):
        if n_x == 2:
            v = v.reshape((2, v.shape[0] // 2) + v.shape[1:])
            keep = lax.dynamic_index_in_dim(v, x, 0, keepdims=False)
            give = lax.dynamic_index_in_dim(v, 1 - x, 0, keepdims=False)
            got = permute(give, lambda a, b, c: (a, b, 1 - c))
            both = jnp.where(x == 0, jnp.stack([keep, got]), jnp.stack([got, keep]))
        else:
            both = v[None]
        every = lax.all_gather(both, "u", axis=0)
        return every.reshape((parts,) + both.shape[1:])

    def sum_all(v):
        total = n_u * n_z * n_x
        for i in range(total.bit_length() - 1):
            bit = 1 << i
            pairs = [(n, n ^ bit) for n in range(total)]
            v = v + lax.ppermute(v, AXES, pairs)
        return v

    entry_home = dot_nn(inputs, w_skip[:d]) + dot_nn(skip_in, w_skip[d:])
    entry = away(entry_home.astype(BF)).astype(F32)
    group_lengths = away(lengths)[0]
    grad_low = away(cotangent)
    inputs_away = away(inputs)
    skip_away = away(skip_in)

    segment, places = frame_segments(group_lengths, jnp.arange(group, dtype=jnp.int32))
    own_places = lax.dynamic_slice_in_dim(places, me * frames, frames)
    tables = rotary_tables(own_places)
    col, row = segment[:, None], segment[None, :]

    inverse_one = rms_parts(entry)
    normed_one = (entry * inverse_one * gain_one).astype(BF)
    qkv = dot_nn(normed_one, w_qkv)
    query = (rotate(qkv[:, :d], tables, 1.0)).astype(BF) * BF(HEAD_DIM**-0.5)
    keys = rotate(qkv[:, d : 2 * d], tables, 1.0).astype(BF)
    values = qkv[:, 2 * d :].astype(BF)

    def to_heads(*arrays):
        n = len(arrays)
        v = jnp.stack([a.reshape(frames, parts, width) for a in arrays], axis=2)
        v = lax.all_to_all(
            v.reshape(frames, parts * n * width), PLANE, split_axis=1, concat_axis=0, tiled=True
        )
        return [v[:, i * width : (i + 1) * width] for i in range(n)]

    def to_frames(*arrays):
        n = len(arrays)
        v = jnp.concatenate(arrays, axis=1)
        v = lax.all_to_all(v, PLANE, split_axis=0, concat_axis=1, tiled=True)
        v = v.reshape(frames, parts, n, width)
        return [v[:, :, i].reshape(frames, d) for i in range(n)]

    head_query, head_keys, head_values = to_heads(query, keys, values)
    head_mixed, lse = call_forward(head_query, head_keys, head_values, col, row)
    (mixed,) = to_frames(head_mixed)

    middle = entry + dot_nn(mixed, w_out)
    inverse_two = rms_parts(middle)
    normed_two = (middle * inverse_two * gain_two).astype(BF)
    up = dot_nn(normed_two, w_up) + b_up
    d_active = dot_nt(grad_low, w_down)
    active, slope = gelu_both(up)
    d_up = (d_active * slope).astype(BF)
    result_away = (middle + dot_nn(active.astype(BF), w_down) + b_down).astype(BF)
    result = home(result_away)
    d_normed_two = dot_nt(d_up, w_up)
    middle_part, g_gain_two = rms_back(middle, inverse_two, gain_two, d_normed_two)
    d_middle = grad_low.astype(F32) + middle_part
    d_branch = d_middle.astype(BF)
    d_mixed = dot_nt(d_branch, w_out).astype(BF)
    (head_grad,) = to_heads(d_mixed)
    dq, dk, dv = call_backward(
        head_query, head_keys, head_values, head_mixed, head_grad, col, row, lse
    )

    chunk = hidden // (n_z * parts)
    w_up_own = lax.dynamic_slice(
        w_up.reshape(d, n_z, n_x, n_u, chunk), (0, 0, x, u, 0), (d, n_z, 1, 1, chunk)
    ).reshape(d, n_z * chunk)
    w_down_own = lax.dynamic_slice(
        w_down.reshape(n_z, n_x, n_u, chunk, d), (0, x, u, 0, 0), (n_z, 1, 1, chunk, d)
    ).reshape(n_z * chunk, d)
    b_up_own = lax.dynamic_slice(
        b_up.reshape(n_z, n_x, n_u, chunk), (0, x, u, 0), (n_z, 1, 1, chunk)
    ).reshape(n_z * chunk)
    plane_grad = gather_plane(grad_low)
    plane_normed = gather_plane(normed_two)
    up_own = dot_nn(plane_normed, w_up_own) + b_up_own
    active_own, slope_own = gelu_both(up_own)
    d_up_own = (dot_nt(plane_grad, w_down_own) * slope_own).astype(BF)
    g_down = dot_tn(active_own.astype(BF), plane_grad)
    g_up = dot_tn(plane_normed, d_up_own)
    down_z = reduce_z(g_down.astype(BF))
    up_z = reduce_z(g_up.astype(BF))
    out_down = lax.all_gather(down_z, "u", axis=0, tiled=True).astype(F32)
    out_up = finish_columns(up_z)
    out_up = (
        out_up.reshape(n_u, n_x, -1, n_z, chunk).transpose(2, 3, 1, 0, 4).reshape(-1, hidden)
    ).astype(F32)

    plane_mixed = gather_plane(mixed)
    own_branch = gather_order(
        lax.all_to_all(d_branch, PLANE, split_axis=1, concat_axis=0, tiled=True)
    )
    g_out = dot_tn(plane_mixed, own_branch)
    out_out = (
        finish_columns(reduce_z(g_out.astype(BF))).transpose(1, 0, 2).reshape(-1, d).astype(F32)
    )

    low = [a.astype(BF) for a in (dq, dk, dv)]
    frame_query, frame_keys, frame_values = to_frames(*low)
    d_qkv = jnp.concatenate(
        [
            rotate(frame_query.astype(F32), tables, -1.0).astype(BF),
            rotate(frame_keys.astype(F32), tables, -1.0).astype(BF),
            frame_values,
        ],
        axis=1,
    )
    d_normed_one = dot_nt(d_qkv, w_qkv)
    entry_part, g_gain_one = rms_back(entry, inverse_one, gain_one, d_normed_one)
    d_entry = (d_middle + entry_part).astype(BF)
    d_entry_home = home(d_entry)
    d_joined = dot_nt(d_entry_home, w_skip)
    d_inputs = d_joined[:, :d].astype(BF)
    d_skip = d_joined[:, d:].astype(BF)

    group_tables = rotary_tables(places)
    head_d_qkv = jnp.concatenate(
        [
            rotate(low[0].astype(F32), group_tables, -1.0).astype(BF),
            rotate(low[1].astype(F32), group_tables, -1.0).astype(BF),
            low[2],
        ],
        axis=1,
    )
    plane_first = gather_plane(normed_one)
    g_qkv = dot_tn(plane_first, gather_order(head_d_qkv))
    plane_inputs = gather_plane(inputs_away)
    plane_skip = gather_plane(skip_away)
    own_entry = gather_order(
        lax.all_to_all(d_entry, PLANE, split_axis=1, concat_axis=0, tiled=True)
    )
    g_skip = jnp.concatenate([dot_tn(plane_inputs, own_entry), dot_tn(plane_skip, own_entry)])
    out_qkv = finish_columns(reduce_z(g_qkv.astype(BF)))
    out_qkv = (
        out_qkv.reshape(parts, -1, 3, width).transpose(1, 2, 0, 3).reshape(-1, 3 * d).astype(F32)
    )
    out_skip = (
        finish_columns(reduce_z(g_skip.astype(BF))).transpose(1, 0, 2).reshape(-1, d).astype(F32)
    )

    early = sum_all(
        jnp.concatenate(
            [
                g_gain_two,
                jnp.sum(d_up.astype(F32), axis=0),
                jnp.sum(cotangent.astype(F32), axis=0),
            ]
        )
    )
    total_gain_one = sum_all(g_gain_one)
    return (
        result,
        d_inputs,
        d_skip,
        out_skip,
        total_gain_one,
        out_qkv,
        out_out,
        early[:d],
        out_up,
        early[d : d + hidden],
        out_down,
        early[d + hidden :],
    )


def local_fast(
    sizes,
    inputs,
    skip_in,
    lengths,
    cotangent,
    w_skip,
    gain_one,
    w_qkv,
    w_out,
    gain_two,
    w_up,
    b_up,
    w_down,
    b_down,
):
    n_u, n_z, n_x = sizes
    d = inputs.shape[1]
    hidden = w_up.shape[1]
    u, x = lax.axis_index("u"), lax.axis_index("x")
    lens = jnp.broadcast_to(
        jnp.pad(lengths[0].astype(F32), (0, 8 - lengths.shape[1]))[:, None], (8, 128)
    )
    b_up_own = lax.dynamic_slice(
        b_up.reshape(n_z, n_x, n_u, -1), (0, x, u, 0), (n_z, 1, 1, hidden // 32)
    ).reshape(1, -1)
    own = call_first(lens, inputs, skip_in, cotangent, w_skip, w_qkv, gain_one[None])
    result, d_inputs, d_skip, g_skip, g_qkv, g_out, g_up, g_down, vectors = call_second(
        own,
        (w_out, w_up, w_down, w_qkv, w_skip),
        (
            gain_one[None],
            gain_two[None],
            b_up.reshape(8, -1),
            b_up_own,
            b_down[None],
        ),
    )
    vectors = vectors.reshape(-1)
    return (
        result,
        d_inputs,
        d_skip,
        g_skip.astype(F32),
        vectors[:d],
        g_qkv.astype(F32),
        g_out.astype(F32),
        vectors[d : 2 * d],
        g_up.astype(F32),
        vectors[4 * d :],
        g_down.astype(F32),
        vectors[2 * d : 3 * d],
    )


def solution(mesh):
    n_u, n_s = mesh.shape["utt"], mesh.shape["seq"]
    sizes = (n_u, n_u, n_s // n_u)
    program = local_fast if sizes == (4, 4, 2) else local
    inner = Mesh(mesh.devices.reshape(sizes), AXES)
    rows, seq = P(AXES, None), P(("z", "x"), None)
    in_specs = (rows, rows, P("u", None), rows) + (P(),) * 9
    out_specs = (rows, rows, rows, seq, P(), seq, seq, P(), seq, P(), seq, P())
    return jax.shard_map(
        functools.partial(program, sizes),
        mesh=inner,
        in_specs=in_specs,
        out_specs=out_specs,
        check_vma=False,
    )
```

```python
import functools
import math

import jax
import jax.numpy as jnp
from jax import lax
from jax.experimental import pallas as pl
from jax.experimental.pallas import tpu as pltpu
from jax.sharding import Mesh, PartitionSpec as P

HEAD_DIM = 64
EPSILON = 1e-06
BF = jnp.bfloat16
F32 = jnp.float32
AXES = ("u", "z", "x")
PLANE = ("u", "x")


def dot_nn(a, b):
    return lax.dot_general(a, b, (((1,), (0,)), ((), ())), preferred_element_type=F32)


def dot_nt(a, b):
    return lax.dot_general(a, b, (((1,), (1,)), ((), ())), preferred_element_type=F32)


def dot_tn(a, b):
    return lax.dot_general(a, b, (((0,), (0,)), ((), ())), preferred_element_type=F32)


def attention_forward(q_ref, k_ref, v_ref, col_ref, row_ref, o_ref, lse_ref, acc, out_t):
    forward_heads(q_ref, k_ref, v_ref, col_ref, row_ref[...], o_ref, lse_ref, acc, out_t)


def forward_heads(q_ref, k_ref, v_ref, col_ref, segment_row, o_ref, lse_ref, acc, out_t):
    frames, width = q_ref.shape
    heads = width // HEAD_DIM
    block = frames // (frames // 352)
    lane = lax.broadcasted_iota(jnp.int32, (1, width), 1)
    for h in range(heads):
        own = (lane // HEAD_DIM == h).astype(BF)
        query = q_ref[...] * own
        acc[...] = jnp.zeros_like(acc)

        def step(j, carry):
            top, total = carry
            rows = pl.ds(pl.multiple_of(j * block, block), block)
            scores = dot_nt(k_ref[rows, :], query)
            scores = jnp.where(col_ref[rows, 0:1] == segment_row, scores, -1e30)
            peak = jnp.maximum(top, jnp.max(scores, axis=0, keepdims=True))
            expos = jnp.exp(scores - peak)
            shrink = jnp.exp(top - peak)
            acc[...] = acc[...] * shrink + dot_tn(v_ref[rows, :], expos.astype(BF))
            return peak, total * shrink + jnp.sum(expos, axis=0, keepdims=True)

        top, total = lax.fori_loop(
            0,
            frames // block,
            step,
            (jnp.full((1, frames), -1e30, F32), jnp.zeros((1, frames), F32)),
        )
        part = slice(h * HEAD_DIM, (h + 1) * HEAD_DIM)
        out_t[part, :] = acc[part, :] / total
        lse_ref[h : h + 1, :] = top + jnp.log(total)
    o_ref[...] = out_t[...].T.astype(BF)


def attention_backward(
    q_ref, k_ref, v_ref, o_ref, do_ref, col_ref, row_ref, lse_ref, dq_ref, dk_ref, dv_ref, acc
):
    backward_heads(
        q_ref, k_ref, v_ref, o_ref, do_ref, col_ref, row_ref[...], lse_ref, dq_ref, dk_ref, dv_ref, acc
    )


def backward_heads(
    q_ref, k_ref, v_ref, o_ref, do_ref, col_ref, segment_row, lse_ref, dq_ref, dk_ref, dv_ref, acc
):
    frames, width = q_ref.shape
    heads = width // HEAD_DIM
    block = frames // (frames // 352)
    lane = lax.broadcasted_iota(jnp.int32, (1, width), 1)
    product_t = (o_ref[...].astype(F32) * do_ref[...].astype(F32)).T
    for h in range(heads):
        own = (lane // HEAD_DIM == h).astype(BF)
        query = q_ref[...] * own
        grad = do_ref[...] * own
        part = slice(h * HEAD_DIM, (h + 1) * HEAD_DIM)
        delta = jnp.sum(product_t[part, :], axis=0, keepdims=True)
        log_total = lse_ref[h : h + 1, :]

        def step(j, _):
            rows = pl.ds(pl.multiple_of(j * block, block), block)
            keys = k_ref[rows, :]
            scores = dot_nt(keys, query)
            same = col_ref[rows, 0:1] == segment_row
            probs = jnp.where(same, jnp.exp(scores - log_total), 0.0)
            d_probs = dot_nt(v_ref[rows, :], grad)
            d_scores = (probs * (d_probs - delta)).astype(BF)
            value_part = dot_nn(probs.astype(BF), grad)
            key_part = dot_nn(d_scores, query)
            if h == 0:
                dv_ref[rows, :] = value_part
                dk_ref[rows, :] = key_part
            else:
                dv_ref[rows, :] += value_part
                dk_ref[rows, :] += key_part
            query_part = dot_tn(keys * own, d_scores)

            if h == 0:

                @pl.when(j == 0)
                def _():
                    acc[...] = query_part

                @pl.when(j > 0)
                def _():
                    acc[...] += query_part

            else:
                acc[...] += query_part
            return 0

        lax.fori_loop(0, frames // block, step, 0)
    dq_ref[...] = acc[...].T * (HEAD_DIM**-0.5)


def call_forward(query, keys, values, col, row):
    frames, width = query.shape
    return pl.pallas_call(
        attention_forward,
        out_shape=(
            jax.ShapeDtypeStruct((frames, width), BF),
            jax.ShapeDtypeStruct((width // HEAD_DIM, frames), F32),
        ),
        scratch_shapes=[pltpu.VMEM((width, frames), F32), pltpu.VMEM((width, frames), F32)],
        compiler_params=pltpu.CompilerParams(vmem_limit_bytes=56 * 2**20),
        cost_estimate=pl.CostEstimate(
            flops=16 * frames * frames * width, bytes_accessed=10 * frames * width, transcendentals=0
        ),
        name="attention_forward",
    )(query, keys, values, col, row)


def call_backward(query, keys, values, mixed, grad, col, row, lse):
    frames, width = query.shape
    shape = jax.ShapeDtypeStruct((frames, width), F32)
    return pl.pallas_call(
        attention_backward,
        out_shape=(shape, shape, shape),
        scratch_shapes=[pltpu.VMEM((width, frames), F32)],
        compiler_params=pltpu.CompilerParams(vmem_limit_bytes=56 * 2**20),
        cost_estimate=pl.CostEstimate(
            flops=32 * frames * frames * width, bytes_accessed=20 * frames * width, transcendentals=0
        ),
        name="attention_backward",
    )(query, keys, values, mixed, grad, col, row, lse)


def frame_segments(own_lengths, positions):
    slots = own_lengths.shape[0]
    upto = jnp.arange(slots)[:, None] >= jnp.arange(slots)[None, :]
    ends_at = jnp.sum(jnp.where(upto, own_lengths[None, :], 0), axis=1)
    starts_at = ends_at - own_lengths
    segment = jnp.sum((positions[:, None] >= ends_at[None, :]).astype(jnp.int32), axis=1)
    index = jnp.arange(slots, dtype=jnp.int32)
    offset = jnp.sum(jnp.where(segment[:, None] == index[None, :], starts_at[None, :], 0), axis=1)
    return segment, positions - offset


def rotary_tables(places):
    freqs = jnp.exp(
        jnp.arange(HEAD_DIM // 2, dtype=F32) * (-2.0 * math.log(10000.0) / HEAD_DIM)
    )
    angles = places.astype(F32)[:, None] * freqs[None, :]
    cosine, sine = jnp.cos(angles), jnp.sin(angles)
    return (
        jnp.concatenate([cosine, cosine], axis=1)[:, None, :],
        jnp.concatenate([-sine, sine], axis=1)[:, None, :],
    )


def rotate(v, tables, sign):
    frames, width = v.shape
    shaped = v.reshape(frames, width // HEAD_DIM, HEAD_DIM)
    half = HEAD_DIM // 2
    swapped = jnp.concatenate([shaped[..., half:], shaped[..., :half]], axis=-1)
    return (shaped * tables[0] + swapped * (sign * tables[1])).reshape(frames, width)


def rms_parts(hidden):
    return lax.rsqrt(jnp.mean(hidden * hidden, axis=-1, keepdims=True) + EPSILON)


def rms_back(hidden, inverse, gain, grad):
    scaled = hidden * inverse
    weighted = grad * gain
    inner = jnp.mean(weighted * scaled, axis=-1, keepdims=True)
    return inverse * (weighted - scaled * inner), jnp.sum(grad * scaled, axis=0)


def gelu_both(t):
    bell = 0.5 * (1.0 + lax.erf(t * 0.7071067811865476))
    return t * bell, bell + t * (0.3989422804014327 * jnp.exp(-0.5 * t * t))


TOK = 176
MESH_ID = pl.DeviceIdType.MESH


def flip_low(u):
    return u + 1 - 2 * lax.rem(u, 2)


def flip_high(u):
    return u + 2 - 4 * lax.div(u, 2)


def swap_bits(u):
    return 2 * lax.rem(u, 2) + lax.div(u, 2)


def both(a, b):
    return jnp.logical_and(a, b)


def rms_back_rows(hidden, inverse, gain, grad):
    scaled = hidden * inverse
    weighted = grad * gain
    inner = jnp.mean(weighted * scaled, axis=-1, keepdims=True)
    return inverse * (weighted - scaled * inner), jnp.sum(grad * scaled, axis=0, keepdims=True)


class Sender:
    def __init__(self, send, recv, load):
        self.send, self.recv, self.load = send, recv, load
        self.n = self.m = 0
        self.sent, self.kept = [], []

    def remote(self, src, dst, device, arrival=None):
        copy = pltpu.make_async_remote_copy(
            src_ref=src,
            dst_ref=dst,
            send_sem=self.send.at[self.n],
            recv_sem=self.recv.at[self.n] if arrival is None else arrival,
            device_id=device,
            device_id_type=MESH_ID,
        )
        self.n += 1
        return copy

    def push(self, src, dst, device):
        copy = self.remote(src, dst, device)
        copy.start()
        self.sent.append(copy)
        return copy

    def push_or_keep(self, src, dst, device, own, arrival=None):
        arrival = self.recv.at[self.n] if arrival is None else arrival
        inside = pltpu.make_async_copy(src, dst, arrival)
        copy = self.remote(src, dst, device, arrival)

        @pl.when(own)
        def _():
            inside.start()

        @pl.when(jnp.logical_not(own))
        def _():
            copy.start()

        self.kept.append((copy, own))
        return copy

    def local(self, src, dst):
        copy = pltpu.make_async_copy(src, dst, self.load.at[self.m])
        self.m += 1
        copy.start()
        return copy

    def finish(self):
        for copy in self.sent:
            copy.wait_send()
        for copy, own in self.kept:

            @pl.when(jnp.logical_not(own))
            def _(copy=copy):
                copy.wait_send()

        self.sent, self.kept = [], []


def plane_peers(u, z, x):
    peers = []
    for k in range(8):
        a = flip_low(u) if k & 2 else u
        a = flip_high(a) if k & 4 else a
        b = 1 - x if k & 1 else x
        peers.append(((a, z, b), 2 * a + b))
    return peers


def rows_of(p, start=0, size=TOK):
    return pl.ds(pl.multiple_of(p * TOK + start, 16), size)


class PlaneGather:
    def __init__(self, sender, buffer, peers, start=0, size=TOK):
        self.sender, self.buffer, self.peers = sender, buffer, peers
        self.first, self.size = start, size
        self.low = size // 32 * 16
        self.copies = []

    def pass_on(self, k, to, start=0, size=None):
        rows = rows_of(self.peers[k][1], self.first + start, size or self.size)
        copy = self.sender.remote(self.buffer.at[rows], self.buffer.at[rows], self.peers[to][0])
        copy.start()
        self.copies.append(copy)
        return copy

    def start(self):
        self.x = self.pass_on(0, 1)
        self.y = self.pass_on(0, 4)
        self.cores = [self.pass_on(0, 2)]

    def forward(self):
        self.x.wait_recv()
        self.over_y = self.pass_on(1, 4, self.low, self.size - self.low)
        self.cores.append(self.pass_on(1, 2))
        self.y.wait_recv()
        self.over_x = self.pass_on(4, 1, 0, self.low)
        self.cores.append(self.pass_on(4, 2))

    def corner(self):
        self.over_x.wait_recv()
        self.over_y.wait_recv()
        self.cores.append(self.pass_on(5, 2))

    def core(self, i):
        self.cores[i].wait_recv()

    def left(self):
        for copy in self.copies:
            copy.wait_send()

    def done(self):
        for copy in self.cores:
            copy.wait_recv()
        self.left()


class PlaneSum:
    def __init__(self, sender, terms, first, second, third, place):
        self.sender, self.terms = sender, terms
        self.first, self.second, self.third = first, second, third
        u, z, x = place
        self.low, self.high = lax.rem(z, 2), lax.div(z, 2)
        self.near, self.far = (u, flip_low(z), x), (u, flip_high(z), x)
        self.rows = third.shape[0]
        self.waits = [
            sender.remote(terms.at[self.chunk(j, 1 - self.low)], first.at[j], self.near)
            for j in range(2)
        ]
        sender.sent += self.waits

    def chunk(self, j, low):
        return pl.ds(pl.multiple_of((2 * j + low) * self.rows, self.rows), self.rows)

    def start(self):
        for copy in self.waits:
            copy.start()

    def middle(self):
        for copy in self.waits:
            copy.wait_recv()
        for j in range(2):
            own = self.terms[self.chunk(j, self.low), :].astype(F32)
            self.second[j] = (own + self.first[j].astype(F32)).astype(BF)
        self.wait = self.sender.push(self.second.at[1 - self.high], self.third, self.far)

    def end(self, out):
        self.wait.wait_recv()
        out[...] = (self.second[self.high].astype(F32) + self.third[...].astype(F32)).astype(BF)


class ColumnGather:
    def __init__(self, sender, source, out, peers, x):
        self.sender, self.out, self.peers = sender, out, peers
        rows = out.shape[1]
        me = peers[0][1]

        def part(b):
            return pl.ds(pl.multiple_of(b * rows, rows), rows)

        self.direct = [
            (k, sender.push(source.at[part(peers[k][0][2])], out.at[me], peers[k][0]))
            for k in (5, 4, 1)
        ]
        self.cores = [sender.push(source.at[part(x)], out.at[me], peers[2][0])]
        out[me] = source[part(x), :]

    def forward(self):
        for k, copy in self.direct:
            copy.wait_recv()
            slot = self.out.at[self.peers[k][1]]
            self.cores.append(self.sender.push(slot, slot, self.peers[2][0]))

    def done(self):
        for copy in self.cores:
            copy.wait_recv()


class RowGather:
    def __init__(self, sender, source, out, peers, u):
        self.sender, self.out, self.peers = sender, out, peers
        self.rows = source.shape[0]
        self.far = sender.push(source, out.at[self.part(u)], peers[4][0])
        self.cores = [sender.push(source, out.at[self.part(u)], peers[2][0])]
        out[self.part(u), :] = source[...]

    def part(self, u):
        return pl.ds(pl.multiple_of(u * self.rows, self.rows), self.rows)

    def forward(self):
        self.far.wait_recv()
        block = self.out.at[self.part(self.peers[4][0][0])]
        self.cores.append(self.sender.push(block, block, self.peers[2][0]))

    def done(self):
        for copy in self.cores:
            copy.wait_recv()


def layer_kernel(
    lengths_ref,
    gain_one_ref,
    gain_two_ref,
    b_up_ref,
    b_down_ref,
    inputs_ref,
    skip_ref,
    cot_ref,
    w_skip_ref,
    w_qkv_ref,
    w_out_ref,
    w_up_ref,
    w_down_ref,
    result_out,
    inputs_out,
    skip_out,
    g_skip_out,
    g_qkv_out,
    g_out_out,
    g_up_out,
    g_down_out,
    vector_out,
    normed_kept,
    wide_a,
    wide_b,
    w_out,
    n2,
    ct,
    db,
    joined,
    q,
    k,
    v,
    o,
    grad,
    lse,
    cos_t,
    sin_t,
    seg,
    entry,
    middle,
    down_sum,
    normed_sum,
    result,
    result_r,
    d_mixed,
    d_heads,
    d_frames,
    entry_r,
    gd,
    gu,
    gq,
    gs,
    go,
    d1,
    d2,
    d3,
    dz,
    u1,
    u2,
    u3,
    uz,
    q1,
    q2,
    q3,
    qz,
    s1,
    s2,
    s3,
    sz,
    o1,
    o2,
    fin_d,
    fin_u,
    fin_q,
    fin_s,
    fin_o,
    vec,
    vec_plane,
    vec_sum,
    vec_z,
    acc,
    lens,
    lens_r,
    send,
    recv,
    load,
    spread,
):
    u, z, x = (lax.axis_index(a) for a in AXES)
    me = 2 * u + x
    peers = plane_peers(u, z, x)
    place = (u, z, x)
    d = entry.shape[1]
    group = n2.shape[0]
    hidden = wide_a.shape[1]
    heads_at = pl.ds(pl.multiple_of(me * 128, 128), 128)
    plane = swap_bits(u)
    away = (z, plane, x)
    stays_away = both(u == z, plane == z)
    own_home = swap_bits(z)
    home = (own_home, u, x)
    stays_home = both(own_home == u, u == z)
    sender = Sender(send, recv, load)
    mine = rows_of(me)
    low, high = 80, 96

    got_x = sender.local(inputs_ref, gd.at[pl.ds(0, TOK)])
    got_s = sender.local(skip_ref, gd.at[pl.ds(TOK, TOK)])
    got_w = [
        sender.local(w_skip_ref.at[pl.ds(i * d, d)], wide_b.at[pl.ds(i * d, d)]) for i in range(2)
    ]
    got_q = [
        sender.local(
            w_qkv_ref.at[:, pl.ds(pl.multiple_of(c * d + me * 128, 128), 128)],
            wide_a.at[:, pl.ds(c * 128, 128)],
        )
        for c in range(3)
    ]
    slots = lengths_ref.shape[1]
    for s in range(slots):
        lens[s : s + 1, :] = jnp.full((1, 128), lengths_ref[0, s].astype(F32), F32)
    lens[slots:8, :] = jnp.zeros((8 - slots, 128), F32)
    sent_lens = sender.push_or_keep(lens, lens_r, away, stays_away)
    got_x.wait()
    got_w[0].wait()
    value = dot_nn(gd[:TOK, :], wide_b[:d, :])
    got_s.wait()
    got_w[1].wait()
    d_mixed[...] = (value + dot_nn(gd[TOK : 2 * TOK, :], wide_b[d : 2 * d, :])).astype(BF)
    sent_entry = [
        sender.push_or_keep(
            d_mixed.at[pl.ds(a, n)], entry.at[pl.ds(a, n)], away, stays_away
        )
        for a, n in ((0, low), (low, high))
    ]
    got_down = sender.local(w_down_ref, wide_b)
    got_out = sender.local(w_out_ref, w_out)

    def joined_block(j):
        return slice(j // 2 * TOK, (j // 2 + 1) * TOK), slice(j % 2 * 256, (j % 2 + 1) * 256)

    lane = lax.broadcasted_iota(jnp.int32, (TOK, 128), 1)
    for a in range(4):
        for b in range(2):
            for pair in range(2):
                halves = []
                for s in range(2):
                    block = 4 * (2 * pair + s) + 2 * b + a // 2
                    top = block // (d // 128) * TOK
                    first = block % (d // 128) * 128
                    piece = gd[top : top + TOK, first : first + 128].astype(F32)
                    if a % 2 != s:
                        piece = pltpu.roll(piece, 64, 1)
                    halves.append(piece)
                j = 2 * a + b
                gu[
                    j // 2 * TOK : (j // 2 + 1) * TOK,
                    j % 2 * 256 + pair * 128 : j % 2 * 256 + (pair + 1) * 128,
                ] = jnp.where(lane < 64, halves[0], halves[1]).astype(BF)

    sent_lens.wait_recv()
    freqs = jnp.exp(lax.rem(lane, 32).astype(F32) * (-2.0 * math.log(10000.0) / HEAD_DIM))
    front = lax.rem(lane, 64) < 32
    sign = jnp.where(front, -1.0, 1.0)

    def table(i, _):
        rows = rows_of(i)
        at = (lax.broadcasted_iota(jnp.int32, (TOK, 128), 0) + i * TOK).astype(F32)
        spot, segment, end = at, jnp.zeros_like(at), jnp.zeros((1, 128), F32)
        for s in range(slots):
            length = lens_r[s : s + 1, :]
            end = end + length
            past = at >= end
            segment = segment + jnp.where(past, 1.0, 0.0)
            spot = spot - jnp.where(past, length, 0.0)
        angle = spot * freqs
        cos_t[rows, :] = jnp.cos(angle)
        sin_t[rows, :] = jnp.sin(angle) * sign
        seg[rows, :] = segment
        return 0

    lax.fori_loop(0, group // TOK, table, 0)
    at = lax.broadcasted_iota(jnp.int32, (1, group), 1).astype(F32)
    segment_row, end = jnp.zeros((1, group), F32), jnp.zeros((1, 1), F32)
    for s in range(slots):
        end = end + lens_r[s : s + 1, 0:1]
        segment_row = segment_row + jnp.where(at >= end, 1.0, 0.0)
    lse[2:3, :] = segment_row
    for copy in got_q:
        copy.wait()

    def turn(t, rows, way):
        swapped = jnp.where(front, pltpu.roll(t, 96, 1), pltpu.roll(t, 32, 1))
        return t * cos_t[rows, :] + swapped * (way * sin_t[rows, :])

    def project(i):
        rows = rows_of(peers[i][1])
        value = dot_nn(n2[rows, :], wide_a[:, :384])
        q[rows, :] = (
            turn(value[:, :128], rows, 1.0).astype(BF).astype(F32) * HEAD_DIM**-0.5
        ).astype(BF)
        k[rows, :] = turn(value[:, 128:256], rows, 1.0).astype(BF)
        v[rows, :] = value[:, 256:].astype(BF)

    first_a = PlaneGather(sender, n2, peers, 0, low)
    first_b = PlaneGather(sender, n2, peers, low, high)
    for copy, gather, (a, n) in zip(sent_entry, (first_a, first_b), ((0, low), (low, high))):
        copy.wait_recv()
        value = entry[a : a + n, :].astype(F32)
        n2[rows_of(me, a, n), :] = (value * rms_parts(value) * gain_one_ref[...]).astype(BF)
        gather.start()
    sent_cot = sender.push_or_keep(cot_ref, ct.at[rows_of(2 * z + x)], away, stays_away)
    first_a.forward()
    project(0)
    first_a.core(0)
    first_b.core(0)
    project(2)
    first_b.forward()
    project(1)
    project(4)
    first_a.corner()
    first_b.corner()
    project(5)
    for gather in (first_a, first_b):
        gather.core(1)
    project(3)
    for gather in (first_a, first_b):
        gather.core(2)
    project(6)
    for gather in (first_a, first_b):
        gather.core(3)
    project(7)
    got_up = sender.local(w_up_ref, wide_a)
    kept_normed = sender.local(n2, normed_kept)
    sent_cot.wait_recv()
    gather_cot = PlaneGather(sender, ct, peers)
    gather_cot.start()
    for a in range(4):
        for b in range(2):
            rows, cols = joined_block(2 * a + b)
            sender.push_or_keep(
                gu.at[rows, cols],
                joined.at[rows_of(2 * z + x)],
                (a, plane, b),
                both(both(u == a, x == b), plane == z),
                spread.at[2 * z + x],
            )

    pl.run_scoped(
        lambda out_t: forward_heads(q, k, v, seg, segment_row, o, lse, acc, out_t),
        pltpu.VMEM((128, group), F32),
    )
    kept_normed.wait()
    for gather in (first_a, first_b):
        gather.left()
    own_mixed = sender.local(o.at[mine], d_frames.at[0, :, heads_at])
    got_mixed = [
        sender.push(o.at[rows_of(peers[i][1])], d_frames.at[0, :, heads_at], peers[i][0])
        for i in range(1, 8)
    ]
    gather_cot.forward()
    own_mixed.wait()
    for copy in got_mixed:
        copy.wait_recv()

    got_out.wait()
    value = entry[...].astype(F32) + dot_nn(d_frames[0], w_out[...])
    middle[...] = value
    n2[mine, :] = (value * rms_parts(value) * gain_two_ref[...]).astype(BF)
    gather_normed = PlaneGather(sender, n2, peers)
    gather_normed.start()

    down_sum[...] = jnp.zeros_like(down_sum)
    normed_sum[...] = jnp.zeros_like(normed_sum)
    got_up.wait()
    got_down.wait()
    step = 512

    def feed(c, _):
        cols = pl.ds(pl.multiple_of(c * step, step), step)
        up = dot_nn(n2[mine, :], wide_a[:, cols]) + b_up_ref[:, cols]
        active, slope = gelu_both(up)
        d_up = (dot_nt(ct[mine, :], wide_b[cols, :]) * slope).astype(BF)
        down_sum[...] += dot_nn(active.astype(BF), wide_b[cols, :])
        normed_sum[...] += dot_nt(d_up, wide_a[:, cols])
        vec[pl.ds(8 + c, 1), :] = jnp.sum(d_up.astype(F32), axis=0, keepdims=True)
        return 0

    half = hidden // step // 2
    lax.fori_loop(0, half, feed, 0)
    gather_cot.corner()
    lax.fori_loop(half, 2 * half, feed, 0)
    gather_normed.forward()
    value = middle[...]
    inverse = rms_parts(value)
    back, g_gain_two = rms_back_rows(value, inverse, gain_two_ref[...], normed_sum[...])
    grad_out = ct[mine, :].astype(F32)
    d_middle = grad_out + back
    result[...] = (value + down_sum[...] + b_down_ref[...]).astype(BF)
    middle[...] = d_middle
    db[mine, :] = d_middle.astype(BF)
    for copy, own in sender.kept[1:3]:

        @pl.when(jnp.logical_not(own))
        def _(copy=copy):
            copy.wait_send()

    sender.kept = sender.kept[:1] + sender.kept[3:]
    d_mixed[...] = dot_nt(db[mine, :], w_out[...]).astype(BF)
    own_grad = sender.local(d_mixed.at[:, heads_at], grad.at[mine])
    got_grad = [
        sender.push(
            d_mixed.at[:, pl.ds(pl.multiple_of(peers[i][1] * 128, 128), 128)],
            grad.at[mine],
            peers[i][0],
        )
        for i in range(1, 8)
    ]
    sent_result = sender.push_or_keep(result, result_r, home, stays_home)
    g_b_down = jnp.sum(grad_out, axis=0, keepdims=True)
    for i in range(2):
        part = slice(i * d // 2, (i + 1) * d // 2)
        vec[2 + i : 3 + i, :] = g_gain_two[:, part]
        vec[4 + i : 5 + i, :] = g_b_down[:, part]
    vec[6:8, :] = jnp.zeros((2, step), F32)
    gather_cot.done()
    gather_normed.corner()
    gather_branch = PlaneGather(sender, db, peers)
    gather_branch.start()
    gather_normed.done()
    for j in range(8):
        rows, cols = joined_block(j)
        copy, own = sender.kept[2 + j]

        @pl.when(jnp.logical_not(own))
        def _(copy=copy):
            copy.wait_send()

    sender.kept = sender.kept[:2] + sender.kept[10:]
    for s in range(8):
        rows = pl.ds(s * TOK, TOK)
        pltpu.make_async_copy(joined.at[rows], joined.at[rows], spread.at[s]).wait()

    chunk = hidden // 32
    sum_down = PlaneSum(sender, gd, d1, d2, d3, place)
    sum_up = PlaneSum(sender, gu, u1, u2, u3, place)

    def own_units(w_up_own, w_down_own, active, d_up):
        copies, starts = [], []
        for s in range(4):
            first = pl.multiple_of((2 * s + x) * (4 * chunk) + u * chunk, chunk)
            starts.append(first)
            copies.append(
                sender.local(
                    w_up_ref.at[:, pl.ds(first, chunk)], w_up_own.at[:, pl.ds(s * chunk, chunk)]
                )
            )
            copies.append(
                sender.local(
                    w_down_ref.at[pl.ds(first, chunk)], w_down_own.at[pl.ds(s * chunk, chunk)]
                )
            )
        for copy in copies:
            copy.wait()
        bias = jnp.concatenate([b_up_ref[:, pl.ds(first, chunk)] for first in starts], axis=1)

        def units(i, _):
            rows = rows_of(i)
            up = dot_nn(n2[rows, :], w_up_own[...]) + bias
            act, slope = gelu_both(up)
            active[rows, :] = act.astype(BF)
            d_up[rows, :] = (dot_nt(ct[rows, :], w_down_own[...]) * slope).astype(BF)
            return 0

        lax.fori_loop(0, group // TOK, units, 0)

        def down_terms(i, _):
            cols = pl.ds(pl.multiple_of(i * 256, 256), 256)
            gd[cols, :] = dot_tn(active[:, cols], ct[...]).astype(BF)
            return 0

        lax.fori_loop(0, 4 * chunk // 256, down_terms, 0)
        sum_down.start()

        def up_terms(i, _):
            cols = pl.ds(pl.multiple_of(i * 256, 256), 256)
            gu[cols, :] = dot_tn(n2[:, cols], d_up[...]).astype(BF)
            return 0

        lax.fori_loop(0, d // 256, up_terms, 0)
        sum_up.start()

    pl.run_scoped(
        own_units,
        pltpu.VMEM((d, 4 * chunk), BF),
        pltpu.VMEM((4 * chunk, d), BF),
        pltpu.VMEM((group, 4 * chunk), BF),
        pltpu.VMEM((group, 4 * chunk), BF),
    )
    got_normed = sender.local(normed_kept, ct)
    got_qkv = sender.local(w_qkv_ref, wide_a.at[:, pl.ds(0, 3 * d)])
    got_skip = sender.local(w_skip_ref, wide_b.at[pl.ds(0, 2 * d)])
    gather_branch.forward()
    own_grad.wait()
    for copy in got_grad:
        copy.wait_recv()

    def heads(dq, dk, dv):
        backward_heads(q, k, v, o, grad, seg, lse[2:3, :], lse, dq, dk, dv, acc)

        def turn_back(i, _):
            rows = rows_of(i)
            for c, ref in ((0, dq), (1, dk)):
                t = ref[rows, :].astype(BF).astype(F32)
                d_heads[c, rows, :] = turn(t, rows, -1.0).astype(BF)
            d_heads[2, rows, :] = dv[rows, :].astype(BF)
            return 0

        lax.fori_loop(0, group // TOK, turn_back, 0)

    pl.run_scoped(heads, *[pltpu.VMEM((group, 128), F32)] * 3)
    own_frames = sender.local(d_heads.at[:, mine], d_frames.at[:, :, heads_at])
    got_frames = [
        sender.push(
            d_heads.at[:, rows_of(peers[i][1])], d_frames.at[:, :, heads_at], peers[i][0]
        )
        for i in range(1, 8)
    ]
    gather_branch.corner()
    got_normed.wait()

    def qkv_terms(i, _):
        cols = pl.ds(pl.multiple_of(i * 256, 256), 256)
        turned = ct[:, cols].T
        for c in range(3):
            gq[cols, c * 128 : (c + 1) * 128] = dot_nn(turned, d_heads[c]).astype(BF)
        return 0

    lax.fori_loop(0, d // 256, qkv_terms, 0)
    sum_qkv = PlaneSum(sender, gq, q1, q2, q3, place)
    sum_qkv.start()
    gather_branch.done()
    go[...] = dot_tn(o[...], db[...]).astype(BF)

    same_high = lax.div(z, 2) == lax.div(u, 2)
    same_low = lax.rem(z, 2) == lax.rem(u, 2)
    owner = z == u
    to_far = sender.remote(go, o1, (u, flip_high(z), x))
    to_near = sender.remote(go, o2, (u, flip_low(z), x))

    @pl.when(jnp.logical_not(same_high))
    def _():
        to_far.start()

    sum_down.middle()
    sum_up.middle()

    own_frames.wait()
    for copy in got_frames:
        copy.wait_recv()
    got_qkv.wait()
    d_normed = dot_nt(d_frames[0], wide_a[:, :d])
    d_normed += dot_nt(d_frames[1], wide_a[:, d : 2 * d])
    d_normed += dot_nt(d_frames[2], wide_a[:, 2 * d : 3 * d])
    value = entry[...].astype(F32)
    back, g_gain_one = rms_back_rows(value, rms_parts(value), gain_one_ref[...], d_normed)
    n2[mine, :] = (middle[...] + back).astype(BF)
    gather_entry = PlaneGather(sender, n2, peers)
    gather_entry.start()
    sent_back = sender.push_or_keep(n2.at[mine], entry_r, home, stays_home)

    for i in range(2):
        vec[i : i + 1, :] = g_gain_one[:, i * d // 2 : (i + 1) * d // 2]
    vec_at = pl.ds(pl.multiple_of(me * 16, 16), 16)
    got_vec = [sender.push(vec, vec_plane.at[vec_at], peers[i][0]) for i in range(1, 8)]
    vec_plane[vec_at, :] = vec[...]

    def skip_terms(i):
        rows = rows_of(peers[i][1])
        return dot_tn(joined[rows, :], n2[rows, :])

    total = skip_terms(0)

    @pl.when(same_high)
    def _():
        to_far.wait_recv()
        go[...] = (go[...].astype(F32) + o1[...].astype(F32)).astype(BF)

    @pl.when(both(same_high, jnp.logical_not(same_low)))
    def _():
        to_near.start()

    gather_entry.forward()
    total += skip_terms(1)
    total += skip_terms(4)
    gather_entry.corner()
    total += skip_terms(5)
    for copy in gather_entry.cores:
        copy.wait_recv()
    for i in (2, 3, 6, 7):
        total += skip_terms(i)
    gs[...] = total.astype(BF)
    sum_skip = PlaneSum(sender, gs, s1, s2, s3, place)
    sum_skip.start()

    sum_qkv.middle()
    for copy in got_vec:
        copy.wait_recv()
    value = vec_plane[0:16, :]
    for i in range(1, 8):
        value += vec_plane[16 * i : 16 * (i + 1), :]
    vec_sum[...] = value
    z_devices = (
        (u, flip_low(z), x),
        (u, flip_high(z), x),
        (u, flip_low(flip_high(z)), x),
    )
    vec_at = pl.ds(pl.multiple_of(z * 16, 16), 16)
    got_vec = [sender.push(vec_sum, vec_z.at[vec_at], device) for device in z_devices]
    vec_z[vec_at, :] = vec_sum[...]

    sum_up.end(uz)
    last_up = ColumnGather(sender, uz, fin_u, peers, x)
    sum_down.end(dz)
    last_down = RowGather(sender, dz, fin_d, peers, u)

    sum_skip.middle()

    outs = []
    sent_back.wait_recv()
    got_skip.wait()
    for i, out in enumerate((inputs_out, skip_out)):
        d_frames[i] = dot_nt(entry_r[...], wide_b[i * d : (i + 1) * d, :]).astype(BF)
        outs.append(sender.local(d_frames.at[i], out))
    sum_qkv.end(qz)
    last_qkv = ColumnGather(sender, qz, fin_q, peers, x)

    @pl.when(owner)
    def _():
        to_near.wait_recv()
        fin_o[...] = (go[...].astype(F32) + o2[...].astype(F32)).astype(BF)

    def tell(i, to):
        return pltpu.make_async_remote_copy(
            src_ref=fin_o,
            dst_ref=fin_o,
            send_sem=spread.at[8 + i],
            recv_sem=spread.at[11],
            device_id=peers[to][0],
            device_id_type=MESH_ID,
        )

    tell_core, tell_far, tell_on = tell(0, 2), tell(1, 4), tell(2, 2)

    @pl.when(owner)
    def _():
        tell_far.start()
        tell_core.start()

    last_up.forward()
    last_down.forward()
    sum_skip.end(sz)
    last_skip = RowGather(sender, sz, fin_s, peers, u)
    last_qkv.forward()
    across = u == flip_high(z)

    @pl.when(jnp.logical_not(owner))
    def _():
        tell_core.wait_recv()

    @pl.when(across)
    def _():
        tell_on.start()

    last_up.done()
    for p in range(8):
        for s in range(4):
            first = (2 * s + p % 2) * 4 * chunk + p // 2 * chunk
            outs.append(
                sender.local(
                    fin_u.at[p, :, pl.ds(s * chunk, chunk)], g_up_out.at[:, pl.ds(first, chunk)]
                )
            )
    last_down.done()
    outs.append(sender.local(fin_d, g_down_out))
    for copy in got_vec:
        copy.wait_recv()
    vec_sum_out = vec_z[0:16, :] + vec_z[16:32, :] + vec_z[32:48, :] + vec_z[48:64, :]
    vec_plane[0:16, :] = vec_sum_out
    outs.append(sender.local(vec_plane.at[pl.ds(0, 16)], vector_out))
    sent_result.wait_recv()
    outs.append(sender.local(result_r, result_out))
    outs.append(sender.local(fin_o, g_out_out))
    last_skip.forward()
    last_qkv.done()
    for p in range(8):
        for c in range(3):
            outs.append(
                sender.local(
                    fin_q.at[p, :, pl.ds(c * 128, 128)],
                    g_qkv_out.at[:, pl.ds(c * d + p * 128, 128)],
                )
            )

    @pl.when(owner)
    def _():
        tell_far.wait_send()
        tell_core.wait_send()

    @pl.when(across)
    def _():
        tell_on.wait_send()

    @pl.when(jnp.logical_not(same_high))
    def _():
        to_far.wait_send()

    @pl.when(both(same_high, jnp.logical_not(same_low)))
    def _():
        to_near.wait_send()

    last_skip.done()
    outs.append(sender.local(fin_s, g_skip_out))
    for copy in outs:
        copy.wait()
    gather_entry.left()
    sender.finish()


def call_layer(arrays, lengths, vectors):
    d = arrays[0].shape[1]
    hidden = arrays[6].shape[1]
    group = 8 * TOK
    any_space = pl.BlockSpec(memory_space=pl.ANY)
    vmem = pl.BlockSpec(memory_space=pltpu.VMEM)
    smem = pl.BlockSpec(memory_space=pltpu.SMEM)
    block, wide = ((TOK, d), BF), ((group, d), BF)
    head, table, total = ((group, 128), BF), ((group, 128), F32), ((TOK, d), F32)
    unit = hidden // 8

    def sums(rows, columns):
        return [
            ((2, rows, columns), BF),
            ((2, rows, columns), BF),
            ((rows, columns), BF),
            ((rows, columns), BF),
        ]

    outs = [
        block,
        block,
        block,
        ((2 * d // 8, d), BF),
        ((d // 8, 3 * d), BF),
        ((d // 8, d), BF),
        ((d // 8, hidden), BF),
        ((unit, d), BF),
        ((16, 512), F32),
        wide,
    ]
    scratch = [
        ((d, hidden), BF),
        ((hidden, d), BF),
        ((d, d), BF),
        wide,
        wide,
        wide,
        ((group, 256), BF),
        head,
        head,
        head,
        head,
        head,
        ((8, group), F32),
        table,
        table,
        table,
        block,
        total,
        total,
        total,
        block,
        block,
        block,
        ((3, group, 128), BF),
        ((3, TOK, d), BF),
        block,
        ((unit, d), BF),
        ((d, unit), BF),
        ((d, 384), BF),
        ((256, d), BF),
        ((128, d), BF),
        *sums(unit // 4, d),
        *sums(d // 4, unit),
        *sums(d // 4, 384),
        *sums(64, d),
        ((128, d), BF),
        ((128, d), BF),
        ((unit, d), BF),
        ((8, d // 8, unit), BF),
        ((8, d // 8, 384), BF),
        ((256, d), BF),
        ((128, d), BF),
        ((16, 512), F32),
        ((128, 512), F32),
        ((16, 512), F32),
        ((64, 512), F32),
        ((128, group), F32),
        ((8, 128), F32),
        ((8, 128), F32),
    ]
    made = pl.pallas_call(
        layer_kernel,
        in_specs=[smem] + [vmem] * len(vectors) + [any_space] * len(arrays),
        out_specs=[any_space] * len(outs),
        out_shape=[jax.ShapeDtypeStruct(*o) for o in outs],
        scratch_shapes=[pltpu.VMEM(*s) for s in scratch]
        + [pltpu.SemaphoreType.DMA((160,))] * 3
        + [pltpu.SemaphoreType.DMA((12,))],
        compiler_params=pltpu.CompilerParams(
            vmem_limit_bytes=60 * 2**20 + 2**18, has_side_effects=True
        ),
        name="layer",
    )(lengths, *vectors, *arrays)
    return made[:9]


def widen_kernel(*refs):
    n = 9
    ins, outs = refs[:n], refs[n:]
    for i in range(8):
        outs[i][...] = ins[i][...].astype(outs[i].dtype)
    vectors = ins[8]
    for out, row in zip(outs[8:], (0, 2, 4, 8)):
        for part in range(out.shape[1] // 512):
            out[:, part * 512 : (part + 1) * 512] = vectors[row + part : row + part + 1, :]


def call_widen(made):
    steps = 8
    whole = [pl.BlockSpec(a.shape, lambda i: (0, 0)) for a in made]
    parts = [
        pl.BlockSpec((a.shape[0] // steps, a.shape[1]), lambda i: (i, 0)) for a in made[3:8]
    ]
    d, hidden = made[5].shape[1], made[6].shape[1]
    ends = [(1, d), (1, d), (1, d), (1, hidden)]
    outs = pl.pallas_call(
        widen_kernel,
        grid=(steps,),
        in_specs=whole[:3] + parts + whole[8:],
        out_specs=whole[:3] + parts + [pl.BlockSpec(e, lambda i: (0, 0)) for e in ends],
        out_shape=[jax.ShapeDtypeStruct(a.shape, BF) for a in made[:3]]
        + [jax.ShapeDtypeStruct(a.shape, F32) for a in made[3:8]]
        + [jax.ShapeDtypeStruct(e, F32) for e in ends],
        name="widen",
    )(*made)
    one, two, down, up = (v[0] for v in outs[8:])
    return (*outs[:8], one, two, up, down)


def local(
    sizes,
    inputs,
    skip_in,
    lengths,
    cotangent,
    w_skip,
    gain_one,
    w_qkv,
    w_out,
    gain_two,
    w_up,
    b_up,
    w_down,
    b_down,
):
    n_u, n_z, n_x = sizes
    frames, d = inputs.shape
    hidden = w_up.shape[1]
    parts = n_u * n_x
    group = frames * parts
    u, z, x = (lax.axis_index(a) for a in AXES)
    me = u * n_x + x
    width = d // parts

    def line(a, b, c):
        return (a * n_z + b) * n_x + c

    def permute(v, to):
        pairs = [
            (line(a, b, c), line(*to(a, b, c)))
            for a in range(n_u)
            for b in range(n_z)
            for c in range(n_x)
        ]
        return lax.ppermute(v, AXES, pairs)

    def plane_of(a):
        return (a % 2) * (n_u // 2) + a // 2

    group_of = {plane_of(a): a for a in range(n_u)}

    def away(v):
        return permute(v, lambda a, b, c: (b, plane_of(a), c))

    def home(v):
        return permute(v, lambda a, b, c: (group_of[b], a, c))

    def swap_plane(v, bit):
        def to(a, b, c):
            other = (a * n_x + c) ^ bit
            return other // n_x, b, other % n_x

        return permute(v, to)

    plane_bits = [1 << i for i in range(parts.bit_length() - 1)]
    if n_x == 2 and n_u == 4:
        orders = ([1, 4, 2], [4, 1, 2])
    else:
        orders = (plane_bits, plane_bits)
    cut = frames // 32 * 16

    def gather_plane(v):
        pieces = []
        for piece, order in zip((v[:cut], v[cut:]), orders):
            for bit in order:
                piece = jnp.concatenate([piece, swap_plane(piece, bit)], axis=0)
            pieces.append(piece)
        return jnp.concatenate(pieces, axis=0)

    def gather_order(v):
        pieces = []
        for start, size, order in ((0, cut, orders[0]), (cut, frames - cut, orders[1])):
            offsets = [0]
            for bit in order:
                offsets = offsets + [o ^ bit for o in offsets]
            for o in offsets:
                pieces.append(
                    lax.dynamic_slice_in_dim(v, (me ^ o) * frames + start, size, axis=0)
                )
        return jnp.concatenate(pieces, axis=0)

    z_bits = n_z.bit_length() - 1

    def reduce_z(v):
        rest = v.shape[1:]
        v = v.reshape((2,) * z_bits + (v.shape[0] // n_z,) + rest)
        for bit in range(z_bits):
            axis = z_bits - 1 - bit
            own = (z >> bit) & 1
            keep = lax.dynamic_index_in_dim(v, own, axis, keepdims=False)
            give = lax.dynamic_index_in_dim(v, 1 - own, axis, keepdims=False)
            got = permute(
                give.astype(BF), lambda a, b, c, bit=bit: (a, b ^ (1 << bit), c)
            )
            v = keep.astype(F32) + got.astype(F32)
            if bit < z_bits - 1:
                v = v.astype(BF)
        return v.astype(BF)

    def finish_columns(v):
        if n_x == 2:
            v = v.reshape((2, v.shape[0] // 2) + v.shape[1:])
            keep = lax.dynamic_index_in_dim(v, x, 0, keepdims=False)
            give = lax.dynamic_index_in_dim(v, 1 - x, 0, keepdims=False)
            got = permute(give, lambda a, b, c: (a, b, 1 - c))
            both = jnp.where(x == 0, jnp.stack([keep, got]), jnp.stack([got, keep]))
        else:
            both = v[None]
        every = lax.all_gather(both, "u", axis=0)
        return every.reshape((parts,) + both.shape[1:])

    def sum_all(v):
        total = n_u * n_z * n_x
        for i in range(total.bit_length() - 1):
            bit = 1 << i
            pairs = [(n, n ^ bit) for n in range(total)]
            v = v + lax.ppermute(v, AXES, pairs)
        return v

    entry_home = dot_nn(inputs, w_skip[:d]) + dot_nn(skip_in, w_skip[d:])
    entry = away(entry_home.astype(BF)).astype(F32)
    group_lengths = away(lengths)[0]
    grad_low = away(cotangent)
    inputs_away = away(inputs)
    skip_away = away(skip_in)

    segment, places = frame_segments(group_lengths, jnp.arange(group, dtype=jnp.int32))
    own_places = lax.dynamic_slice_in_dim(places, me * frames, frames)
    tables = rotary_tables(own_places)
    col, row = segment[:, None], segment[None, :]

    inverse_one = rms_parts(entry)
    normed_one = (entry * inverse_one * gain_one).astype(BF)
    qkv = dot_nn(normed_one, w_qkv)
    query = (rotate(qkv[:, :d], tables, 1.0)).astype(BF) * BF(HEAD_DIM**-0.5)
    keys = rotate(qkv[:, d : 2 * d], tables, 1.0).astype(BF)
    values = qkv[:, 2 * d :].astype(BF)

    def to_heads(*arrays):
        n = len(arrays)
        v = jnp.stack([a.reshape(frames, parts, width) for a in arrays], axis=2)
        v = lax.all_to_all(
            v.reshape(frames, parts * n * width), PLANE, split_axis=1, concat_axis=0, tiled=True
        )
        return [v[:, i * width : (i + 1) * width] for i in range(n)]

    def to_frames(*arrays):
        n = len(arrays)
        v = jnp.concatenate(arrays, axis=1)
        v = lax.all_to_all(v, PLANE, split_axis=0, concat_axis=1, tiled=True)
        v = v.reshape(frames, parts, n, width)
        return [v[:, :, i].reshape(frames, d) for i in range(n)]

    head_query, head_keys, head_values = to_heads(query, keys, values)
    head_mixed, lse = call_forward(head_query, head_keys, head_values, col, row)
    (mixed,) = to_frames(head_mixed)

    middle = entry + dot_nn(mixed, w_out)
    inverse_two = rms_parts(middle)
    normed_two = (middle * inverse_two * gain_two).astype(BF)
    up = dot_nn(normed_two, w_up) + b_up
    d_active = dot_nt(grad_low, w_down)
    active, slope = gelu_both(up)
    d_up = (d_active * slope).astype(BF)
    result_away = (middle + dot_nn(active.astype(BF), w_down) + b_down).astype(BF)
    result = home(result_away)
    d_normed_two = dot_nt(d_up, w_up)
    middle_part, g_gain_two = rms_back(middle, inverse_two, gain_two, d_normed_two)
    d_middle = grad_low.astype(F32) + middle_part
    d_branch = d_middle.astype(BF)
    d_mixed = dot_nt(d_branch, w_out).astype(BF)
    (head_grad,) = to_heads(d_mixed)
    dq, dk, dv = call_backward(
        head_query, head_keys, head_values, head_mixed, head_grad, col, row, lse
    )

    chunk = hidden // (n_z * parts)
    w_up_own = lax.dynamic_slice(
        w_up.reshape(d, n_z, n_x, n_u, chunk), (0, 0, x, u, 0), (d, n_z, 1, 1, chunk)
    ).reshape(d, n_z * chunk)
    w_down_own = lax.dynamic_slice(
        w_down.reshape(n_z, n_x, n_u, chunk, d), (0, x, u, 0, 0), (n_z, 1, 1, chunk, d)
    ).reshape(n_z * chunk, d)
    b_up_own = lax.dynamic_slice(
        b_up.reshape(n_z, n_x, n_u, chunk), (0, x, u, 0), (n_z, 1, 1, chunk)
    ).reshape(n_z * chunk)
    plane_grad = gather_plane(grad_low)
    plane_normed = gather_plane(normed_two)
    up_own = dot_nn(plane_normed, w_up_own) + b_up_own
    active_own, slope_own = gelu_both(up_own)
    d_up_own = (dot_nt(plane_grad, w_down_own) * slope_own).astype(BF)
    g_down = dot_tn(active_own.astype(BF), plane_grad)
    g_up = dot_tn(plane_normed, d_up_own)
    down_z = reduce_z(g_down.astype(BF))
    up_z = reduce_z(g_up.astype(BF))
    out_down = lax.all_gather(down_z, "u", axis=0, tiled=True).astype(F32)
    out_up = finish_columns(up_z)
    out_up = (
        out_up.reshape(n_u, n_x, -1, n_z, chunk).transpose(2, 3, 1, 0, 4).reshape(-1, hidden)
    ).astype(F32)

    plane_mixed = gather_plane(mixed)
    own_branch = gather_order(
        lax.all_to_all(d_branch, PLANE, split_axis=1, concat_axis=0, tiled=True)
    )
    g_out = dot_tn(plane_mixed, own_branch)
    out_out = (
        finish_columns(reduce_z(g_out.astype(BF))).transpose(1, 0, 2).reshape(-1, d).astype(F32)
    )

    low = [a.astype(BF) for a in (dq, dk, dv)]
    frame_query, frame_keys, frame_values = to_frames(*low)
    d_qkv = jnp.concatenate(
        [
            rotate(frame_query.astype(F32), tables, -1.0).astype(BF),
            rotate(frame_keys.astype(F32), tables, -1.0).astype(BF),
            frame_values,
        ],
        axis=1,
    )
    d_normed_one = dot_nt(d_qkv, w_qkv)
    entry_part, g_gain_one = rms_back(entry, inverse_one, gain_one, d_normed_one)
    d_entry = (d_middle + entry_part).astype(BF)
    d_entry_home = home(d_entry)
    d_joined = dot_nt(d_entry_home, w_skip)
    d_inputs = d_joined[:, :d].astype(BF)
    d_skip = d_joined[:, d:].astype(BF)

    group_tables = rotary_tables(places)
    head_d_qkv = jnp.concatenate(
        [
            rotate(low[0].astype(F32), group_tables, -1.0).astype(BF),
            rotate(low[1].astype(F32), group_tables, -1.0).astype(BF),
            low[2],
        ],
        axis=1,
    )
    plane_first = gather_plane(normed_one)
    g_qkv = dot_tn(plane_first, gather_order(head_d_qkv))
    plane_inputs = gather_plane(inputs_away)
    plane_skip = gather_plane(skip_away)
    own_entry = gather_order(
        lax.all_to_all(d_entry, PLANE, split_axis=1, concat_axis=0, tiled=True)
    )
    g_skip = jnp.concatenate([dot_tn(plane_inputs, own_entry), dot_tn(plane_skip, own_entry)])
    out_qkv = finish_columns(reduce_z(g_qkv.astype(BF)))
    out_qkv = (
        out_qkv.reshape(parts, -1, 3, width).transpose(1, 2, 0, 3).reshape(-1, 3 * d).astype(F32)
    )
    out_skip = (
        finish_columns(reduce_z(g_skip.astype(BF))).transpose(1, 0, 2).reshape(-1, d).astype(F32)
    )

    early = sum_all(
        jnp.concatenate(
            [
                g_gain_two,
                jnp.sum(d_up.astype(F32), axis=0),
                jnp.sum(cotangent.astype(F32), axis=0),
            ]
        )
    )
    total_gain_one = sum_all(g_gain_one)
    return (
        result,
        d_inputs,
        d_skip,
        out_skip,
        total_gain_one,
        out_qkv,
        out_out,
        early[:d],
        out_up,
        early[d : d + hidden],
        out_down,
        early[d + hidden :],
    )


def local_fast(
    sizes,
    inputs,
    skip_in,
    lengths,
    cotangent,
    w_skip,
    gain_one,
    w_qkv,
    w_out,
    gain_two,
    w_up,
    b_up,
    w_down,
    b_down,
):
    made = call_layer(
        (inputs, skip_in, cotangent, w_skip, w_qkv, w_out, w_up, w_down),
        lengths,
        (gain_one[None], gain_two[None], b_up[None], b_down[None]),
    )
    (
        result,
        d_inputs,
        d_skip,
        g_skip,
        g_qkv,
        g_out,
        g_up,
        g_down,
        total_one,
        total_two,
        total_up,
        total_down,
    ) = call_widen(made)
    return (
        result,
        d_inputs,
        d_skip,
        g_skip,
        total_one,
        g_qkv,
        g_out,
        total_two,
        g_up,
        total_up,
        g_down,
        total_down,
    )


def solution(mesh):
    n_u, n_s = mesh.shape["utt"], mesh.shape["seq"]
    sizes = (n_u, n_u, n_s // n_u)
    program = local_fast if sizes == (4, 4, 2) else local
    inner = Mesh(mesh.devices.reshape(sizes), AXES)
    rows, seq = P(AXES, None), P(("z", "x"), None)
    in_specs = (rows, rows, P("u", None), rows) + (P(),) * 9
    out_specs = (rows, rows, rows, seq, P(), seq, seq, P(), seq, P(), seq, P())
    return jax.shard_map(
        functools.partial(program, sizes),
        mesh=inner,
        in_specs=in_specs,
        out_specs=out_specs,
        check_vma=False,
    )
```

```python
import functools
import math

import jax
import jax.numpy as jnp
from jax import lax
from jax.experimental import pallas as pl
from jax.experimental.pallas import tpu as pltpu
from jax.sharding import Mesh, PartitionSpec as P

HEAD_DIM = 64
EPSILON = 1e-06
BF = jnp.bfloat16
F32 = jnp.float32
AXES = ("u", "z", "x")
PLANE = ("u", "x")


def dot_nn(a, b):
    return lax.dot_general(a, b, (((1,), (0,)), ((), ())), preferred_element_type=F32)


def dot_nt(a, b):
    return lax.dot_general(a, b, (((1,), (1,)), ((), ())), preferred_element_type=F32)


def dot_tn(a, b):
    return lax.dot_general(a, b, (((0,), (0,)), ((), ())), preferred_element_type=F32)


def attention_forward(q_ref, k_ref, v_ref, col_ref, row_ref, o_ref, lse_ref, acc, out_t):
    forward_heads(q_ref, k_ref, v_ref, col_ref, row_ref[...], o_ref, lse_ref, acc, out_t)


def forward_heads(q_ref, k_ref, v_ref, col_ref, segment_row, o_ref, lse_ref, acc, out_t):
    frames, width = q_ref.shape
    heads = width // HEAD_DIM
    block = frames // (frames // 352)
    lane = lax.broadcasted_iota(jnp.int32, (1, width), 1)
    for h in range(heads):
        own = (lane // HEAD_DIM == h).astype(BF)
        query = q_ref[...] * own
        acc[...] = jnp.zeros_like(acc)

        def step(j, carry):
            top, total = carry
            rows = pl.ds(pl.multiple_of(j * block, block), block)
            scores = dot_nt(k_ref[rows, :], query)
            scores = jnp.where(col_ref[rows, 0:1] == segment_row, scores, -1e30)
            peak = jnp.maximum(top, jnp.max(scores, axis=0, keepdims=True))
            expos = jnp.exp(scores - peak)
            shrink = jnp.exp(top - peak)
            acc[...] = acc[...] * shrink + dot_tn(v_ref[rows, :], expos.astype(BF))
            return peak, total * shrink + jnp.sum(expos, axis=0, keepdims=True)

        top, total = lax.fori_loop(
            0,
            frames // block,
            step,
            (jnp.full((1, frames), -1e30, F32), jnp.zeros((1, frames), F32)),
        )
        part = slice(h * HEAD_DIM, (h + 1) * HEAD_DIM)
        out_t[part, :] = acc[part, :] / total
        lse_ref[h : h + 1, :] = top + jnp.log(total)
    o_ref[...] = out_t[...].T.astype(BF)


def attention_backward(
    q_ref, k_ref, v_ref, o_ref, do_ref, col_ref, row_ref, lse_ref, dq_ref, dk_ref, dv_ref, acc
):
    backward_heads(
        q_ref, k_ref, v_ref, o_ref, do_ref, col_ref, row_ref[...], lse_ref, dq_ref, dk_ref, dv_ref, acc
    )


def backward_heads(
    q_ref, k_ref, v_ref, o_ref, do_ref, col_ref, segment_row, lse_ref, dq_ref, dk_ref, dv_ref, acc, between=None
):
    frames, width = q_ref.shape
    heads = width // HEAD_DIM
    block = frames // (frames // 352)
    lane = lax.broadcasted_iota(jnp.int32, (1, width), 1)
    product_t = (o_ref[...].astype(F32) * do_ref[...].astype(F32)).T
    for h in range(heads):
        own = (lane // HEAD_DIM == h).astype(BF)
        query = q_ref[...] * own
        grad = do_ref[...] * own
        part = slice(h * HEAD_DIM, (h + 1) * HEAD_DIM)
        delta = jnp.sum(product_t[part, :], axis=0, keepdims=True)
        log_total = lse_ref[h : h + 1, :]

        def step(j, _):
            rows = pl.ds(pl.multiple_of(j * block, block), block)
            keys = k_ref[rows, :]
            scores = dot_nt(keys, query)
            same = col_ref[rows, 0:1] == segment_row
            probs = jnp.where(same, jnp.exp(scores - log_total), 0.0)
            d_probs = dot_nt(v_ref[rows, :], grad)
            d_scores = (probs * (d_probs - delta)).astype(BF)
            value_part = dot_nn(probs.astype(BF), grad)
            key_part = dot_nn(d_scores, query)
            if h == 0:
                dv_ref[rows, :] = value_part
                dk_ref[rows, :] = key_part
            else:
                dv_ref[rows, :] += value_part
                dk_ref[rows, :] += key_part
            query_part = dot_tn(keys * own, d_scores)

            if h == 0:

                @pl.when(j == 0)
                def _():
                    acc[...] = query_part

                @pl.when(j > 0)
                def _():
                    acc[...] += query_part

            else:
                acc[...] += query_part
            return 0

        lax.fori_loop(0, frames // block, step, 0)
        if h == 0 and between is not None:
            between()
    dq_ref[...] = acc[...].T * (HEAD_DIM**-0.5)


def call_forward(query, keys, values, col, row):
    frames, width = query.shape
    return pl.pallas_call(
        attention_forward,
        out_shape=(
            jax.ShapeDtypeStruct((frames, width), BF),
            jax.ShapeDtypeStruct((width // HEAD_DIM, frames), F32),
        ),
        scratch_shapes=[pltpu.VMEM((width, frames), F32), pltpu.VMEM((width, frames), F32)],
        compiler_params=pltpu.CompilerParams(vmem_limit_bytes=56 * 2**20),
        cost_estimate=pl.CostEstimate(
            flops=16 * frames * frames * width, bytes_accessed=10 * frames * width, transcendentals=0
        ),
        name="attention_forward",
    )(query, keys, values, col, row)


def call_backward(query, keys, values, mixed, grad, col, row, lse):
    frames, width = query.shape
    shape = jax.ShapeDtypeStruct((frames, width), F32)
    return pl.pallas_call(
        attention_backward,
        out_shape=(shape, shape, shape),
        scratch_shapes=[pltpu.VMEM((width, frames), F32)],
        compiler_params=pltpu.CompilerParams(vmem_limit_bytes=56 * 2**20),
        cost_estimate=pl.CostEstimate(
            flops=32 * frames * frames * width, bytes_accessed=20 * frames * width, transcendentals=0
        ),
        name="attention_backward",
    )(query, keys, values, mixed, grad, col, row, lse)


def frame_segments(own_lengths, positions):
    slots = own_lengths.shape[0]
    upto = jnp.arange(slots)[:, None] >= jnp.arange(slots)[None, :]
    ends_at = jnp.sum(jnp.where(upto, own_lengths[None, :], 0), axis=1)
    starts_at = ends_at - own_lengths
    segment = jnp.sum((positions[:, None] >= ends_at[None, :]).astype(jnp.int32), axis=1)
    index = jnp.arange(slots, dtype=jnp.int32)
    offset = jnp.sum(jnp.where(segment[:, None] == index[None, :], starts_at[None, :], 0), axis=1)
    return segment, positions - offset


def rotary_tables(places):
    freqs = jnp.exp(
        jnp.arange(HEAD_DIM // 2, dtype=F32) * (-2.0 * math.log(10000.0) / HEAD_DIM)
    )
    angles = places.astype(F32)[:, None] * freqs[None, :]
    cosine, sine = jnp.cos(angles), jnp.sin(angles)
    return (
        jnp.concatenate([cosine, cosine], axis=1)[:, None, :],
        jnp.concatenate([-sine, sine], axis=1)[:, None, :],
    )


def rotate(v, tables, sign):
    frames, width = v.shape
    shaped = v.reshape(frames, width // HEAD_DIM, HEAD_DIM)
    half = HEAD_DIM // 2
    swapped = jnp.concatenate([shaped[..., half:], shaped[..., :half]], axis=-1)
    return (shaped * tables[0] + swapped * (sign * tables[1])).reshape(frames, width)


def rms_parts(hidden):
    return lax.rsqrt(jnp.mean(hidden * hidden, axis=-1, keepdims=True) + EPSILON)


def rms_back(hidden, inverse, gain, grad):
    scaled = hidden * inverse
    weighted = grad * gain
    inner = jnp.mean(weighted * scaled, axis=-1, keepdims=True)
    return inverse * (weighted - scaled * inner), jnp.sum(grad * scaled, axis=0)


def gelu_both(t):
    bell = 0.5 * (1.0 + lax.erf(t * 0.7071067811865476))
    return t * bell, bell + t * (0.3989422804014327 * jnp.exp(-0.5 * t * t))


TOK = 176
MESH_ID = pl.DeviceIdType.MESH


def flip_low(u):
    return u + 1 - 2 * lax.rem(u, 2)


def flip_high(u):
    return u + 2 - 4 * lax.div(u, 2)


def swap_bits(u):
    return 2 * lax.rem(u, 2) + lax.div(u, 2)


def both(a, b):
    return jnp.logical_and(a, b)


def gelu_pair(t):
    bell = jnp.exp(-0.5 * (t * t))
    s = 1.0 / (1.0 + jnp.abs(t) * (0.3275911 * 0.7071067811865476))
    tail = 0.5 * 1.061405429 * s - 0.5 * 1.453152027
    tail = tail * s + 0.5 * 1.421413741
    tail = tail * s - 0.5 * 0.284496736
    tail = (tail * s + 0.5 * 0.254829592) * s * bell
    below = jnp.where(t < 0.0, tail, 1.0 - tail)
    return t * below, below + t * (0.3989422804014327 * bell)


def rms_back_rows(hidden, inverse, gain, grad):
    scaled = hidden * inverse
    weighted = grad * gain
    inner = jnp.mean(weighted * scaled, axis=-1, keepdims=True)
    return inverse * (weighted - scaled * inner), jnp.sum(grad * scaled, axis=0, keepdims=True)


class Sender:
    def __init__(self, send, recv, load):
        self.send, self.recv, self.load = send, recv, load
        self.n = self.m = 0
        self.sent, self.kept = [], []

    def remote(self, src, dst, device, arrival=None):
        copy = pltpu.make_async_remote_copy(
            src_ref=src,
            dst_ref=dst,
            send_sem=self.send.at[self.n],
            recv_sem=self.recv.at[self.n] if arrival is None else arrival,
            device_id=device,
            device_id_type=MESH_ID,
        )
        self.n += 1
        return copy

    def push(self, src, dst, device):
        copy = self.remote(src, dst, device)
        copy.start()
        self.sent.append(copy)
        return copy

    def push_or_keep(self, src, dst, device, own, arrival=None):
        arrival = self.recv.at[self.n] if arrival is None else arrival
        inside = pltpu.make_async_copy(src, dst, arrival)
        copy = self.remote(src, dst, device, arrival)

        @pl.when(own)
        def _():
            inside.start()

        @pl.when(jnp.logical_not(own))
        def _():
            copy.start()

        self.kept.append((copy, own))
        return copy

    def local(self, src, dst):
        copy = pltpu.make_async_copy(src, dst, self.load.at[self.m])
        self.m += 1
        copy.start()
        return copy

    def finish(self):
        for copy in self.sent:
            copy.wait_send()
        settle(self.kept)
        self.sent, self.kept = [], []

    def take(self, n):
        taken, self.kept = self.kept[-n:], self.kept[:-n]
        return taken


def settle(kept):
    for copy, own in kept:

        @pl.when(jnp.logical_not(own))
        def _(copy=copy):
            copy.wait_send()


def plane_peers(u, z, x):
    peers = []
    for k in range(8):
        a = flip_low(u) if k & 2 else u
        a = flip_high(a) if k & 4 else a
        b = 1 - x if k & 1 else x
        peers.append(((a, z, b), 2 * a + b))
    return peers


def rows_of(p, start=0, size=TOK):
    return pl.ds(pl.multiple_of(p * TOK + start, 16), size)


class PlaneGather:
    def __init__(self, sender, buffer, peers, start=0, size=TOK):
        self.sender, self.buffer, self.peers = sender, buffer, peers
        self.first, self.size = start, size
        self.low = size // 32 * 16
        self.x, self.y = self.copy(0, 1), self.copy(0, 4)
        self.over_y = self.copy(1, 4, self.low, size - self.low)
        self.over_x = self.copy(4, 1, 0, self.low)
        self.cores = [self.copy(k, 2) for k in (0, 1, 4, 5)]
        self.copies = [self.x, self.y, self.over_x, self.over_y] + self.cores

    def copy(self, k, to, start=0, size=None):
        rows = rows_of(self.peers[k][1], self.first + start, size or self.size)
        return self.sender.remote(self.buffer.at[rows], self.buffer.at[rows], self.peers[to][0])

    def start(self):
        self.x.start()
        self.y.start()
        self.cores[0].start()

    def forward(self):
        self.x.wait_recv()
        self.over_y.start()
        self.cores[1].start()
        self.y.wait_recv()
        self.over_x.start()
        self.cores[2].start()

    def corner(self):
        self.over_x.wait_recv()
        self.over_y.wait_recv()
        self.cores[3].start()

    def core(self, i):
        self.cores[i].wait_recv()

    def left(self):
        for copy in self.copies:
            copy.wait_send()

    def done(self):
        for copy in self.cores:
            copy.wait_recv()
        self.left()


class PlaneSum:
    def __init__(self, sender, terms, first, second, third, place):
        self.sender, self.terms = sender, terms
        self.first, self.second, self.third = first, second, third
        u, z, x = place
        self.low, self.high = lax.rem(z, 2), lax.div(z, 2)
        self.near, self.far = (u, flip_low(z), x), (u, flip_high(z), x)
        self.rows = third.shape[0]
        self.waits = [
            sender.remote(terms.at[self.chunk(j, 1 - self.low)], first.at[j], self.near)
            for j in range(2)
        ]
        sender.sent += self.waits

    def chunk(self, j, low):
        return pl.ds(pl.multiple_of((2 * j + low) * self.rows, self.rows), self.rows)

    def start(self):
        for copy in self.waits:
            copy.start()

    def middle(self):
        for copy in self.waits:
            copy.wait_recv()
        for j in range(2):
            own = self.terms[self.chunk(j, self.low), :].astype(F32)
            self.second[j] = (own + self.first[j].astype(F32)).astype(BF)
        self.wait = self.sender.push(self.second.at[1 - self.high], self.third, self.far)

    def end(self, out):
        self.wait.wait_recv()
        out[...] = (self.second[self.high].astype(F32) + self.third[...].astype(F32)).astype(BF)


class ColumnGather:
    def __init__(self, sender, source, out, peers, x):
        self.sender, self.out, self.peers = sender, out, peers
        rows = out.shape[1]
        me = peers[0][1]

        def part(b):
            return pl.ds(pl.multiple_of(b * rows, rows), rows)

        self.direct = [
            (k, sender.push(source.at[part(peers[k][0][2])], out.at[me], peers[k][0]))
            for k in (5, 4, 1)
        ]
        self.cores = [sender.push(source.at[part(x)], out.at[me], peers[2][0])]
        out[me] = source[part(x), :]

    def forward(self):
        for k, copy in self.direct:
            copy.wait_recv()
            slot = self.out.at[self.peers[k][1]]
            self.cores.append(self.sender.push(slot, slot, self.peers[2][0]))

    def done(self):
        for copy in self.cores:
            copy.wait_recv()


class RowGather:
    def __init__(self, sender, source, out, peers, u):
        self.sender, self.out, self.peers = sender, out, peers
        self.rows = source.shape[0]
        self.far = sender.push(source, out.at[self.part(u)], peers[4][0])
        self.cores = [sender.push(source, out.at[self.part(u)], peers[2][0])]
        out[self.part(u), :] = source[...]

    def part(self, u):
        return pl.ds(pl.multiple_of(u * self.rows, self.rows), self.rows)

    def forward(self):
        self.far.wait_recv()
        block = self.out.at[self.part(self.peers[4][0][0])]
        self.cores.append(self.sender.push(block, block, self.peers[2][0]))

    def done(self):
        for copy in self.cores:
            copy.wait_recv()


def layer_kernel(
    lengths_ref,
    gain_one_ref,
    gain_two_ref,
    b_up_ref,
    b_down_ref,
    inputs_ref,
    skip_ref,
    cot_ref,
    w_skip_ref,
    w_qkv_ref,
    w_out_ref,
    w_up_ref,
    w_down_ref,
    result_out,
    inputs_out,
    skip_out,
    g_skip_out,
    g_qkv_out,
    g_out_out,
    g_up_out,
    g_down_out,
    vector_out,
    normed_kept,
    wide_a,
    wide_b,
    w_out,
    n2,
    ct,
    db,
    joined,
    q,
    k,
    v,
    o,
    grad,
    lse,
    cos_t,
    sin_t,
    seg,
    entry,
    middle,
    dq,
    dk,
    result,
    result_r,
    d_mixed,
    d_heads,
    d_frames,
    entry_r,
    gd,
    gu,
    gq,
    gs,
    go,
    d_up,
    d1,
    d2,
    d3,
    dz,
    u1,
    u2,
    u3,
    uz,
    q1,
    q2,
    q3,
    qz,
    s1,
    s2,
    s3,
    sz,
    o1,
    o2,
    fin_d,
    fin_u,
    fin_q,
    fin_s,
    fin_o,
    vec,
    vec_plane,
    vec_sum,
    vec_z,
    acc,
    lens,
    lens_r,
    send,
    recv,
    load,
    spread,
):
    u, z, x = (lax.axis_index(a) for a in AXES)
    me = 2 * u + x
    peers = plane_peers(u, z, x)
    place = (u, z, x)
    d = entry.shape[1]
    group = n2.shape[0]
    hidden = wide_a.shape[1]
    heads_at = pl.ds(pl.multiple_of(me * 128, 128), 128)
    plane = swap_bits(u)
    away = (z, plane, x)
    stays_away = both(u == z, plane == z)
    own_home = swap_bits(z)
    home = (own_home, u, x)
    stays_home = both(own_home == u, u == z)
    sender = Sender(send, recv, load)
    mine = rows_of(me)
    low, high = 80, 96
    z_devices = (
        (u, flip_low(z), x),
        (u, flip_high(z), x),
        (u, flip_low(flip_high(z)), x),
    )

    barrier = pltpu.get_barrier_semaphore()

    def greet(device):
        pl.semaphore_signal(barrier, inc=1, device_id=device, device_id_type=MESH_ID)

    for device, _ in peers[1:]:
        greet(device)
    for device in z_devices:
        greet(device)

    @pl.when(jnp.logical_not(stays_away))
    def _():
        greet(away)
        greet(home)

    got_x = sender.local(inputs_ref, gd.at[pl.ds(0, TOK)])
    got_s = sender.local(skip_ref, gd.at[pl.ds(TOK, TOK)])
    got_w = [
        sender.local(w_skip_ref.at[pl.ds(i * d, d)], wide_b.at[pl.ds(i * d, d)]) for i in range(2)
    ]
    got_q = [
        sender.local(
            w_qkv_ref.at[:, pl.ds(pl.multiple_of(c * d + me * 128, 128), 128)],
            wide_a.at[:, pl.ds(c * 128, 128)],
        )
        for c in range(3)
    ]
    slots = lengths_ref.shape[1]
    for s in range(slots):
        lens[s : s + 1, :] = jnp.full((1, 128), lengths_ref[0, s].astype(F32), F32)
    lens[slots:8, :] = jnp.zeros((8 - slots, 128), F32)
    got_x.wait()
    got_w[0].wait()
    value = dot_nn(gd[:TOK, :], wide_b[:d, :])
    got_s.wait()
    got_w[1].wait()
    d_mixed[...] = (value + dot_nn(gd[TOK : 2 * TOK, :], wide_b[d : 2 * d, :])).astype(BF)
    pl.semaphore_wait(barrier, jnp.where(stays_away, 10, 12))
    sent_entry = [
        sender.push_or_keep(
            d_mixed.at[pl.ds(a, n)], entry.at[pl.ds(a, n)], away, stays_away
        )
        for a, n in ((0, low), (low, high))
    ]
    entry_left = sender.take(2)
    sent_lens = sender.push_or_keep(lens, lens_r, away, stays_away)
    got_down = sender.local(w_down_ref, wide_b)
    got_out = sender.local(w_out_ref, w_out)

    lane = lax.broadcasted_iota(jnp.int32, (TOK, 128), 1)
    for a in range(4):
        for b in range(2):
            for pair in range(2):
                halves = []
                for s in range(2):
                    block = 4 * (2 * pair + s) + 2 * b + a // 2
                    top = block // (d // 128) * TOK
                    first = block % (d // 128) * 128
                    piece = gd[top : top + TOK, first : first + 128].astype(F32)
                    if a % 2 != s:
                        piece = pltpu.roll(piece, 64, 1)
                    halves.append(piece)
                j = 2 * a + b
                gu[
                    j // 2 * TOK : (j // 2 + 1) * TOK,
                    j % 2 * 256 + pair * 128 : j % 2 * 256 + (pair + 1) * 128,
                ] = jnp.where(lane < 64, halves[0], halves[1]).astype(BF)

    def joined_for(a, b):
        return gu.at[
            pl.ds(pl.multiple_of(a * TOK, 16), TOK), pl.ds(pl.multiple_of(b * 256, 256), 256)
        ]

    def joined_from(a, b):
        first = lax.rem(a, 2) * 512 + b * 256
        return fin_d.at[
            pl.ds(pl.multiple_of(lax.div(a, 2) * TOK, 16), TOK),
            pl.ds(pl.multiple_of(first, 256), 256),
        ]

    own_joined = sender.local(joined_for(u, x), joined_from(u, x))
    got_joined = []
    for device, _ in peers[1:]:
        copy = sender.remote(joined_for(device[0], device[2]), joined_from(u, x), device)
        copy.start()
        got_joined.append(copy)

    sent_lens.wait_recv()
    freqs = jnp.exp(lax.rem(lane, 32).astype(F32) * (-2.0 * math.log(10000.0) / HEAD_DIM))
    front = lax.rem(lane, 64) < 32
    sign = jnp.where(front, -1.0, 1.0)

    def table(i, _):
        rows = rows_of(i)
        at = (lax.broadcasted_iota(jnp.int32, (TOK, 128), 0) + i * TOK).astype(F32)
        spot, segment, end = at, jnp.zeros_like(at), jnp.zeros((1, 128), F32)
        for s in range(slots):
            length = lens_r[s : s + 1, :]
            end = end + length
            past = at >= end
            segment = segment + jnp.where(past, 1.0, 0.0)
            spot = spot - jnp.where(past, length, 0.0)
        angle = spot * freqs
        cos_t[rows, :] = jnp.cos(angle)
        sin_t[rows, :] = jnp.sin(angle) * sign
        seg[rows, :] = segment
        return 0

    lax.fori_loop(0, group // TOK, table, 0)
    at = lax.broadcasted_iota(jnp.int32, (1, group), 1).astype(F32)
    segment_row, end = jnp.zeros((1, group), F32), jnp.zeros((1, 1), F32)
    for s in range(slots):
        end = end + lens_r[s : s + 1, 0:1]
        segment_row = segment_row + jnp.where(at >= end, 1.0, 0.0)
    lse[2:3, :] = segment_row
    for copy in got_q:
        copy.wait()

    def turn(t, rows, way):
        swapped = jnp.where(front, pltpu.roll(t, 96, 1), pltpu.roll(t, 32, 1))
        return t * cos_t[rows, :] + swapped * (way * sin_t[rows, :])

    def project(i):
        rows = rows_of(peers[i][1])
        value = dot_nn(n2[rows, :], wide_a[:, :384])
        q[rows, :] = (
            turn(value[:, :128], rows, 1.0).astype(BF).astype(F32) * HEAD_DIM**-0.5
        ).astype(BF)
        k[rows, :] = turn(value[:, 128:256], rows, 1.0).astype(BF)
        v[rows, :] = value[:, 256:].astype(BF)

    first_a = PlaneGather(sender, n2, peers, 0, low)
    first_b = PlaneGather(sender, n2, peers, low, high)
    for copy, gather, (a, n) in zip(sent_entry, (first_a, first_b), ((0, low), (low, high))):
        copy.wait_recv()
        value = entry[a : a + n, :].astype(F32)
        n2[rows_of(me, a, n), :] = (value * rms_parts(value) * gain_one_ref[...]).astype(BF)
        gather.start()
    sent_cot = sender.push_or_keep(cot_ref, ct.at[rows_of(2 * z + x)], away, stays_away)
    first_a.forward()
    project(0)
    first_a.core(0)
    first_b.core(0)
    project(2)
    first_b.forward()
    project(1)
    project(4)
    first_a.corner()
    first_b.corner()
    project(5)
    for gather in (first_a, first_b):
        gather.core(1)
    project(3)
    for gather in (first_a, first_b):
        gather.core(2)
    project(6)
    for gather in (first_a, first_b):
        gather.core(3)
    project(7)
    got_up = sender.local(w_up_ref, wide_a)
    kept_normed = sender.local(n2, normed_kept)
    sent_cot.wait_recv()
    gather_cot = PlaneGather(sender, ct, peers)
    gather_cot.start()
    own_joined.wait()
    for copy in got_joined:
        copy.wait_recv()
    for a in range(4):
        to = a % 2 * 2 + a // 2
        for b in range(2):
            sender.push_or_keep(
                joined_from(jnp.int32(a), jnp.int32(b)),
                joined.at[rows_of(2 * z + b)],
                (u, jnp.int32(to), x),
                z == to,
                spread.at[2 * z + b],
            )
    joined_left = sender.take(8)

    pl.run_scoped(
        lambda out_t: forward_heads(q, k, v, seg, segment_row, o, lse, acc, out_t),
        pltpu.VMEM((128, group), F32),
    )
    kept_normed.wait()
    for gather in (first_a, first_b):
        gather.left()
    own_mixed = sender.local(o.at[mine], d_frames.at[0, :, heads_at])
    got_mixed = [
        sender.push(o.at[rows_of(peers[i][1])], d_frames.at[0, :, heads_at], peers[i][0])
        for i in range(1, 8)
    ]
    gather_cot.forward()
    got_down.wait()
    step = d

    def back_feed(c, _):
        cols = pl.ds(pl.multiple_of(c * step, step), step)
        db[rows_of(c), :] = dot_nt(ct[mine, :], wide_b[cols, :]).astype(BF)
        return 0

    lax.fori_loop(0, hidden // step, back_feed, 0)
    own_mixed.wait()
    for copy in got_mixed:
        copy.wait_recv()

    got_out.wait()
    value = entry[...].astype(F32) + dot_nn(d_frames[0], w_out[...])
    middle[...] = value
    n2[mine, :] = (value * rms_parts(value) * gain_two_ref[...]).astype(BF)
    gather_normed = PlaneGather(sender, n2, peers)
    gather_normed.start()

    dq[...] = jnp.zeros_like(dq)
    dk[...] = jnp.zeros_like(dk)

    def add_to(ref, value):
        for j in range(d // 128):
            ref[j * TOK : (j + 1) * TOK, :] += value[:, j * 128 : (j + 1) * 128]

    def side_by_side(ref):
        return jnp.concatenate([ref[j * TOK : (j + 1) * TOK, :] for j in range(d // 128)], axis=1)

    got_up.wait()

    def feed(c, _):
        cols = pl.ds(pl.multiple_of(c * step, step), step)
        up = dot_nn(n2[mine, :], wide_a[:, cols]) + b_up_ref[:, cols]
        active, slope = gelu_pair(up)
        d_up = (db[rows_of(c), :].astype(F32) * slope).astype(BF)
        add_to(dq, dot_nn(active.astype(BF), wide_b[cols, :]))
        add_to(dk, dot_nt(d_up, wide_a[:, cols]))
        sums = jnp.sum(d_up.astype(F32), axis=0, keepdims=True)
        vec[pl.ds(8 + 2 * c, 1), :] = sums[:, : step // 2]
        vec[pl.ds(9 + 2 * c, 1), :] = sums[:, step // 2 :]
        return 0

    half = hidden // step // 2
    lax.fori_loop(0, half, feed, 0)
    gather_cot.corner()
    lax.fori_loop(half, 2 * half, feed, 0)
    gather_normed.forward()
    value = middle[...]
    inverse = rms_parts(value)
    back, g_gain_two = rms_back_rows(value, inverse, gain_two_ref[...], side_by_side(dk))
    grad_out = ct[mine, :].astype(F32)
    d_middle = grad_out + back
    result[...] = (value + side_by_side(dq) + b_down_ref[...]).astype(BF)
    middle[...] = d_middle
    db[mine, :] = d_middle.astype(BF)
    settle(entry_left)
    d_mixed[...] = dot_nt(db[mine, :], w_out[...]).astype(BF)
    own_grad = sender.local(d_mixed.at[:, heads_at], grad.at[mine])
    got_grad = [
        sender.push(
            d_mixed.at[:, pl.ds(pl.multiple_of(peers[i][1] * 128, 128), 128)],
            grad.at[mine],
            peers[i][0],
        )
        for i in range(1, 8)
    ]
    sent_result = sender.push_or_keep(result, result_r, home, stays_home)
    g_b_down = jnp.sum(grad_out, axis=0, keepdims=True)
    for i in range(2):
        part = slice(i * d // 2, (i + 1) * d // 2)
        vec[2 + i : 3 + i, :] = g_gain_two[:, part]
        vec[4 + i : 5 + i, :] = g_b_down[:, part]
    vec[6:8, :] = jnp.zeros((2, d // 2), F32)
    gather_cot.done()

    chunk = hidden // 32
    sum_down = PlaneSum(sender, gd, d1, d2, d3, place)
    sum_up = PlaneSum(sender, gu, u1, u2, u3, place)
    gather_branch = PlaneGather(sender, db, peers)

    def own_units(w_up_own, w_down_own, active):
        starts = [
            pl.multiple_of((2 * s + x) * (4 * chunk) + u * chunk, chunk) for s in range(4)
        ]
        for s, first in enumerate(starts):
            part = slice(s * chunk, (s + 1) * chunk)
            w_up_own[:, part] = wide_a[:, pl.ds(first, chunk)]
            w_down_own[part, :] = wide_b[pl.ds(first, chunk), :]
        bias = jnp.concatenate([b_up_ref[:, pl.ds(first, chunk)] for first in starts], axis=1)

        def units(i):
            rows = pl.ds(pl.multiple_of(peers[i][0][0] * (2 * TOK), 16), 2 * TOK)
            up = dot_nn(n2[rows, :], w_up_own[...]) + bias
            act, slope = gelu_pair(up)
            active[rows, :] = act.astype(BF)
            d_up[rows, :] = (dot_nt(ct[rows, :], w_down_own[...]) * slope).astype(BF)

        units(0)
        gather_normed.corner()
        gather_normed.core(0)
        gather_normed.core(1)
        units(2)
        units(4)
        gather_normed.core(2)
        gather_normed.core(3)
        units(6)
        gather_normed.left()
        gather_branch.start()

        def down_terms(i, _):
            cols = pl.ds(pl.multiple_of(i * 256, 256), 256)
            gd[cols, :] = dot_tn(active[:, cols], ct[...]).astype(BF)
            return 0

        lax.fori_loop(0, 4 * chunk // 256, down_terms, 0)
        sum_down.start()

    pl.run_scoped(
        own_units,
        pltpu.VMEM((d, 4 * chunk), BF),
        pltpu.VMEM((4 * chunk, d), BF),
        pltpu.VMEM((group, 4 * chunk), BF),
    )
    got_normed = sender.local(normed_kept, ct)
    got_qkv = sender.local(w_qkv_ref, wide_a.at[:, pl.ds(0, 3 * d)])
    got_skip = sender.local(w_skip_ref, wide_b.at[pl.ds(0, 2 * d)])
    own_grad.wait()
    for copy in got_grad:
        copy.wait_recv()

    def heads(dv):
        backward_heads(q, k, v, o, grad, seg, lse[2:3, :], lse, dq, dk, dv, acc, gather_branch.forward)

        def turn_back(i, _):
            rows = rows_of(i)
            for c, ref in ((0, dq), (1, dk)):
                t = ref[rows, :].astype(BF).astype(F32)
                d_heads[c, rows, :] = turn(t, rows, -1.0).astype(BF)
            d_heads[2, rows, :] = dv[rows, :].astype(BF)
            return 0

        lax.fori_loop(0, group // TOK, turn_back, 0)

    pl.run_scoped(heads, pltpu.VMEM((group, 128), F32))
    settle(joined_left)
    for copy in got_joined:
        copy.wait_send()
    own_frames = sender.local(d_heads.at[:, mine], d_frames.at[:, :, heads_at])
    got_frames = [
        sender.push(
            d_heads.at[:, rows_of(peers[i][1])], d_frames.at[:, :, heads_at], peers[i][0]
        )
        for i in range(1, 8)
    ]
    gather_branch.corner()

    def up_terms(i, _):
        cols = pl.ds(pl.multiple_of(i * 256, 256), 256)
        gu[cols, :] = dot_tn(n2[:, cols], d_up[...]).astype(BF)
        return 0

    lax.fori_loop(0, d // 256, up_terms, 0)
    sum_up.start()
    got_normed.wait()

    def qkv_terms(i, _):
        cols = pl.ds(pl.multiple_of(i * 256, 256), 256)
        turned = ct[:, cols].T
        for c in range(3):
            gq[cols, c * 128 : (c + 1) * 128] = dot_nn(turned, d_heads[c]).astype(BF)
        return 0

    lax.fori_loop(0, d // 256, qkv_terms, 0)
    sum_qkv = PlaneSum(sender, gq, q1, q2, q3, place)
    sum_qkv.start()
    gather_branch.done()
    go[...] = dot_tn(o[...], db[...]).astype(BF)

    same_high = lax.div(z, 2) == lax.div(u, 2)
    same_low = lax.rem(z, 2) == lax.rem(u, 2)
    owner = z == u
    to_far = sender.remote(go, o1, (u, flip_high(z), x))
    to_near = sender.remote(go, o2, (u, flip_low(z), x))

    @pl.when(jnp.logical_not(same_low))
    def _():
        to_near.start()

    sum_down.middle()

    own_frames.wait()
    for copy in got_frames:
        copy.wait_recv()
    got_qkv.wait()
    d_normed = dot_nt(d_frames[0], wide_a[:, :d])
    d_normed += dot_nt(d_frames[1], wide_a[:, d : 2 * d])
    d_normed += dot_nt(d_frames[2], wide_a[:, 2 * d : 3 * d])
    value = entry[...].astype(F32)
    back, g_gain_one = rms_back_rows(value, rms_parts(value), gain_one_ref[...], d_normed)
    wide_b[rows_of(me, 2 * d), :] = (middle[...] + back).astype(BF)
    gather_entry = PlaneGather(sender, wide_b, peers, 2 * d)
    gather_entry.start()
    sent_back = sender.push_or_keep(
        wide_b.at[rows_of(me, 2 * d)], entry_r, home, stays_home
    )

    for i in range(2):
        vec[i : i + 1, :] = g_gain_one[:, i * d // 2 : (i + 1) * d // 2]
    vec_at = pl.ds(pl.multiple_of(me * 16, 16), 16)
    got_vec = [sender.push(vec, vec_plane.at[vec_at], peers[i][0]) for i in range(1, 8)]
    vec_plane[vec_at, :] = vec[...]

    sum_up.middle()
    for s in range(8):
        rows = pl.ds(s * TOK, TOK)
        pltpu.make_async_copy(joined.at[rows], joined.at[rows], spread.at[s]).wait()
    def skip_terms(i):
        p = peers[i][1]
        return dot_tn(joined[rows_of(p), :], wide_b[rows_of(p, 2 * d), :])

    total = skip_terms(0)

    gather_entry.forward()
    sum_qkv.middle()
    total += skip_terms(1)
    total += skip_terms(4)
    gather_entry.corner()
    total += skip_terms(5)
    for copy in gather_entry.cores:
        copy.wait_recv()
    for i in (2, 3, 6, 7):
        total += skip_terms(i)
    gs[...] = total.astype(BF)
    sum_skip = PlaneSum(sender, gs, s1, s2, s3, place)
    sum_skip.start()

    @pl.when(same_low)
    def _():
        to_near.wait_recv()
        go[...] = (go[...].astype(F32) + o2[...].astype(F32)).astype(BF)

    @pl.when(both(same_low, jnp.logical_not(same_high)))
    def _():
        to_far.start()

    for copy in got_vec:
        copy.wait_recv()
    value = vec_plane[0:16, :]
    for i in range(1, 8):
        value += vec_plane[16 * i : 16 * (i + 1), :]
    vec_sum[...] = value
    vec_at = pl.ds(pl.multiple_of(z * 16, 16), 16)
    got_vec = [sender.push(vec_sum, vec_z.at[vec_at], device) for device in z_devices]
    vec_z[vec_at, :] = vec_sum[...]

    sum_up.end(uz)
    last_up = ColumnGather(sender, uz, fin_u, peers, x)
    sum_down.end(dz)
    last_down = RowGather(sender, dz, fin_d, peers, u)

    sum_skip.middle()

    outs = []
    sent_back.wait_recv()
    got_skip.wait()
    for i, out in enumerate((inputs_out, skip_out)):
        d_frames[i] = dot_nt(entry_r[...], wide_b[i * d : (i + 1) * d, :]).astype(BF)
        outs.append(sender.local(d_frames.at[i], out))
    sum_qkv.end(qz)
    last_qkv = ColumnGather(sender, qz, fin_q, peers, x)

    @pl.when(owner)
    def _():
        to_far.wait_recv()
        fin_o[...] = (go[...].astype(F32) + o1[...].astype(F32)).astype(BF)

    def tell(i, to):
        return pltpu.make_async_remote_copy(
            src_ref=fin_o,
            dst_ref=fin_o,
            send_sem=spread.at[8 + i],
            recv_sem=spread.at[11],
            device_id=peers[to][0],
            device_id_type=MESH_ID,
        )

    tell_core, tell_far, tell_on = tell(0, 2), tell(1, 4), tell(2, 2)

    @pl.when(owner)
    def _():
        tell_far.start()
        tell_core.start()

    last_up.forward()
    last_down.forward()
    sum_skip.end(sz)
    last_skip = RowGather(sender, sz, fin_s, peers, u)
    last_qkv.forward()
    across = u == flip_high(z)

    @pl.when(jnp.logical_not(owner))
    def _():
        tell_core.wait_recv()

    @pl.when(across)
    def _():
        tell_on.start()

    last_up.done()
    for p in range(8):
        for s in range(4):
            first = (2 * s + p % 2) * 4 * chunk + p // 2 * chunk
            outs.append(
                sender.local(
                    fin_u.at[p, :, pl.ds(s * chunk, chunk)], g_up_out.at[:, pl.ds(first, chunk)]
                )
            )
    last_down.done()
    outs.append(sender.local(fin_d, g_down_out))
    for copy in got_vec:
        copy.wait_recv()
    vec_sum_out = vec_z[0:16, :] + vec_z[16:32, :] + vec_z[32:48, :] + vec_z[48:64, :]
    vec_plane[0:16, :] = vec_sum_out
    outs.append(sender.local(vec_plane.at[pl.ds(0, 16)], vector_out))
    sent_result.wait_recv()
    outs.append(sender.local(result_r, result_out))
    outs.append(sender.local(fin_o, g_out_out))
    last_skip.forward()
    last_qkv.done()
    for p in range(8):
        for c in range(3):
            outs.append(
                sender.local(
                    fin_q.at[p, :, pl.ds(c * 128, 128)],
                    g_qkv_out.at[:, pl.ds(c * d + p * 128, 128)],
                )
            )

    @pl.when(owner)
    def _():
        tell_far.wait_send()
        tell_core.wait_send()

    @pl.when(across)
    def _():
        tell_on.wait_send()

    @pl.when(jnp.logical_not(same_low))
    def _():
        to_near.wait_send()

    @pl.when(both(same_low, jnp.logical_not(same_high)))
    def _():
        to_far.wait_send()

    last_skip.done()
    outs.append(sender.local(fin_s, g_skip_out))
    for copy in outs:
        copy.wait()
    gather_entry.left()
    sender.finish()


def call_layer(arrays, lengths, vectors):
    d = arrays[0].shape[1]
    hidden = arrays[6].shape[1]
    group = 8 * TOK
    any_space = pl.BlockSpec(memory_space=pl.ANY)
    vmem = pl.BlockSpec(memory_space=pltpu.VMEM)
    smem = pl.BlockSpec(memory_space=pltpu.SMEM)
    block, wide = ((TOK, d), BF), ((group, d), BF)
    head, table, total = ((group, 128), BF), ((group, 128), F32), ((TOK, d), F32)
    unit = hidden // 8

    def sums(rows, columns):
        return [
            ((2, rows, columns), BF),
            ((2, rows, columns), BF),
            ((rows, columns), BF),
            ((rows, columns), BF),
        ]

    outs = [
        block,
        block,
        block,
        ((2 * d // 8, d), BF),
        ((d // 8, 3 * d), BF),
        ((d // 8, d), BF),
        ((d // 8, hidden), BF),
        ((unit, d), BF),
        ((16, 512), F32),
        wide,
    ]
    scratch = [
        ((d, hidden), BF),
        ((hidden, d), BF),
        ((d, d), BF),
        wide,
        wide,
        wide,
        ((group, 256), BF),
        head,
        head,
        head,
        head,
        head,
        ((8, group), F32),
        table,
        table,
        table,
        block,
        total,
        table,
        table,
        block,
        block,
        block,
        ((3, group, 128), BF),
        ((3, TOK, d), BF),
        block,
        ((unit, d), BF),
        ((d, unit), BF),
        ((d, 384), BF),
        ((256, d), BF),
        ((128, d), BF),
        ((group, unit), BF),
        *sums(unit // 4, d),
        *sums(d // 4, unit),
        *sums(d // 4, 384),
        *sums(64, d),
        ((128, d), BF),
        ((128, d), BF),
        ((unit, d), BF),
        ((8, d // 8, unit), BF),
        ((8, d // 8, 384), BF),
        ((256, d), BF),
        ((128, d), BF),
        ((16, 512), F32),
        ((128, 512), F32),
        ((16, 512), F32),
        ((64, 512), F32),
        ((128, group), F32),
        ((8, 128), F32),
        ((8, 128), F32),
    ]
    made = pl.pallas_call(
        layer_kernel,
        in_specs=[smem] + [vmem] * len(vectors) + [any_space] * len(arrays),
        out_specs=[any_space] * len(outs),
        out_shape=[jax.ShapeDtypeStruct(*o) for o in outs],
        scratch_shapes=[pltpu.VMEM(*s) for s in scratch]
        + [pltpu.SemaphoreType.DMA((160,))] * 3
        + [pltpu.SemaphoreType.DMA((12,))],
        compiler_params=pltpu.CompilerParams(
            vmem_limit_bytes=60 * 2**20 + 2**18, has_side_effects=True, collective_id=0
        ),
        name="layer",
    )(lengths, *vectors, *arrays)
    return made[:9]


def widen_kernel(*refs):
    n = 9
    ins, outs = refs[:n], refs[n:]
    for i in range(8):
        outs[i][...] = ins[i][...].astype(outs[i].dtype)
    vectors = ins[8]
    for out, row in zip(outs[8:], (0, 2, 4, 8)):
        for part in range(out.shape[1] // 512):
            out[:, part * 512 : (part + 1) * 512] = vectors[row + part : row + part + 1, :]


def call_widen(made):
    steps = 8
    whole = [pl.BlockSpec(a.shape, lambda i: (0, 0)) for a in made]
    parts = [
        pl.BlockSpec((a.shape[0] // steps, a.shape[1]), lambda i: (i, 0)) for a in made[3:8]
    ]
    d, hidden = made[5].shape[1], made[6].shape[1]
    ends = [(1, d), (1, d), (1, d), (1, hidden)]
    outs = pl.pallas_call(
        widen_kernel,
        grid=(steps,),
        in_specs=whole[:3] + parts + whole[8:],
        out_specs=whole[:3] + parts + [pl.BlockSpec(e, lambda i: (0, 0)) for e in ends],
        out_shape=[jax.ShapeDtypeStruct(a.shape, BF) for a in made[:3]]
        + [jax.ShapeDtypeStruct(a.shape, F32) for a in made[3:8]]
        + [jax.ShapeDtypeStruct(e, F32) for e in ends],
        name="widen",
    )(*made)
    one, two, down, up = (v[0] for v in outs[8:])
    return (*outs[:8], one, two, up, down)


def local(
    sizes,
    inputs,
    skip_in,
    lengths,
    cotangent,
    w_skip,
    gain_one,
    w_qkv,
    w_out,
    gain_two,
    w_up,
    b_up,
    w_down,
    b_down,
):
    n_u, n_z, n_x = sizes
    frames, d = inputs.shape
    hidden = w_up.shape[1]
    parts = n_u * n_x
    group = frames * parts
    u, z, x = (lax.axis_index(a) for a in AXES)
    me = u * n_x + x
    width = d // parts

    def line(a, b, c):
        return (a * n_z + b) * n_x + c

    def permute(v, to):
        pairs = [
            (line(a, b, c), line(*to(a, b, c)))
            for a in range(n_u)
            for b in range(n_z)
            for c in range(n_x)
        ]
        return lax.ppermute(v, AXES, pairs)

    def plane_of(a):
        return (a % 2) * (n_u // 2) + a // 2

    group_of = {plane_of(a): a for a in range(n_u)}

    def away(v):
        return permute(v, lambda a, b, c: (b, plane_of(a), c))

    def home(v):
        return permute(v, lambda a, b, c: (group_of[b], a, c))

    def swap_plane(v, bit):
        def to(a, b, c):
            other = (a * n_x + c) ^ bit
            return other // n_x, b, other % n_x

        return permute(v, to)

    plane_bits = [1 << i for i in range(parts.bit_length() - 1)]
    if n_x == 2 and n_u == 4:
        orders = ([1, 4, 2], [4, 1, 2])
    else:
        orders = (plane_bits, plane_bits)
    cut = frames // 32 * 16

    def gather_plane(v):
        pieces = []
        for piece, order in zip((v[:cut], v[cut:]), orders):
            for bit in order:
                piece = jnp.concatenate([piece, swap_plane(piece, bit)], axis=0)
            pieces.append(piece)
        return jnp.concatenate(pieces, axis=0)

    def gather_order(v):
        pieces = []
        for start, size, order in ((0, cut, orders[0]), (cut, frames - cut, orders[1])):
            offsets = [0]
            for bit in order:
                offsets = offsets + [o ^ bit for o in offsets]
            for o in offsets:
                pieces.append(
                    lax.dynamic_slice_in_dim(v, (me ^ o) * frames + start, size, axis=0)
                )
        return jnp.concatenate(pieces, axis=0)

    z_bits = n_z.bit_length() - 1

    def reduce_z(v):
        rest = v.shape[1:]
        v = v.reshape((2,) * z_bits + (v.shape[0] // n_z,) + rest)
        for bit in range(z_bits):
            axis = z_bits - 1 - bit
            own = (z >> bit) & 1
            keep = lax.dynamic_index_in_dim(v, own, axis, keepdims=False)
            give = lax.dynamic_index_in_dim(v, 1 - own, axis, keepdims=False)
            got = permute(
                give.astype(BF), lambda a, b, c, bit=bit: (a, b ^ (1 << bit), c)
            )
            v = keep.astype(F32) + got.astype(F32)
            if bit < z_bits - 1:
                v = v.astype(BF)
        return v.astype(BF)

    def finish_columns(v):
        if n_x == 2:
            v = v.reshape((2, v.shape[0] // 2) + v.shape[1:])
            keep = lax.dynamic_index_in_dim(v, x, 0, keepdims=False)
            give = lax.dynamic_index_in_dim(v, 1 - x, 0, keepdims=False)
            got = permute(give, lambda a, b, c: (a, b, 1 - c))
            both = jnp.where(x == 0, jnp.stack([keep, got]), jnp.stack([got, keep]))
        else:
            both = v[None]
        every = lax.all_gather(both, "u", axis=0)
        return every.reshape((parts,) + both.shape[1:])

    def sum_all(v):
        total = n_u * n_z * n_x
        for i in range(total.bit_length() - 1):
            bit = 1 << i
            pairs = [(n, n ^ bit) for n in range(total)]
            v = v + lax.ppermute(v, AXES, pairs)
        return v

    entry_home = dot_nn(inputs, w_skip[:d]) + dot_nn(skip_in, w_skip[d:])
    entry = away(entry_home.astype(BF)).astype(F32)
    group_lengths = away(lengths)[0]
    grad_low = away(cotangent)
    inputs_away = away(inputs)
    skip_away = away(skip_in)

    segment, places = frame_segments(group_lengths, jnp.arange(group, dtype=jnp.int32))
    own_places = lax.dynamic_slice_in_dim(places, me * frames, frames)
    tables = rotary_tables(own_places)
    col, row = segment[:, None], segment[None, :]

    inverse_one = rms_parts(entry)
    normed_one = (entry * inverse_one * gain_one).astype(BF)
    qkv = dot_nn(normed_one, w_qkv)
    query = (rotate(qkv[:, :d], tables, 1.0)).astype(BF) * BF(HEAD_DIM**-0.5)
    keys = rotate(qkv[:, d : 2 * d], tables, 1.0).astype(BF)
    values = qkv[:, 2 * d :].astype(BF)

    def to_heads(*arrays):
        n = len(arrays)
        v = jnp.stack([a.reshape(frames, parts, width) for a in arrays], axis=2)
        v = lax.all_to_all(
            v.reshape(frames, parts * n * width), PLANE, split_axis=1, concat_axis=0, tiled=True
        )
        return [v[:, i * width : (i + 1) * width] for i in range(n)]

    def to_frames(*arrays):
        n = len(arrays)
        v = jnp.concatenate(arrays, axis=1)
        v = lax.all_to_all(v, PLANE, split_axis=0, concat_axis=1, tiled=True)
        v = v.reshape(frames, parts, n, width)
        return [v[:, :, i].reshape(frames, d) for i in range(n)]

    head_query, head_keys, head_values = to_heads(query, keys, values)
    head_mixed, lse = call_forward(head_query, head_keys, head_values, col, row)
    (mixed,) = to_frames(head_mixed)

    middle = entry + dot_nn(mixed, w_out)
    inverse_two = rms_parts(middle)
    normed_two = (middle * inverse_two * gain_two).astype(BF)
    up = dot_nn(normed_two, w_up) + b_up
    d_active = dot_nt(grad_low, w_down)
    active, slope = gelu_both(up)
    d_up = (d_active * slope).astype(BF)
    result_away = (middle + dot_nn(active.astype(BF), w_down) + b_down).astype(BF)
    result = home(result_away)
    d_normed_two = dot_nt(d_up, w_up)
    middle_part, g_gain_two = rms_back(middle, inverse_two, gain_two, d_normed_two)
    d_middle = grad_low.astype(F32) + middle_part
    d_branch = d_middle.astype(BF)
    d_mixed = dot_nt(d_branch, w_out).astype(BF)
    (head_grad,) = to_heads(d_mixed)
    dq, dk, dv = call_backward(
        head_query, head_keys, head_values, head_mixed, head_grad, col, row, lse
    )

    chunk = hidden // (n_z * parts)
    w_up_own = lax.dynamic_slice(
        w_up.reshape(d, n_z, n_x, n_u, chunk), (0, 0, x, u, 0), (d, n_z, 1, 1, chunk)
    ).reshape(d, n_z * chunk)
    w_down_own = lax.dynamic_slice(
        w_down.reshape(n_z, n_x, n_u, chunk, d), (0, x, u, 0, 0), (n_z, 1, 1, chunk, d)
    ).reshape(n_z * chunk, d)
    b_up_own = lax.dynamic_slice(
        b_up.reshape(n_z, n_x, n_u, chunk), (0, x, u, 0), (n_z, 1, 1, chunk)
    ).reshape(n_z * chunk)
    plane_grad = gather_plane(grad_low)
    plane_normed = gather_plane(normed_two)
    up_own = dot_nn(plane_normed, w_up_own) + b_up_own
    active_own, slope_own = gelu_both(up_own)
    d_up_own = (dot_nt(plane_grad, w_down_own) * slope_own).astype(BF)
    g_down = dot_tn(active_own.astype(BF), plane_grad)
    g_up = dot_tn(plane_normed, d_up_own)
    down_z = reduce_z(g_down.astype(BF))
    up_z = reduce_z(g_up.astype(BF))
    out_down = lax.all_gather(down_z, "u", axis=0, tiled=True).astype(F32)
    out_up = finish_columns(up_z)
    out_up = (
        out_up.reshape(n_u, n_x, -1, n_z, chunk).transpose(2, 3, 1, 0, 4).reshape(-1, hidden)
    ).astype(F32)

    plane_mixed = gather_plane(mixed)
    own_branch = gather_order(
        lax.all_to_all(d_branch, PLANE, split_axis=1, concat_axis=0, tiled=True)
    )
    g_out = dot_tn(plane_mixed, own_branch)
    out_out = (
        finish_columns(reduce_z(g_out.astype(BF))).transpose(1, 0, 2).reshape(-1, d).astype(F32)
    )

    low = [a.astype(BF) for a in (dq, dk, dv)]
    frame_query, frame_keys, frame_values = to_frames(*low)
    d_qkv = jnp.concatenate(
        [
            rotate(frame_query.astype(F32), tables, -1.0).astype(BF),
            rotate(frame_keys.astype(F32), tables, -1.0).astype(BF),
            frame_values,
        ],
        axis=1,
    )
    d_normed_one = dot_nt(d_qkv, w_qkv)
    entry_part, g_gain_one = rms_back(entry, inverse_one, gain_one, d_normed_one)
    d_entry = (d_middle + entry_part).astype(BF)
    d_entry_home = home(d_entry)
    d_joined = dot_nt(d_entry_home, w_skip)
    d_inputs = d_joined[:, :d].astype(BF)
    d_skip = d_joined[:, d:].astype(BF)

    group_tables = rotary_tables(places)
    head_d_qkv = jnp.concatenate(
        [
            rotate(low[0].astype(F32), group_tables, -1.0).astype(BF),
            rotate(low[1].astype(F32), group_tables, -1.0).astype(BF),
            low[2],
        ],
        axis=1,
    )
    plane_first = gather_plane(normed_one)
    g_qkv = dot_tn(plane_first, gather_order(head_d_qkv))
    plane_inputs = gather_plane(inputs_away)
    plane_skip = gather_plane(skip_away)
    own_entry = gather_order(
        lax.all_to_all(d_entry, PLANE, split_axis=1, concat_axis=0, tiled=True)
    )
    g_skip = jnp.concatenate([dot_tn(plane_inputs, own_entry), dot_tn(plane_skip, own_entry)])
    out_qkv = finish_columns(reduce_z(g_qkv.astype(BF)))
    out_qkv = (
        out_qkv.reshape(parts, -1, 3, width).transpose(1, 2, 0, 3).reshape(-1, 3 * d).astype(F32)
    )
    out_skip = (
        finish_columns(reduce_z(g_skip.astype(BF))).transpose(1, 0, 2).reshape(-1, d).astype(F32)
    )

    early = sum_all(
        jnp.concatenate(
            [
                g_gain_two,
                jnp.sum(d_up.astype(F32), axis=0),
                jnp.sum(cotangent.astype(F32), axis=0),
            ]
        )
    )
    total_gain_one = sum_all(g_gain_one)
    return (
        result,
        d_inputs,
        d_skip,
        out_skip,
        total_gain_one,
        out_qkv,
        out_out,
        early[:d],
        out_up,
        early[d : d + hidden],
        out_down,
        early[d + hidden :],
    )


def local_fast(
    sizes,
    inputs,
    skip_in,
    lengths,
    cotangent,
    w_skip,
    gain_one,
    w_qkv,
    w_out,
    gain_two,
    w_up,
    b_up,
    w_down,
    b_down,
):
    made = call_layer(
        (inputs, skip_in, cotangent, w_skip, w_qkv, w_out, w_up, w_down),
        lengths,
        (gain_one[None], gain_two[None], b_up[None], b_down[None]),
    )
    (
        result,
        d_inputs,
        d_skip,
        g_skip,
        g_qkv,
        g_out,
        g_up,
        g_down,
        total_one,
        total_two,
        total_up,
        total_down,
    ) = call_widen(made)
    return (
        result,
        d_inputs,
        d_skip,
        g_skip,
        total_one,
        g_qkv,
        g_out,
        total_two,
        g_up,
        total_up,
        g_down,
        total_down,
    )


def solution(mesh):
    n_u, n_s = mesh.shape["utt"], mesh.shape["seq"]
    sizes = (n_u, n_u, n_s // n_u)
    program = local_fast if sizes == (4, 4, 2) else local
    inner = Mesh(mesh.devices.reshape(sizes), AXES)
    rows, seq = P(AXES, None), P(("z", "x"), None)
    in_specs = (rows, rows, P("u", None), rows) + (P(),) * 9
    out_specs = (rows, rows, rows, seq, P(), seq, seq, P(), seq, P(), seq, P())
    return jax.shard_map(
        functools.partial(program, sizes),
        mesh=inner,
        in_specs=in_specs,
        out_specs=out_specs,
        check_vma=False,
    )
```

```python
import functools
import math

import jax
import jax.numpy as jnp
from jax import lax
from jax.experimental import pallas as pl
from jax.experimental.pallas import tpu as pltpu
from jax.sharding import Mesh, PartitionSpec as P

HEAD_DIM = 64
EPSILON = 1e-06
BF = jnp.bfloat16
F32 = jnp.float32
AXES = ("u", "z", "x")
PLANE = ("u", "x")


def dot_nn(a, b):
    return lax.dot_general(a, b, (((1,), (0,)), ((), ())), preferred_element_type=F32)


def dot_nt(a, b):
    return lax.dot_general(a, b, (((1,), (1,)), ((), ())), preferred_element_type=F32)


def dot_tn(a, b):
    return lax.dot_general(a, b, (((0,), (0,)), ((), ())), preferred_element_type=F32)


def attention_forward(q_ref, k_ref, v_ref, col_ref, row_ref, o_ref, lse_ref, acc, out_t):
    forward_heads(q_ref, k_ref, v_ref, col_ref, row_ref[...], o_ref, lse_ref, acc, out_t)


def forward_heads(q_ref, k_ref, v_ref, col_ref, segment_row, o_ref, lse_ref, acc, out_t):
    frames, width = q_ref.shape
    heads = width // HEAD_DIM
    block = frames // (frames // 352)
    lane = lax.broadcasted_iota(jnp.int32, (1, width), 1)
    for h in range(heads):
        own = (lane // HEAD_DIM == h).astype(BF)
        query = q_ref[...] * own
        acc[...] = jnp.zeros_like(acc)

        def step(j, carry):
            top, total = carry
            rows = pl.ds(pl.multiple_of(j * block, block), block)
            scores = dot_nt(k_ref[rows, :], query)
            scores = jnp.where(col_ref[rows, 0:1] == segment_row, scores, -1e30)
            peak = jnp.maximum(top, jnp.max(scores, axis=0, keepdims=True))
            expos = jnp.exp(scores - peak)
            shrink = jnp.exp(top - peak)
            acc[...] = acc[...] * shrink + dot_tn(v_ref[rows, :], expos.astype(BF))
            return peak, total * shrink + jnp.sum(expos, axis=0, keepdims=True)

        top, total = lax.fori_loop(
            0,
            frames // block,
            step,
            (jnp.full((1, frames), -1e30, F32), jnp.zeros((1, frames), F32)),
        )
        part = slice(h * HEAD_DIM, (h + 1) * HEAD_DIM)
        out_t[part, :] = acc[part, :] / total
        lse_ref[h : h + 1, :] = top + jnp.log(total)
    o_ref[...] = out_t[...].T.astype(BF)


def attention_backward(
    q_ref, k_ref, v_ref, o_ref, do_ref, col_ref, row_ref, lse_ref, dq_ref, dk_ref, dv_ref, acc
):
    backward_heads(
        q_ref, k_ref, v_ref, o_ref, do_ref, col_ref, row_ref[...], lse_ref, dq_ref, dk_ref, dv_ref, acc
    )


def backward_heads(
    q_ref, k_ref, v_ref, o_ref, do_ref, col_ref, segment_row, lse_ref, dq_ref, dk_ref, dv_ref, acc, between=None
):
    frames, width = q_ref.shape
    heads = width // HEAD_DIM
    block = frames // (frames // 352)
    lane = lax.broadcasted_iota(jnp.int32, (1, width), 1)
    product_t = (o_ref[...].astype(F32) * do_ref[...].astype(F32)).T
    for h in range(heads):
        own = (lane // HEAD_DIM == h).astype(BF)
        query = q_ref[...] * own
        grad = do_ref[...] * own
        part = slice(h * HEAD_DIM, (h + 1) * HEAD_DIM)
        delta = jnp.sum(product_t[part, :], axis=0, keepdims=True)
        log_total = lse_ref[h : h + 1, :]

        def step(j, _):
            rows = pl.ds(pl.multiple_of(j * block, block), block)
            keys = k_ref[rows, :]
            scores = dot_nt(keys, query)
            same = col_ref[rows, 0:1] == segment_row
            probs = jnp.where(same, jnp.exp(scores - log_total), 0.0)
            d_probs = dot_nt(v_ref[rows, :], grad)
            d_scores = (probs * (d_probs - delta)).astype(BF)
            value_part = dot_nn(probs.astype(BF), grad)
            key_part = dot_nn(d_scores, query)
            if h == 0:
                dv_ref[rows, :] = value_part
                dk_ref[rows, :] = key_part
            else:
                dv_ref[rows, :] += value_part
                dk_ref[rows, :] += key_part
            query_part = dot_tn(keys * own, d_scores)

            if h == 0:

                @pl.when(j == 0)
                def _():
                    acc[...] = query_part

                @pl.when(j > 0)
                def _():
                    acc[...] += query_part

            else:
                acc[...] += query_part
            return 0

        lax.fori_loop(0, frames // block, step, 0)
        if h == 0 and between is not None:
            between()
    dq_ref[...] = acc[...].T * (HEAD_DIM**-0.5)


def call_forward(query, keys, values, col, row):
    frames, width = query.shape
    return pl.pallas_call(
        attention_forward,
        out_shape=(
            jax.ShapeDtypeStruct((frames, width), BF),
            jax.ShapeDtypeStruct((width // HEAD_DIM, frames), F32),
        ),
        scratch_shapes=[pltpu.VMEM((width, frames), F32), pltpu.VMEM((width, frames), F32)],
        compiler_params=pltpu.CompilerParams(vmem_limit_bytes=56 * 2**20),
        cost_estimate=pl.CostEstimate(
            flops=16 * frames * frames * width, bytes_accessed=10 * frames * width, transcendentals=0
        ),
        name="attention_forward",
    )(query, keys, values, col, row)


def call_backward(query, keys, values, mixed, grad, col, row, lse):
    frames, width = query.shape
    shape = jax.ShapeDtypeStruct((frames, width), F32)
    return pl.pallas_call(
        attention_backward,
        out_shape=(shape, shape, shape),
        scratch_shapes=[pltpu.VMEM((width, frames), F32)],
        compiler_params=pltpu.CompilerParams(vmem_limit_bytes=56 * 2**20),
        cost_estimate=pl.CostEstimate(
            flops=32 * frames * frames * width, bytes_accessed=20 * frames * width, transcendentals=0
        ),
        name="attention_backward",
    )(query, keys, values, mixed, grad, col, row, lse)


def frame_segments(own_lengths, positions):
    slots = own_lengths.shape[0]
    upto = jnp.arange(slots)[:, None] >= jnp.arange(slots)[None, :]
    ends_at = jnp.sum(jnp.where(upto, own_lengths[None, :], 0), axis=1)
    starts_at = ends_at - own_lengths
    segment = jnp.sum((positions[:, None] >= ends_at[None, :]).astype(jnp.int32), axis=1)
    index = jnp.arange(slots, dtype=jnp.int32)
    offset = jnp.sum(jnp.where(segment[:, None] == index[None, :], starts_at[None, :], 0), axis=1)
    return segment, positions - offset


def rotary_tables(places):
    freqs = jnp.exp(
        jnp.arange(HEAD_DIM // 2, dtype=F32) * (-2.0 * math.log(10000.0) / HEAD_DIM)
    )
    angles = places.astype(F32)[:, None] * freqs[None, :]
    cosine, sine = jnp.cos(angles), jnp.sin(angles)
    return (
        jnp.concatenate([cosine, cosine], axis=1)[:, None, :],
        jnp.concatenate([-sine, sine], axis=1)[:, None, :],
    )


def rotate(v, tables, sign):
    frames, width = v.shape
    shaped = v.reshape(frames, width // HEAD_DIM, HEAD_DIM)
    half = HEAD_DIM // 2
    swapped = jnp.concatenate([shaped[..., half:], shaped[..., :half]], axis=-1)
    return (shaped * tables[0] + swapped * (sign * tables[1])).reshape(frames, width)


def rms_parts(hidden):
    return lax.rsqrt(jnp.mean(hidden * hidden, axis=-1, keepdims=True) + EPSILON)


def rms_back(hidden, inverse, gain, grad):
    scaled = hidden * inverse
    weighted = grad * gain
    inner = jnp.mean(weighted * scaled, axis=-1, keepdims=True)
    return inverse * (weighted - scaled * inner), jnp.sum(grad * scaled, axis=0)


def gelu_both(t):
    bell = 0.5 * (1.0 + lax.erf(t * 0.7071067811865476))
    return t * bell, bell + t * (0.3989422804014327 * jnp.exp(-0.5 * t * t))


TOK = 176
MESH_ID = pl.DeviceIdType.MESH


def flip_low(u):
    return u + 1 - 2 * lax.rem(u, 2)


def flip_high(u):
    return u + 2 - 4 * lax.div(u, 2)


def swap_bits(u):
    return 2 * lax.rem(u, 2) + lax.div(u, 2)


def both(a, b):
    return jnp.logical_and(a, b)


def gelu_pair(t):
    bell = jnp.exp(-0.5 * (t * t))
    s = 1.0 / (1.0 + jnp.abs(t) * (0.3275911 * 0.7071067811865476))
    tail = 0.5 * 1.061405429 * s - 0.5 * 1.453152027
    tail = tail * s + 0.5 * 1.421413741
    tail = tail * s - 0.5 * 0.284496736
    tail = (tail * s + 0.5 * 0.254829592) * s * bell
    below = jnp.where(t < 0.0, tail, 1.0 - tail)
    return t * below, below + t * (0.3989422804014327 * bell)


def rms_back_rows(hidden, inverse, gain, grad):
    scaled = hidden * inverse
    weighted = grad * gain
    inner = jnp.mean(weighted * scaled, axis=-1, keepdims=True)
    return inverse * (weighted - scaled * inner), jnp.sum(grad * scaled, axis=0, keepdims=True)


class Sender:
    def __init__(self, send, recv, load):
        self.send, self.recv, self.load = send, recv, load
        self.n = self.m = 0
        self.sent, self.kept = [], []

    def remote(self, src, dst, device, arrival=None):
        copy = pltpu.make_async_remote_copy(
            src_ref=src,
            dst_ref=dst,
            send_sem=self.send.at[self.n],
            recv_sem=self.recv.at[self.n] if arrival is None else arrival,
            device_id=device,
            device_id_type=MESH_ID,
        )
        self.n += 1
        return copy

    def push(self, src, dst, device):
        copy = self.remote(src, dst, device)
        copy.start()
        self.sent.append(copy)
        return copy

    def push_or_keep(self, src, dst, device, own, arrival=None):
        arrival = self.recv.at[self.n] if arrival is None else arrival
        inside = pltpu.make_async_copy(src, dst, arrival)
        copy = self.remote(src, dst, device, arrival)

        @pl.when(own)
        def _():
            inside.start()

        @pl.when(jnp.logical_not(own))
        def _():
            copy.start()

        self.kept.append((copy, own))
        return copy

    def local(self, src, dst):
        copy = pltpu.make_async_copy(src, dst, self.load.at[self.m])
        self.m += 1
        copy.start()
        return copy

    def finish(self):
        for copy in self.sent:
            copy.wait_send()
        settle(self.kept)
        self.sent, self.kept = [], []

    def take(self, n):
        taken, self.kept = self.kept[-n:], self.kept[:-n]
        return taken


def settle(kept):
    for copy, own in kept:

        @pl.when(jnp.logical_not(own))
        def _(copy=copy):
            copy.wait_send()


def plane_peers(u, z, x):
    peers = []
    for k in range(8):
        a = flip_low(u) if k & 2 else u
        a = flip_high(a) if k & 4 else a
        b = 1 - x if k & 1 else x
        peers.append(((a, z, b), 2 * a + b))
    return peers


def rows_of(p, start=0, size=TOK):
    return pl.ds(pl.multiple_of(p * TOK + start, 16), size)


class PlaneGather:
    def __init__(self, sender, buffer, peers, start=0, size=TOK):
        self.sender, self.buffer, self.peers = sender, buffer, peers
        self.first, self.size = start, size
        self.low = size // 32 * 16
        self.x, self.y = self.copy(0, 1), self.copy(0, 4)
        self.over_y = self.copy(1, 4, self.low, size - self.low)
        self.over_x = self.copy(4, 1, 0, self.low)
        self.cores = [self.copy(k, 2) for k in (0, 1, 4, 5)]
        self.copies = [self.x, self.y, self.over_x, self.over_y] + self.cores

    def copy(self, k, to, start=0, size=None):
        rows = rows_of(self.peers[k][1], self.first + start, size or self.size)
        return self.sender.remote(self.buffer.at[rows], self.buffer.at[rows], self.peers[to][0])

    def start(self):
        self.x.start()
        self.y.start()
        self.cores[0].start()

    def forward(self):
        self.x.wait_recv()
        self.over_y.start()
        self.cores[1].start()
        self.y.wait_recv()
        self.over_x.start()
        self.cores[2].start()

    def corner(self):
        self.over_x.wait_recv()
        self.over_y.wait_recv()
        self.cores[3].start()

    def core(self, i):
        self.cores[i].wait_recv()

    def left(self):
        for copy in self.copies:
            copy.wait_send()

    def done(self):
        for copy in self.cores:
            copy.wait_recv()
        self.left()


class PlaneSum:
    def __init__(self, sender, terms, first, second, third, place):
        self.sender, self.terms = sender, terms
        self.first, self.second, self.third = first, second, third
        u, z, x = place
        self.low, self.high = lax.rem(z, 2), lax.div(z, 2)
        self.near, self.far = (u, flip_low(z), x), (u, flip_high(z), x)
        self.rows = third.shape[0]
        self.waits = [
            sender.remote(terms.at[self.chunk(j, 1 - self.low)], first.at[j], self.near)
            for j in range(2)
        ]
        sender.sent += self.waits

    def chunk(self, j, low):
        return pl.ds(pl.multiple_of((2 * j + low) * self.rows, self.rows), self.rows)

    def start(self):
        for copy in self.waits:
            copy.start()

    def middle(self):
        for copy in self.waits:
            copy.wait_recv()
        for j in range(2):
            own = self.terms[self.chunk(j, self.low), :].astype(F32)
            self.second[j] = (own + self.first[j].astype(F32)).astype(BF)
        self.wait = self.sender.push(self.second.at[1 - self.high], self.third, self.far)

    def end(self, out):
        self.wait.wait_recv()
        out[...] = (self.second[self.high].astype(F32) + self.third[...].astype(F32)).astype(BF)


class ColumnGather:
    def __init__(self, sender, source, out, peers, x):
        self.sender, self.out, self.peers = sender, out, peers
        rows = out.shape[1]
        me = peers[0][1]

        def part(b):
            return pl.ds(pl.multiple_of(b * rows, rows), rows)

        self.direct = [
            (k, sender.push(source.at[part(peers[k][0][2])], out.at[me], peers[k][0]))
            for k in (5, 4, 1)
        ]
        self.cores = [sender.push(source.at[part(x)], out.at[me], peers[2][0])]
        out[me] = source[part(x), :]

    def forward(self):
        for k, copy in self.direct:
            copy.wait_recv()
            slot = self.out.at[self.peers[k][1]]
            self.cores.append(self.sender.push(slot, slot, self.peers[2][0]))

    def done(self):
        for copy in self.cores:
            copy.wait_recv()


class RowGather:
    def __init__(self, sender, source, out, peers, u):
        self.sender, self.out, self.peers = sender, out, peers
        self.rows = source.shape[0]
        self.far = sender.push(source, out.at[self.part(u)], peers[4][0])
        self.cores = [sender.push(source, out.at[self.part(u)], peers[2][0])]
        out[self.part(u), :] = source[...]

    def part(self, u):
        return pl.ds(pl.multiple_of(u * self.rows, self.rows), self.rows)

    def forward(self):
        self.far.wait_recv()
        block = self.out.at[self.part(self.peers[4][0][0])]
        self.cores.append(self.sender.push(block, block, self.peers[2][0]))

    def done(self):
        for copy in self.cores:
            copy.wait_recv()


def layer_kernel(
    lengths_ref,
    gain_one_ref,
    gain_two_ref,
    b_up_ref,
    b_down_ref,
    inputs_ref,
    skip_ref,
    cot_ref,
    w_skip_ref,
    w_qkv_ref,
    w_out_ref,
    w_up_ref,
    w_down_ref,
    result_out,
    inputs_out,
    skip_out,
    g_skip_out,
    g_qkv_out,
    g_out_out,
    g_up_out,
    g_down_out,
    vector_out,
    normed_kept,
    wide_a,
    wide_b,
    w_out,
    n2,
    ct,
    db,
    joined,
    q,
    k,
    v,
    o,
    grad,
    lse,
    cos_t,
    sin_t,
    seg,
    entry,
    middle,
    dq,
    dk,
    result,
    result_r,
    d_mixed,
    d_heads,
    d_frames,
    entry_r,
    gd,
    gu,
    gq,
    gs,
    go,
    d_up,
    d1,
    d2,
    d3,
    dz,
    u1,
    u2,
    u3,
    uz,
    q1,
    q2,
    q3,
    qz,
    s1,
    s2,
    s3,
    sz,
    o1,
    o2,
    fin_d,
    fin_u,
    fin_q,
    fin_s,
    fin_o,
    vec,
    vec_plane,
    vec_sum,
    vec_z,
    acc,
    lens,
    lens_r,
    send,
    recv,
    load,
    spread,
):
    u, z, x = (lax.axis_index(a) for a in AXES)
    me = 2 * u + x
    peers = plane_peers(u, z, x)
    place = (u, z, x)
    d = entry.shape[1]
    group = n2.shape[0]
    hidden = wide_a.shape[1]
    heads_at = pl.ds(pl.multiple_of(me * 128, 128), 128)
    plane = swap_bits(u)
    away = (z, plane, x)
    stays_away = both(u == z, plane == z)
    own_home = swap_bits(z)
    home = (own_home, u, x)
    stays_home = both(own_home == u, u == z)
    sender = Sender(send, recv, load)
    mine = rows_of(me)
    low, high = 80, 96
    z_devices = (
        (u, flip_low(z), x),
        (u, flip_high(z), x),
        (u, flip_low(flip_high(z)), x),
    )

    barrier = pltpu.get_barrier_semaphore()

    def greet(device):
        pl.semaphore_signal(barrier, inc=1, device_id=device, device_id_type=MESH_ID)

    for device, _ in peers[1:]:
        greet(device)
    for device in z_devices:
        greet(device)

    @pl.when(jnp.logical_not(stays_away))
    def _():
        greet(away)
        greet(home)

    got_x = sender.local(inputs_ref, gd.at[pl.ds(0, TOK)])
    got_s = sender.local(skip_ref, gd.at[pl.ds(TOK, TOK)])
    got_w = [
        sender.local(w_skip_ref.at[pl.ds(i * d, d)], wide_b.at[pl.ds(i * d, d)]) for i in range(2)
    ]
    got_q = [
        sender.local(
            w_qkv_ref.at[:, pl.ds(pl.multiple_of(c * d + me * 128, 128), 128)],
            wide_a.at[:, pl.ds(c * 128, 128)],
        )
        for c in range(3)
    ]
    slots = lengths_ref.shape[1]
    for s in range(slots):
        lens[s : s + 1, :] = jnp.full((1, 128), lengths_ref[0, s].astype(F32), F32)
    lens[slots:8, :] = jnp.zeros((8 - slots, 128), F32)
    got_x.wait()
    got_w[0].wait()
    value = dot_nn(gd[:TOK, :], wide_b[:d, :])
    got_s.wait()
    got_w[1].wait()
    d_mixed[...] = (value + dot_nn(gd[TOK : 2 * TOK, :], wide_b[d : 2 * d, :])).astype(BF)
    pl.semaphore_wait(barrier, jnp.where(stays_away, 10, 12))
    sent_entry = [
        sender.push_or_keep(
            d_mixed.at[pl.ds(a, n)], entry.at[pl.ds(a, n)], away, stays_away
        )
        for a, n in ((0, low), (low, high))
    ]
    entry_left = sender.take(2)
    sent_lens = sender.push_or_keep(lens, lens_r, away, stays_away)
    got_down = sender.local(w_down_ref, wide_b)
    got_out = sender.local(w_out_ref, w_out)

    lane = lax.broadcasted_iota(jnp.int32, (TOK, 128), 1)
    for a in range(4):
        for b in range(2):
            for pair in range(2):
                halves = []
                for s in range(2):
                    block = 4 * (2 * pair + s) + 2 * b + a // 2
                    top = block // (d // 128) * TOK
                    first = block % (d // 128) * 128
                    piece = gd[top : top + TOK, first : first + 128].astype(F32)
                    if a % 2 != s:
                        piece = pltpu.roll(piece, 64, 1)
                    halves.append(piece)
                j = 2 * a + b
                gu[
                    j // 2 * TOK : (j // 2 + 1) * TOK,
                    j % 2 * 256 + pair * 128 : j % 2 * 256 + (pair + 1) * 128,
                ] = jnp.where(lane < 64, halves[0], halves[1]).astype(BF)

    def joined_for(a, b):
        return gu.at[
            pl.ds(pl.multiple_of(a * TOK, 16), TOK), pl.ds(pl.multiple_of(b * 256, 256), 256)
        ]

    def joined_from(a, b):
        first = lax.rem(a, 2) * 512 + b * 256
        return fin_d.at[
            pl.ds(pl.multiple_of(lax.div(a, 2) * TOK, 16), TOK),
            pl.ds(pl.multiple_of(first, 256), 256),
        ]

    own_joined = sender.local(joined_for(u, x), joined_from(u, x))
    got_joined = []
    for device, _ in peers[1:]:
        copy = sender.remote(joined_for(device[0], device[2]), joined_from(u, x), device)
        copy.start()
        got_joined.append(copy)

    sent_lens.wait_recv()
    freqs = jnp.exp(lax.rem(lane, 32).astype(F32) * (-2.0 * math.log(10000.0) / HEAD_DIM))
    front = lax.rem(lane, 64) < 32
    sign = jnp.where(front, -1.0, 1.0)

    def table(i, _):
        rows = rows_of(i)
        at = (lax.broadcasted_iota(jnp.int32, (TOK, 128), 0) + i * TOK).astype(F32)
        spot, segment, end = at, jnp.zeros_like(at), jnp.zeros((1, 128), F32)
        for s in range(slots):
            length = lens_r[s : s + 1, :]
            end = end + length
            past = at >= end
            segment = segment + jnp.where(past, 1.0, 0.0)
            spot = spot - jnp.where(past, length, 0.0)
        angle = spot * freqs
        cos_t[rows, :] = jnp.cos(angle)
        sin_t[rows, :] = jnp.sin(angle) * sign
        seg[rows, :] = segment
        return 0

    lax.fori_loop(0, group // TOK, table, 0)
    at = lax.broadcasted_iota(jnp.int32, (1, group), 1).astype(F32)
    segment_row, end = jnp.zeros((1, group), F32), jnp.zeros((1, 1), F32)
    for s in range(slots):
        end = end + lens_r[s : s + 1, 0:1]
        segment_row = segment_row + jnp.where(at >= end, 1.0, 0.0)
    lse[2:3, :] = segment_row
    for copy in got_q:
        copy.wait()

    def turn(t, rows, way):
        swapped = jnp.where(front, pltpu.roll(t, 96, 1), pltpu.roll(t, 32, 1))
        return t * cos_t[rows, :] + swapped * (way * sin_t[rows, :])

    def project(i):
        first = peers[i][0][0] * (2 * TOK)
        rows = pl.ds(pl.multiple_of(first, 16), 2 * TOK)
        value = dot_nn(n2[rows, :], wide_a[:, :384])
        for h in range(2):
            rows = pl.ds(pl.multiple_of(first + h * TOK, 16), TOK)
            part = value[h * TOK : (h + 1) * TOK]
            q[rows, :] = (
                turn(part[:, :128], rows, 1.0).astype(BF).astype(F32) * HEAD_DIM**-0.5
            ).astype(BF)
            k[rows, :] = turn(part[:, 128:256], rows, 1.0).astype(BF)
            v[rows, :] = part[:, 256:].astype(BF)

    first_a = PlaneGather(sender, n2, peers, 0, low)
    first_b = PlaneGather(sender, n2, peers, low, high)
    for copy, gather, (a, n) in zip(sent_entry, (first_a, first_b), ((0, low), (low, high))):
        copy.wait_recv()
        value = entry[a : a + n, :].astype(F32)
        n2[rows_of(me, a, n), :] = (value * rms_parts(value) * gain_one_ref[...]).astype(BF)
        gather.start()
    sent_cot = sender.push_or_keep(cot_ref, ct.at[rows_of(2 * z + x)], away, stays_away)
    first_a.forward()
    first_b.forward()
    project(0)
    for gather in (first_a, first_b):
        gather.core(0)
        gather.core(1)
    project(2)
    first_a.corner()
    first_b.corner()
    project(4)
    for gather in (first_a, first_b):
        gather.core(2)
        gather.core(3)
    project(6)
    got_up = sender.local(w_up_ref, wide_a)
    kept_normed = sender.local(n2, normed_kept)
    sent_cot.wait_recv()
    gather_cot = PlaneGather(sender, ct, peers)
    gather_cot.start()
    own_joined.wait()
    for copy in got_joined:
        copy.wait_recv()
    for a in range(4):
        to = a % 2 * 2 + a // 2
        for b in range(2):
            sender.push_or_keep(
                joined_from(jnp.int32(a), jnp.int32(b)),
                joined.at[rows_of(2 * z + b)],
                (u, jnp.int32(to), x),
                z == to,
                spread.at[2 * z + b],
            )
    joined_left = sender.take(8)

    pl.run_scoped(
        lambda out_t: forward_heads(q, k, v, seg, segment_row, o, lse, acc, out_t),
        pltpu.VMEM((128, group), F32),
    )
    kept_normed.wait()
    for gather in (first_a, first_b):
        gather.left()
    own_mixed = sender.local(o.at[mine], d_frames.at[0, :, heads_at])
    got_mixed = [
        sender.push(o.at[rows_of(peers[i][1])], d_frames.at[0, :, heads_at], peers[i][0])
        for i in range(1, 8)
    ]
    gather_cot.forward()
    got_down.wait()
    step = d

    def back_feed(c, _):
        cols = pl.ds(pl.multiple_of(c * step, step), step)
        db[rows_of(c), :] = dot_nt(ct[mine, :], wide_b[cols, :]).astype(BF)
        return 0

    lax.fori_loop(0, hidden // step, back_feed, 0)
    own_mixed.wait()
    for copy in got_mixed:
        copy.wait_recv()

    got_out.wait()
    value = entry[...].astype(F32) + dot_nn(d_frames[0], w_out[...])
    middle[...] = value
    n2[mine, :] = (value * rms_parts(value) * gain_two_ref[...]).astype(BF)
    normed_a = PlaneGather(sender, n2, peers, 0, low)
    normed_b = PlaneGather(sender, n2, peers, low, high)
    normed_a.start()
    normed_b.start()

    dq[...] = jnp.zeros_like(dq)
    dk[...] = jnp.zeros_like(dk)

    def add_to(ref, value):
        for j in range(d // 128):
            ref[j * TOK : (j + 1) * TOK, :] += value[:, j * 128 : (j + 1) * 128]

    def side_by_side(ref):
        return jnp.concatenate([ref[j * TOK : (j + 1) * TOK, :] for j in range(d // 128)], axis=1)

    got_up.wait()

    def feed(c, _):
        cols = pl.ds(pl.multiple_of(c * step, step), step)
        up = dot_nn(n2[mine, :], wide_a[:, cols]) + b_up_ref[:, cols]
        active, slope = gelu_pair(up)
        d_up = (db[rows_of(c), :].astype(F32) * slope).astype(BF)
        add_to(dq, dot_nn(active.astype(BF), wide_b[cols, :]))
        add_to(dk, dot_nt(d_up, wide_a[:, cols]))
        sums = jnp.sum(d_up.astype(F32), axis=0, keepdims=True)
        vec[pl.ds(8 + 2 * c, 1), :] = sums[:, : step // 2]
        vec[pl.ds(9 + 2 * c, 1), :] = sums[:, step // 2 :]
        return 0

    half = hidden // step // 2
    lax.fori_loop(0, half, feed, 0)
    gather_cot.corner()
    lax.fori_loop(half, 2 * half, feed, 0)
    normed_a.forward()
    normed_b.forward()
    value = middle[...]
    inverse = rms_parts(value)
    back, g_gain_two = rms_back_rows(value, inverse, gain_two_ref[...], side_by_side(dk))
    grad_out = ct[mine, :].astype(F32)
    d_middle = grad_out + back
    result[...] = (value + side_by_side(dq) + b_down_ref[...]).astype(BF)
    middle[...] = d_middle
    db[mine, :] = d_middle.astype(BF)
    settle(entry_left)
    d_mixed[...] = dot_nt(db[mine, :], w_out[...]).astype(BF)
    own_grad = sender.local(d_mixed.at[:, heads_at], grad.at[mine])
    got_grad = [
        sender.push(
            d_mixed.at[:, pl.ds(pl.multiple_of(peers[i][1] * 128, 128), 128)],
            grad.at[mine],
            peers[i][0],
        )
        for i in range(1, 8)
    ]
    g_b_down = jnp.sum(grad_out, axis=0, keepdims=True)
    for i in range(2):
        part = slice(i * d // 2, (i + 1) * d // 2)
        vec[2 + i : 3 + i, :] = g_gain_two[:, part]
        vec[4 + i : 5 + i, :] = g_b_down[:, part]
    vec[6:8, :] = jnp.zeros((2, d // 2), F32)
    gather_cot.done()

    chunk = hidden // 32
    sum_down = PlaneSum(sender, gd, d1, d2, d3, place)
    sum_up = PlaneSum(sender, gu, u1, u2, u3, place)
    gather_branch = PlaneGather(sender, db, peers)

    def own_units(w_up_own, w_down_own, active):
        starts = [
            pl.multiple_of((2 * s + x) * (4 * chunk) + u * chunk, chunk) for s in range(4)
        ]
        for s, first in enumerate(starts):
            part = slice(s * chunk, (s + 1) * chunk)
            w_up_own[:, part] = wide_a[:, pl.ds(first, chunk)]
            w_down_own[part, :] = wide_b[pl.ds(first, chunk), :]
        bias = jnp.concatenate([b_up_ref[:, pl.ds(first, chunk)] for first in starts], axis=1)

        def units(i):
            rows = pl.ds(pl.multiple_of(peers[i][0][0] * (2 * TOK), 16), 2 * TOK)
            up = dot_nn(n2[rows, :], w_up_own[...]) + bias
            act, slope = gelu_pair(up)
            active[rows, :] = act.astype(BF)
            d_up[rows, :] = (dot_nt(ct[rows, :], w_down_own[...]) * slope).astype(BF)

        units(0)
        normed_a.corner()
        normed_b.corner()
        normed_a.core(0)
        normed_b.core(0)
        normed_a.core(1)
        normed_b.core(1)
        units(2)
        units(4)
        normed_a.core(2)
        normed_b.core(2)
        normed_a.core(3)
        normed_b.core(3)
        units(6)
        normed_a.left()
        normed_b.left()
        gather_branch.start()

        def down_terms(i, _):
            cols = pl.ds(pl.multiple_of(i * 256, 256), 256)
            gd[cols, :] = dot_tn(active[:, cols], ct[...]).astype(BF)
            return 0

        lax.fori_loop(0, 4 * chunk // 256, down_terms, 0)
        sum_down.start()

    pl.run_scoped(
        own_units,
        pltpu.VMEM((d, 4 * chunk), BF),
        pltpu.VMEM((4 * chunk, d), BF),
        pltpu.VMEM((group, 4 * chunk), BF),
    )
    got_normed = sender.local(normed_kept, ct)
    got_qkv = sender.local(w_qkv_ref, wide_a.at[:, pl.ds(0, 3 * d)])
    got_skip = sender.local(w_skip_ref, wide_b.at[pl.ds(0, 2 * d)])
    own_grad.wait()
    for copy in got_grad:
        copy.wait_recv()
    sent_result = sender.push_or_keep(result, result_r, home, stays_home)

    def heads(dv):
        backward_heads(q, k, v, o, grad, seg, lse[2:3, :], lse, dq, dk, dv, acc, gather_branch.forward)

        def turn_back(i, _):
            rows = rows_of(i)
            for c, ref in ((0, dq), (1, dk)):
                t = ref[rows, :].astype(BF).astype(F32)
                d_heads[c, rows, :] = turn(t, rows, -1.0).astype(BF)
            d_heads[2, rows, :] = dv[rows, :].astype(BF)
            return 0

        lax.fori_loop(0, group // TOK, turn_back, 0)

    pl.run_scoped(heads, pltpu.VMEM((group, 128), F32))
    settle(joined_left)
    for copy in got_joined:
        copy.wait_send()
    own_frames = sender.local(d_heads.at[:, mine], d_frames.at[:, :, heads_at])
    got_frames = [
        sender.push(
            d_heads.at[:, rows_of(peers[i][1])], d_frames.at[:, :, heads_at], peers[i][0]
        )
        for i in range(1, 8)
    ]
    gather_branch.corner()

    def up_terms(i, _):
        cols = pl.ds(pl.multiple_of(i * 256, 256), 256)
        gu[cols, :] = dot_tn(n2[:, cols], d_up[...]).astype(BF)
        return 0

    lax.fori_loop(0, d // 256, up_terms, 0)
    sum_up.start()
    got_normed.wait()

    def qkv_terms(i, _):
        cols = pl.ds(pl.multiple_of(i * 256, 256), 256)
        turned = ct[:, cols].T
        for c in range(3):
            gq[cols, c * 128 : (c + 1) * 128] = dot_nn(turned, d_heads[c]).astype(BF)
        return 0

    lax.fori_loop(0, d // 256, qkv_terms, 0)
    sum_qkv = PlaneSum(sender, gq, q1, q2, q3, place)
    sum_qkv.start()
    gather_branch.done()
    go[...] = dot_tn(o[...], db[...]).astype(BF)

    same_high = lax.div(z, 2) == lax.div(u, 2)
    same_low = lax.rem(z, 2) == lax.rem(u, 2)
    owner = z == u
    to_far = sender.remote(go, o1, (u, flip_high(z), x))
    to_near = sender.remote(go, o2, (u, flip_low(z), x))

    @pl.when(jnp.logical_not(same_low))
    def _():
        to_near.start()

    sum_down.middle()

    own_frames.wait()
    for copy in got_frames:
        copy.wait_recv()
    got_qkv.wait()
    d_normed = dot_nt(d_frames[0], wide_a[:, :d])
    d_normed += dot_nt(d_frames[1], wide_a[:, d : 2 * d])
    d_normed += dot_nt(d_frames[2], wide_a[:, 2 * d : 3 * d])
    value = entry[...].astype(F32)
    back, g_gain_one = rms_back_rows(value, rms_parts(value), gain_one_ref[...], d_normed)
    wide_b[rows_of(me, 2 * d), :] = (middle[...] + back).astype(BF)
    entry_a = PlaneGather(sender, wide_b, peers, 2 * d, low)
    entry_b = PlaneGather(sender, wide_b, peers, 2 * d + low, high)
    entry_a.start()
    entry_b.start()
    sent_back = sender.push_or_keep(
        wide_b.at[rows_of(me, 2 * d)], entry_r, home, stays_home
    )

    for i in range(2):
        vec[i : i + 1, :] = g_gain_one[:, i * d // 2 : (i + 1) * d // 2]
    vec_at = pl.ds(pl.multiple_of(me * 16, 16), 16)
    got_vec = [sender.push(vec, vec_plane.at[vec_at], peers[i][0]) for i in range(1, 8)]
    vec_plane[vec_at, :] = vec[...]

    sum_up.middle()
    for s in range(8):
        rows = pl.ds(s * TOK, TOK)
        pltpu.make_async_copy(joined.at[rows], joined.at[rows], spread.at[s]).wait()
    def skip_terms(i):
        p = peers[i][1]
        return dot_tn(joined[rows_of(p), :], wide_b[rows_of(p, 2 * d), :])

    total = skip_terms(0)

    entry_a.forward()
    entry_b.forward()
    sum_qkv.middle()
    total += skip_terms(1)
    total += skip_terms(4)
    entry_a.corner()
    entry_b.corner()
    total += skip_terms(5)
    for copy in entry_a.cores + entry_b.cores:
        copy.wait_recv()
    for i in (2, 3, 6, 7):
        total += skip_terms(i)
    gs[...] = total.astype(BF)
    sum_skip = PlaneSum(sender, gs, s1, s2, s3, place)
    sum_skip.start()

    @pl.when(same_low)
    def _():
        to_near.wait_recv()
        go[...] = (go[...].astype(F32) + o2[...].astype(F32)).astype(BF)

    @pl.when(both(same_low, jnp.logical_not(same_high)))
    def _():
        to_far.start()

    for copy in got_vec:
        copy.wait_recv()
    value = vec_plane[0:16, :]
    for i in range(1, 8):
        value += vec_plane[16 * i : 16 * (i + 1), :]
    vec_sum[...] = value
    vec_at = pl.ds(pl.multiple_of(z * 16, 16), 16)
    got_vec = [sender.push(vec_sum, vec_z.at[vec_at], device) for device in z_devices]
    vec_z[vec_at, :] = vec_sum[...]

    sum_up.end(uz)
    last_up = ColumnGather(sender, uz, fin_u, peers, x)
    sum_down.end(dz)
    last_down = RowGather(sender, dz, fin_d, peers, u)

    sum_skip.middle()

    outs = []
    sent_back.wait_recv()
    got_skip.wait()
    for i, out in enumerate((inputs_out, skip_out)):
        d_frames[i] = dot_nt(entry_r[...], wide_b[i * d : (i + 1) * d, :]).astype(BF)
        outs.append(sender.local(d_frames.at[i], out))
    sum_qkv.end(qz)
    last_qkv = ColumnGather(sender, qz, fin_q, peers, x)

    @pl.when(owner)
    def _():
        to_far.wait_recv()
        fin_o[...] = (go[...].astype(F32) + o1[...].astype(F32)).astype(BF)

    def tell(i, to):
        return pltpu.make_async_remote_copy(
            src_ref=fin_o,
            dst_ref=fin_o,
            send_sem=spread.at[8 + i],
            recv_sem=spread.at[11],
            device_id=peers[to][0],
            device_id_type=MESH_ID,
        )

    tell_core, tell_far, tell_on = tell(0, 2), tell(1, 4), tell(2, 2)

    @pl.when(owner)
    def _():
        tell_far.start()
        tell_core.start()

    last_up.forward()
    last_down.forward()
    sum_skip.end(sz)
    last_skip = RowGather(sender, sz, fin_s, peers, u)
    last_qkv.forward()
    across = u == flip_high(z)

    @pl.when(jnp.logical_not(owner))
    def _():
        tell_core.wait_recv()

    @pl.when(across)
    def _():
        tell_on.start()

    last_up.done()
    for p in range(8):
        for s in range(4):
            first = (2 * s + p % 2) * 4 * chunk + p // 2 * chunk
            outs.append(
                sender.local(
                    fin_u.at[p, :, pl.ds(s * chunk, chunk)], g_up_out.at[:, pl.ds(first, chunk)]
                )
            )
    last_down.done()
    outs.append(sender.local(fin_d, g_down_out))
    for copy in got_vec:
        copy.wait_recv()
    vec_sum_out = vec_z[0:16, :] + vec_z[16:32, :] + vec_z[32:48, :] + vec_z[48:64, :]
    vec_plane[0:16, :] = vec_sum_out
    outs.append(sender.local(vec_plane.at[pl.ds(0, 16)], vector_out))
    sent_result.wait_recv()
    outs.append(sender.local(result_r, result_out))
    outs.append(sender.local(fin_o, g_out_out))
    last_skip.forward()
    last_qkv.done()
    for p in range(8):
        for c in range(3):
            outs.append(
                sender.local(
                    fin_q.at[p, :, pl.ds(c * 128, 128)],
                    g_qkv_out.at[:, pl.ds(c * d + p * 128, 128)],
                )
            )

    @pl.when(owner)
    def _():
        tell_far.wait_send()
        tell_core.wait_send()

    @pl.when(across)
    def _():
        tell_on.wait_send()

    @pl.when(jnp.logical_not(same_low))
    def _():
        to_near.wait_send()

    @pl.when(both(same_low, jnp.logical_not(same_high)))
    def _():
        to_far.wait_send()

    last_skip.done()
    outs.append(sender.local(fin_s, g_skip_out))
    for copy in outs:
        copy.wait()
    entry_a.left()
    entry_b.left()
    sender.finish()


def call_layer(arrays, lengths, vectors):
    d = arrays[0].shape[1]
    hidden = arrays[6].shape[1]
    group = 8 * TOK
    any_space = pl.BlockSpec(memory_space=pl.ANY)
    vmem = pl.BlockSpec(memory_space=pltpu.VMEM)
    smem = pl.BlockSpec(memory_space=pltpu.SMEM)
    block, wide = ((TOK, d), BF), ((group, d), BF)
    head, table, total = ((group, 128), BF), ((group, 128), F32), ((TOK, d), F32)
    unit = hidden // 8

    def sums(rows, columns):
        return [
            ((2, rows, columns), BF),
            ((2, rows, columns), BF),
            ((rows, columns), BF),
            ((rows, columns), BF),
        ]

    outs = [
        block,
        block,
        block,
        ((2 * d // 8, d), BF),
        ((d // 8, 3 * d), BF),
        ((d // 8, d), BF),
        ((d // 8, hidden), BF),
        ((unit, d), BF),
        ((16, 512), F32),
        wide,
    ]
    scratch = [
        ((d, hidden), BF),
        ((hidden, d), BF),
        ((d, d), BF),
        wide,
        wide,
        wide,
        ((group, 256), BF),
        head,
        head,
        head,
        head,
        head,
        ((8, group), F32),
        table,
        table,
        table,
        block,
        total,
        table,
        table,
        block,
        block,
        block,
        ((3, group, 128), BF),
        ((3, TOK, d), BF),
        block,
        ((unit, d), BF),
        ((d, unit), BF),
        ((d, 384), BF),
        ((256, d), BF),
        ((128, d), BF),
        ((group, unit), BF),
        *sums(unit // 4, d),
        *sums(d // 4, unit),
        *sums(d // 4, 384),
        *sums(64, d),
        ((128, d), BF),
        ((128, d), BF),
        ((unit, d), BF),
        ((8, d // 8, unit), BF),
        ((8, d // 8, 384), BF),
        ((256, d), BF),
        ((128, d), BF),
        ((16, 512), F32),
        ((128, 512), F32),
        ((16, 512), F32),
        ((64, 512), F32),
        ((128, group), F32),
        ((8, 128), F32),
        ((8, 128), F32),
    ]
    made = pl.pallas_call(
        layer_kernel,
        in_specs=[smem] + [vmem] * len(vectors) + [any_space] * len(arrays),
        out_specs=[any_space] * len(outs),
        out_shape=[jax.ShapeDtypeStruct(*o) for o in outs],
        scratch_shapes=[pltpu.VMEM(*s) for s in scratch]
        + [pltpu.SemaphoreType.DMA((160,))] * 3
        + [pltpu.SemaphoreType.DMA((12,))],
        compiler_params=pltpu.CompilerParams(
            vmem_limit_bytes=60 * 2**20 + 2**18, has_side_effects=True, collective_id=0
        ),
        name="layer",
    )(lengths, *vectors, *arrays)
    return made[:9]


def widen_kernel(*refs):
    n = 9
    ins, outs = refs[:n], refs[n:]
    for i in range(8):
        outs[i][...] = ins[i][...].astype(outs[i].dtype)
    vectors = ins[8]
    for out, row in zip(outs[8:], (0, 2, 4, 8)):
        for part in range(out.shape[1] // 512):
            out[:, part * 512 : (part + 1) * 512] = vectors[row + part : row + part + 1, :]


def call_widen(made):
    steps = 4
    whole = [pl.BlockSpec(a.shape, lambda i: (0, 0)) for a in made]
    parts = [
        pl.BlockSpec((a.shape[0] // steps, a.shape[1]), lambda i: (i, 0)) for a in made[3:8]
    ]
    d, hidden = made[5].shape[1], made[6].shape[1]
    ends = [(1, d), (1, d), (1, d), (1, hidden)]
    outs = pl.pallas_call(
        widen_kernel,
        grid=(steps,),
        in_specs=whole[:3] + parts + whole[8:],
        out_specs=whole[:3] + parts + [pl.BlockSpec(e, lambda i: (0, 0)) for e in ends],
        out_shape=[jax.ShapeDtypeStruct(a.shape, BF) for a in made[:3]]
        + [jax.ShapeDtypeStruct(a.shape, F32) for a in made[3:8]]
        + [jax.ShapeDtypeStruct(e, F32) for e in ends],
        name="widen",
    )(*made)
    one, two, down, up = (v[0] for v in outs[8:])
    return (*outs[:8], one, two, up, down)


def local(
    sizes,
    inputs,
    skip_in,
    lengths,
    cotangent,
    w_skip,
    gain_one,
    w_qkv,
    w_out,
    gain_two,
    w_up,
    b_up,
    w_down,
    b_down,
):
    n_u, n_z, n_x = sizes
    frames, d = inputs.shape
    hidden = w_up.shape[1]
    parts = n_u * n_x
    group = frames * parts
    u, z, x = (lax.axis_index(a) for a in AXES)
    me = u * n_x + x
    width = d // parts

    def line(a, b, c):
        return (a * n_z + b) * n_x + c

    def permute(v, to):
        pairs = [
            (line(a, b, c), line(*to(a, b, c)))
            for a in range(n_u)
            for b in range(n_z)
            for c in range(n_x)
        ]
        return lax.ppermute(v, AXES, pairs)

    def plane_of(a):
        return (a % 2) * (n_u // 2) + a // 2

    group_of = {plane_of(a): a for a in range(n_u)}

    def away(v):
        return permute(v, lambda a, b, c: (b, plane_of(a), c))

    def home(v):
        return permute(v, lambda a, b, c: (group_of[b], a, c))

    def swap_plane(v, bit):
        def to(a, b, c):
            other = (a * n_x + c) ^ bit
            return other // n_x, b, other % n_x

        return permute(v, to)

    plane_bits = [1 << i for i in range(parts.bit_length() - 1)]
    if n_x == 2 and n_u == 4:
        orders = ([1, 4, 2], [4, 1, 2])
    else:
        orders = (plane_bits, plane_bits)
    cut = frames // 32 * 16

    def gather_plane(v):
        pieces = []
        for piece, order in zip((v[:cut], v[cut:]), orders):
            for bit in order:
                piece = jnp.concatenate([piece, swap_plane(piece, bit)], axis=0)
            pieces.append(piece)
        return jnp.concatenate(pieces, axis=0)

    def gather_order(v):
        pieces = []
        for start, size, order in ((0, cut, orders[0]), (cut, frames - cut, orders[1])):
            offsets = [0]
            for bit in order:
                offsets = offsets + [o ^ bit for o in offsets]
            for o in offsets:
                pieces.append(
                    lax.dynamic_slice_in_dim(v, (me ^ o) * frames + start, size, axis=0)
                )
        return jnp.concatenate(pieces, axis=0)

    z_bits = n_z.bit_length() - 1

    def reduce_z(v):
        rest = v.shape[1:]
        v = v.reshape((2,) * z_bits + (v.shape[0] // n_z,) + rest)
        for bit in range(z_bits):
            axis = z_bits - 1 - bit
            own = (z >> bit) & 1
            keep = lax.dynamic_index_in_dim(v, own, axis, keepdims=False)
            give = lax.dynamic_index_in_dim(v, 1 - own, axis, keepdims=False)
            got = permute(
                give.astype(BF), lambda a, b, c, bit=bit: (a, b ^ (1 << bit), c)
            )
            v = keep.astype(F32) + got.astype(F32)
            if bit < z_bits - 1:
                v = v.astype(BF)
        return v.astype(BF)

    def finish_columns(v):
        if n_x == 2:
            v = v.reshape((2, v.shape[0] // 2) + v.shape[1:])
            keep = lax.dynamic_index_in_dim(v, x, 0, keepdims=False)
            give = lax.dynamic_index_in_dim(v, 1 - x, 0, keepdims=False)
            got = permute(give, lambda a, b, c: (a, b, 1 - c))
            both = jnp.where(x == 0, jnp.stack([keep, got]), jnp.stack([got, keep]))
        else:
            both = v[None]
        every = lax.all_gather(both, "u", axis=0)
        return every.reshape((parts,) + both.shape[1:])

    def sum_all(v):
        total = n_u * n_z * n_x
        for i in range(total.bit_length() - 1):
            bit = 1 << i
            pairs = [(n, n ^ bit) for n in range(total)]
            v = v + lax.ppermute(v, AXES, pairs)
        return v

    entry_home = dot_nn(inputs, w_skip[:d]) + dot_nn(skip_in, w_skip[d:])
    entry = away(entry_home.astype(BF)).astype(F32)
    group_lengths = away(lengths)[0]
    grad_low = away(cotangent)
    inputs_away = away(inputs)
    skip_away = away(skip_in)

    segment, places = frame_segments(group_lengths, jnp.arange(group, dtype=jnp.int32))
    own_places = lax.dynamic_slice_in_dim(places, me * frames, frames)
    tables = rotary_tables(own_places)
    col, row = segment[:, None], segment[None, :]

    inverse_one = rms_parts(entry)
    normed_one = (entry * inverse_one * gain_one).astype(BF)
    qkv = dot_nn(normed_one, w_qkv)
    query = (rotate(qkv[:, :d], tables, 1.0)).astype(BF) * BF(HEAD_DIM**-0.5)
    keys = rotate(qkv[:, d : 2 * d], tables, 1.0).astype(BF)
    values = qkv[:, 2 * d :].astype(BF)

    def to_heads(*arrays):
        n = len(arrays)
        v = jnp.stack([a.reshape(frames, parts, width) for a in arrays], axis=2)
        v = lax.all_to_all(
            v.reshape(frames, parts * n * width), PLANE, split_axis=1, concat_axis=0, tiled=True
        )
        return [v[:, i * width : (i + 1) * width] for i in range(n)]

    def to_frames(*arrays):
        n = len(arrays)
        v = jnp.concatenate(arrays, axis=1)
        v = lax.all_to_all(v, PLANE, split_axis=0, concat_axis=1, tiled=True)
        v = v.reshape(frames, parts, n, width)
        return [v[:, :, i].reshape(frames, d) for i in range(n)]

    head_query, head_keys, head_values = to_heads(query, keys, values)
    head_mixed, lse = call_forward(head_query, head_keys, head_values, col, row)
    (mixed,) = to_frames(head_mixed)

    middle = entry + dot_nn(mixed, w_out)
    inverse_two = rms_parts(middle)
    normed_two = (middle * inverse_two * gain_two).astype(BF)
    up = dot_nn(normed_two, w_up) + b_up
    d_active = dot_nt(grad_low, w_down)
    active, slope = gelu_both(up)
    d_up = (d_active * slope).astype(BF)
    result_away = (middle + dot_nn(active.astype(BF), w_down) + b_down).astype(BF)
    result = home(result_away)
    d_normed_two = dot_nt(d_up, w_up)
    middle_part, g_gain_two = rms_back(middle, inverse_two, gain_two, d_normed_two)
    d_middle = grad_low.astype(F32) + middle_part
    d_branch = d_middle.astype(BF)
    d_mixed = dot_nt(d_branch, w_out).astype(BF)
    (head_grad,) = to_heads(d_mixed)
    dq, dk, dv = call_backward(
        head_query, head_keys, head_values, head_mixed, head_grad, col, row, lse
    )

    chunk = hidden // (n_z * parts)
    w_up_own = lax.dynamic_slice(
        w_up.reshape(d, n_z, n_x, n_u, chunk), (0, 0, x, u, 0), (d, n_z, 1, 1, chunk)
    ).reshape(d, n_z * chunk)
    w_down_own = lax.dynamic_slice(
        w_down.reshape(n_z, n_x, n_u, chunk, d), (0, x, u, 0, 0), (n_z, 1, 1, chunk, d)
    ).reshape(n_z * chunk, d)
    b_up_own = lax.dynamic_slice(
        b_up.reshape(n_z, n_x, n_u, chunk), (0, x, u, 0), (n_z, 1, 1, chunk)
    ).reshape(n_z * chunk)
    plane_grad = gather_plane(grad_low)
    plane_normed = gather_plane(normed_two)
    up_own = dot_nn(plane_normed, w_up_own) + b_up_own
    active_own, slope_own = gelu_both(up_own)
    d_up_own = (dot_nt(plane_grad, w_down_own) * slope_own).astype(BF)
    g_down = dot_tn(active_own.astype(BF), plane_grad)
    g_up = dot_tn(plane_normed, d_up_own)
    down_z = reduce_z(g_down.astype(BF))
    up_z = reduce_z(g_up.astype(BF))
    out_down = lax.all_gather(down_z, "u", axis=0, tiled=True).astype(F32)
    out_up = finish_columns(up_z)
    out_up = (
        out_up.reshape(n_u, n_x, -1, n_z, chunk).transpose(2, 3, 1, 0, 4).reshape(-1, hidden)
    ).astype(F32)

    plane_mixed = gather_plane(mixed)
    own_branch = gather_order(
        lax.all_to_all(d_branch, PLANE, split_axis=1, concat_axis=0, tiled=True)
    )
    g_out = dot_tn(plane_mixed, own_branch)
    out_out = (
        finish_columns(reduce_z(g_out.astype(BF))).transpose(1, 0, 2).reshape(-1, d).astype(F32)
    )

    low = [a.astype(BF) for a in (dq, dk, dv)]
    frame_query, frame_keys, frame_values = to_frames(*low)
    d_qkv = jnp.concatenate(
        [
            rotate(frame_query.astype(F32), tables, -1.0).astype(BF),
            rotate(frame_keys.astype(F32), tables, -1.0).astype(BF),
            frame_values,
        ],
        axis=1,
    )
    d_normed_one = dot_nt(d_qkv, w_qkv)
    entry_part, g_gain_one = rms_back(entry, inverse_one, gain_one, d_normed_one)
    d_entry = (d_middle + entry_part).astype(BF)
    d_entry_home = home(d_entry)
    d_joined = dot_nt(d_entry_home, w_skip)
    d_inputs = d_joined[:, :d].astype(BF)
    d_skip = d_joined[:, d:].astype(BF)

    group_tables = rotary_tables(places)
    head_d_qkv = jnp.concatenate(
        [
            rotate(low[0].astype(F32), group_tables, -1.0).astype(BF),
            rotate(low[1].astype(F32), group_tables, -1.0).astype(BF),
            low[2],
        ],
        axis=1,
    )
    plane_first = gather_plane(normed_one)
    g_qkv = dot_tn(plane_first, gather_order(head_d_qkv))
    plane_inputs = gather_plane(inputs_away)
    plane_skip = gather_plane(skip_away)
    own_entry = gather_order(
        lax.all_to_all(d_entry, PLANE, split_axis=1, concat_axis=0, tiled=True)
    )
    g_skip = jnp.concatenate([dot_tn(plane_inputs, own_entry), dot_tn(plane_skip, own_entry)])
    out_qkv = finish_columns(reduce_z(g_qkv.astype(BF)))
    out_qkv = (
        out_qkv.reshape(parts, -1, 3, width).transpose(1, 2, 0, 3).reshape(-1, 3 * d).astype(F32)
    )
    out_skip = (
        finish_columns(reduce_z(g_skip.astype(BF))).transpose(1, 0, 2).reshape(-1, d).astype(F32)
    )

    early = sum_all(
        jnp.concatenate(
            [
                g_gain_two,
                jnp.sum(d_up.astype(F32), axis=0),
                jnp.sum(cotangent.astype(F32), axis=0),
            ]
        )
    )
    total_gain_one = sum_all(g_gain_one)
    return (
        result,
        d_inputs,
        d_skip,
        out_skip,
        total_gain_one,
        out_qkv,
        out_out,
        early[:d],
        out_up,
        early[d : d + hidden],
        out_down,
        early[d + hidden :],
    )


def local_fast(
    sizes,
    inputs,
    skip_in,
    lengths,
    cotangent,
    w_skip,
    gain_one,
    w_qkv,
    w_out,
    gain_two,
    w_up,
    b_up,
    w_down,
    b_down,
):
    made = call_layer(
        (inputs, skip_in, cotangent, w_skip, w_qkv, w_out, w_up, w_down),
        lengths,
        (gain_one[None], gain_two[None], b_up[None], b_down[None]),
    )
    (
        result,
        d_inputs,
        d_skip,
        g_skip,
        g_qkv,
        g_out,
        g_up,
        g_down,
        total_one,
        total_two,
        total_up,
        total_down,
    ) = call_widen(made)
    return (
        result,
        d_inputs,
        d_skip,
        g_skip,
        total_one,
        g_qkv,
        g_out,
        total_two,
        g_up,
        total_up,
        g_down,
        total_down,
    )


def solution(mesh):
    n_u, n_s = mesh.shape["utt"], mesh.shape["seq"]
    sizes = (n_u, n_u, n_s // n_u)
    program = local_fast if sizes == (4, 4, 2) else local
    inner = Mesh(mesh.devices.reshape(sizes), AXES)
    rows, seq = P(AXES, None), P(("z", "x"), None)
    in_specs = (rows, rows, P("u", None), rows) + (P(),) * 9
    out_specs = (rows, rows, rows, seq, P(), seq, seq, P(), seq, P(), seq, P())
    return jax.shard_map(
        functools.partial(program, sizes),
        mesh=inner,
        in_specs=in_specs,
        out_specs=out_specs,
        check_vma=False,
    )
```

```python
import functools
import math

import jax
import jax.numpy as jnp
from jax import lax
from jax.experimental import pallas as pl
from jax.experimental.pallas import tpu as pltpu
from jax.sharding import Mesh, PartitionSpec as P

HEAD_DIM = 64
EPSILON = 1e-06
BF = jnp.bfloat16
F32 = jnp.float32
AXES = ("u", "z", "x")
PLANE = ("u", "x")


def dot_nn(a, b):
    return lax.dot_general(a, b, (((1,), (0,)), ((), ())), preferred_element_type=F32)


def dot_nt(a, b):
    return lax.dot_general(a, b, (((1,), (1,)), ((), ())), preferred_element_type=F32)


def dot_tn(a, b):
    return lax.dot_general(a, b, (((0,), (0,)), ((), ())), preferred_element_type=F32)


def attention_forward(q_ref, k_ref, v_ref, col_ref, row_ref, o_ref, lse_ref, acc, out_t):
    forward_heads(q_ref, k_ref, v_ref, col_ref, row_ref[...], o_ref, lse_ref, acc, out_t)


def forward_heads(q_ref, k_ref, v_ref, col_ref, segment_row, o_ref, lse_ref, acc, out_t):
    frames, width = q_ref.shape
    heads = width // HEAD_DIM
    block = frames // (frames // 352)
    lane = lax.broadcasted_iota(jnp.int32, (1, width), 1)
    for h in range(heads):
        own = (lane // HEAD_DIM == h).astype(BF)
        query = q_ref[...] * own
        acc[...] = jnp.zeros_like(acc)

        def step(j, carry):
            top, total = carry
            rows = pl.ds(pl.multiple_of(j * block, block), block)
            scores = dot_nt(k_ref[rows, :], query)
            scores = jnp.where(col_ref[rows, 0:1] == segment_row, scores, -1e30)
            peak = jnp.maximum(top, jnp.max(scores, axis=0, keepdims=True))
            expos = jnp.exp(scores - peak)
            shrink = jnp.exp(top - peak)
            acc[...] = acc[...] * shrink + dot_tn(v_ref[rows, :], expos.astype(BF))
            return peak, total * shrink + jnp.sum(expos, axis=0, keepdims=True)

        top, total = lax.fori_loop(
            0,
            frames // block,
            step,
            (jnp.full((1, frames), -1e30, F32), jnp.zeros((1, frames), F32)),
        )
        part = slice(h * HEAD_DIM, (h + 1) * HEAD_DIM)
        out_t[part, :] = acc[part, :] / total
        lse_ref[h : h + 1, :] = top + jnp.log(total)
    o_ref[...] = out_t[...].T.astype(BF)


def attention_backward(
    q_ref, k_ref, v_ref, o_ref, do_ref, col_ref, row_ref, lse_ref, dq_ref, dk_ref, dv_ref, acc
):
    backward_heads(
        q_ref, k_ref, v_ref, o_ref, do_ref, col_ref, row_ref[...], lse_ref, dq_ref, dk_ref, dv_ref, acc
    )


def backward_heads(
    q_ref, k_ref, v_ref, o_ref, do_ref, col_ref, segment_row, lse_ref, dq_ref, dk_ref, dv_ref, acc, between=None
):
    frames, width = q_ref.shape
    heads = width // HEAD_DIM
    block = frames // (frames // 352)
    lane = lax.broadcasted_iota(jnp.int32, (1, width), 1)
    product_t = (o_ref[...].astype(F32) * do_ref[...].astype(F32)).T
    for h in range(heads):
        own = (lane // HEAD_DIM == h).astype(BF)
        query = q_ref[...] * own
        grad = do_ref[...] * own
        part = slice(h * HEAD_DIM, (h + 1) * HEAD_DIM)
        delta = jnp.sum(product_t[part, :], axis=0, keepdims=True)
        log_total = lse_ref[h : h + 1, :]

        def step(j, _):
            rows = pl.ds(pl.multiple_of(j * block, block), block)
            keys = k_ref[rows, :]
            scores = dot_nt(keys, query)
            same = col_ref[rows, 0:1] == segment_row
            probs = jnp.where(same, jnp.exp(scores - log_total), 0.0)
            d_probs = dot_nt(v_ref[rows, :], grad)
            d_scores = (probs * (d_probs - delta)).astype(BF)
            value_part = dot_nn(probs.astype(BF), grad)
            key_part = dot_nn(d_scores, query)
            if h == 0:
                dv_ref[rows, :] = value_part
                dk_ref[rows, :] = key_part
            else:
                dv_ref[rows, :] += value_part
                dk_ref[rows, :] += key_part
            query_part = dot_tn(keys * own, d_scores)

            if h == 0:

                @pl.when(j == 0)
                def _():
                    acc[...] = query_part

                @pl.when(j > 0)
                def _():
                    acc[...] += query_part

            else:
                acc[...] += query_part
            return 0

        lax.fori_loop(0, frames // block, step, 0)
        if h == 0 and between is not None:
            between()
    dq_ref[...] = acc[...].T * (HEAD_DIM**-0.5)


def call_forward(query, keys, values, col, row):
    frames, width = query.shape
    return pl.pallas_call(
        attention_forward,
        out_shape=(
            jax.ShapeDtypeStruct((frames, width), BF),
            jax.ShapeDtypeStruct((width // HEAD_DIM, frames), F32),
        ),
        scratch_shapes=[pltpu.VMEM((width, frames), F32), pltpu.VMEM((width, frames), F32)],
        compiler_params=pltpu.CompilerParams(vmem_limit_bytes=56 * 2**20),
        cost_estimate=pl.CostEstimate(
            flops=16 * frames * frames * width, bytes_accessed=10 * frames * width, transcendentals=0
        ),
        name="attention_forward",
    )(query, keys, values, col, row)


def call_backward(query, keys, values, mixed, grad, col, row, lse):
    frames, width = query.shape
    shape = jax.ShapeDtypeStruct((frames, width), F32)
    return pl.pallas_call(
        attention_backward,
        out_shape=(shape, shape, shape),
        scratch_shapes=[pltpu.VMEM((width, frames), F32)],
        compiler_params=pltpu.CompilerParams(vmem_limit_bytes=56 * 2**20),
        cost_estimate=pl.CostEstimate(
            flops=32 * frames * frames * width, bytes_accessed=20 * frames * width, transcendentals=0
        ),
        name="attention_backward",
    )(query, keys, values, mixed, grad, col, row, lse)


def frame_segments(own_lengths, positions):
    slots = own_lengths.shape[0]
    upto = jnp.arange(slots)[:, None] >= jnp.arange(slots)[None, :]
    ends_at = jnp.sum(jnp.where(upto, own_lengths[None, :], 0), axis=1)
    starts_at = ends_at - own_lengths
    segment = jnp.sum((positions[:, None] >= ends_at[None, :]).astype(jnp.int32), axis=1)
    index = jnp.arange(slots, dtype=jnp.int32)
    offset = jnp.sum(jnp.where(segment[:, None] == index[None, :], starts_at[None, :], 0), axis=1)
    return segment, positions - offset


def rotary_tables(places):
    freqs = jnp.exp(
        jnp.arange(HEAD_DIM // 2, dtype=F32) * (-2.0 * math.log(10000.0) / HEAD_DIM)
    )
    angles = places.astype(F32)[:, None] * freqs[None, :]
    cosine, sine = jnp.cos(angles), jnp.sin(angles)
    return (
        jnp.concatenate([cosine, cosine], axis=1)[:, None, :],
        jnp.concatenate([-sine, sine], axis=1)[:, None, :],
    )


def rotate(v, tables, sign):
    frames, width = v.shape
    shaped = v.reshape(frames, width // HEAD_DIM, HEAD_DIM)
    half = HEAD_DIM // 2
    swapped = jnp.concatenate([shaped[..., half:], shaped[..., :half]], axis=-1)
    return (shaped * tables[0] + swapped * (sign * tables[1])).reshape(frames, width)


def rms_parts(hidden):
    return lax.rsqrt(jnp.mean(hidden * hidden, axis=-1, keepdims=True) + EPSILON)


def rms_back(hidden, inverse, gain, grad):
    scaled = hidden * inverse
    weighted = grad * gain
    inner = jnp.mean(weighted * scaled, axis=-1, keepdims=True)
    return inverse * (weighted - scaled * inner), jnp.sum(grad * scaled, axis=0)


def gelu_both(t):
    bell = 0.5 * (1.0 + lax.erf(t * 0.7071067811865476))
    return t * bell, bell + t * (0.3989422804014327 * jnp.exp(-0.5 * t * t))


TOK = 176
MESH_ID = pl.DeviceIdType.MESH


def flip_low(u):
    return u + 1 - 2 * lax.rem(u, 2)


def flip_high(u):
    return u + 2 - 4 * lax.div(u, 2)


def swap_bits(u):
    return 2 * lax.rem(u, 2) + lax.div(u, 2)


def both(a, b):
    return jnp.logical_and(a, b)


def gelu_pair(t):
    bell = jnp.exp(-0.5 * (t * t))
    s = 1.0 / (1.0 + jnp.abs(t) * (0.3275911 * 0.7071067811865476))
    tail = 0.5 * 1.061405429 * s - 0.5 * 1.453152027
    tail = tail * s + 0.5 * 1.421413741
    tail = tail * s - 0.5 * 0.284496736
    tail = (tail * s + 0.5 * 0.254829592) * s * bell
    below = jnp.where(t < 0.0, tail, 1.0 - tail)
    return t * below, below + t * (0.3989422804014327 * bell)


def rms_back_rows(hidden, inverse, gain, grad):
    scaled = hidden * inverse
    weighted = grad * gain
    inner = jnp.mean(weighted * scaled, axis=-1, keepdims=True)
    return inverse * (weighted - scaled * inner), jnp.sum(grad * scaled, axis=0, keepdims=True)


class Sender:
    def __init__(self, send, recv, load):
        self.send, self.recv, self.load = send, recv, load
        self.n = self.m = 0
        self.sent, self.kept = [], []

    def remote(self, src, dst, device, arrival=None):
        copy = pltpu.make_async_remote_copy(
            src_ref=src,
            dst_ref=dst,
            send_sem=self.send.at[self.n],
            recv_sem=self.recv.at[self.n] if arrival is None else arrival,
            device_id=device,
            device_id_type=MESH_ID,
        )
        self.n += 1
        return copy

    def push(self, src, dst, device):
        copy = self.remote(src, dst, device)
        copy.start()
        self.sent.append(copy)
        return copy

    def push_or_keep(self, src, dst, device, own, arrival=None):
        arrival = self.recv.at[self.n] if arrival is None else arrival
        inside = pltpu.make_async_copy(src, dst, arrival)
        copy = self.remote(src, dst, device, arrival)

        @pl.when(own)
        def _():
            inside.start()

        @pl.when(jnp.logical_not(own))
        def _():
            copy.start()

        self.kept.append((copy, own))
        return copy

    def local(self, src, dst):
        copy = pltpu.make_async_copy(src, dst, self.load.at[self.m])
        self.m += 1
        copy.start()
        return copy

    def finish(self):
        for copy in self.sent:
            copy.wait_send()
        settle(self.kept)
        self.sent, self.kept = [], []

    def take(self, n):
        taken, self.kept = self.kept[-n:], self.kept[:-n]
        return taken


def settle(kept):
    for copy, own in kept:

        @pl.when(jnp.logical_not(own))
        def _(copy=copy):
            copy.wait_send()


def plane_peers(u, z, x):
    peers = []
    for k in range(8):
        a = flip_low(u) if k & 2 else u
        a = flip_high(a) if k & 4 else a
        b = 1 - x if k & 1 else x
        peers.append(((a, z, b), 2 * a + b))
    return peers


def rows_of(p, start=0, size=TOK):
    return pl.ds(pl.multiple_of(p * TOK + start, 16), size)


class PlaneGather:
    def __init__(self, sender, buffer, peers, start=0, size=TOK):
        self.sender, self.buffer, self.peers = sender, buffer, peers
        self.first, self.size = start, size
        self.low = size // 32 * 16
        self.x, self.y = self.copy(0, 1), self.copy(0, 4)
        self.over_y = self.copy(1, 4, self.low, size - self.low)
        self.over_x = self.copy(4, 1, 0, self.low)
        self.cores = [self.copy(k, 2) for k in (0, 1, 4, 5)]
        self.copies = [self.x, self.y, self.over_x, self.over_y] + self.cores

    def copy(self, k, to, start=0, size=None):
        rows = rows_of(self.peers[k][1], self.first + start, size or self.size)
        return self.sender.remote(self.buffer.at[rows], self.buffer.at[rows], self.peers[to][0])

    def start(self):
        self.x.start()
        self.y.start()
        self.cores[0].start()

    def forward(self):
        self.x.wait_recv()
        self.over_y.start()
        self.cores[1].start()
        self.y.wait_recv()
        self.over_x.start()
        self.cores[2].start()

    def corner(self):
        self.over_x.wait_recv()
        self.over_y.wait_recv()
        self.cores[3].start()

    def core(self, i):
        self.cores[i].wait_recv()

    def left(self):
        for copy in self.copies:
            copy.wait_send()

    def done(self):
        for copy in self.cores:
            copy.wait_recv()
        self.left()


class PlaneSum:
    def __init__(self, sender, terms, first, second, third, place):
        self.sender, self.terms = sender, terms
        self.first, self.second, self.third = first, second, third
        u, z, x = place
        self.low, self.high = lax.rem(z, 2), lax.div(z, 2)
        self.near, self.far = (u, flip_low(z), x), (u, flip_high(z), x)
        self.rows = third.shape[0]
        self.waits = [
            sender.remote(terms.at[self.chunk(j, 1 - self.low)], first.at[j], self.near)
            for j in range(2)
        ]
        sender.sent += self.waits

    def chunk(self, j, low):
        return pl.ds(pl.multiple_of((2 * j + low) * self.rows, self.rows), self.rows)

    def start(self):
        for copy in self.waits:
            copy.start()

    def middle(self):
        for copy in self.waits:
            copy.wait_recv()
        for j in range(2):
            own = self.terms[self.chunk(j, self.low), :].astype(F32)
            self.second[j] = (own + self.first[j].astype(F32)).astype(BF)
        self.wait = self.sender.push(self.second.at[1 - self.high], self.third, self.far)

    def end(self, out):
        self.wait.wait_recv()
        out[...] = (self.second[self.high].astype(F32) + self.third[...].astype(F32)).astype(BF)


class ColumnGather:
    def __init__(self, sender, source, out, peers, x):
        self.sender, self.out, self.peers = sender, out, peers
        rows = out.shape[1]
        me = peers[0][1]

        def part(b):
            return pl.ds(pl.multiple_of(b * rows, rows), rows)

        self.direct = [
            (k, sender.push(source.at[part(peers[k][0][2])], out.at[me], peers[k][0]))
            for k in (5, 4, 1)
        ]
        self.cores = [sender.push(source.at[part(x)], out.at[me], peers[2][0])]
        out[me] = source[part(x), :]

    def forward(self):
        for k, copy in self.direct:
            copy.wait_recv()
            slot = self.out.at[self.peers[k][1]]
            self.cores.append(self.sender.push(slot, slot, self.peers[2][0]))

    def done(self):
        for copy in self.cores:
            copy.wait_recv()


class RowGather:
    def __init__(self, sender, source, out, peers, u):
        self.sender, self.out, self.peers = sender, out, peers
        self.rows = source.shape[0]
        self.far = sender.push(source, out.at[self.part(u)], peers[4][0])
        self.cores = [sender.push(source, out.at[self.part(u)], peers[2][0])]
        out[self.part(u), :] = source[...]

    def part(self, u):
        return pl.ds(pl.multiple_of(u * self.rows, self.rows), self.rows)

    def forward(self):
        self.far.wait_recv()
        block = self.out.at[self.part(self.peers[4][0][0])]
        self.cores.append(self.sender.push(block, block, self.peers[2][0]))

    def done(self):
        for copy in self.cores:
            copy.wait_recv()


def layer_kernel(
    lengths_ref,
    gain_one_ref,
    gain_two_ref,
    b_up_ref,
    b_down_ref,
    inputs_ref,
    skip_ref,
    cot_ref,
    w_skip_ref,
    w_qkv_ref,
    w_out_ref,
    w_up_ref,
    w_down_ref,
    result_out,
    inputs_out,
    skip_out,
    g_skip_out,
    g_qkv_out,
    g_out_out,
    g_up_out,
    g_down_out,
    vector_out,
    normed_kept,
    wide_a,
    wide_b,
    w_out,
    n2,
    ct,
    db,
    joined,
    q,
    k,
    v,
    o,
    grad,
    lse,
    cos_t,
    sin_t,
    seg,
    entry,
    middle,
    dq,
    dk,
    result,
    result_r,
    d_mixed,
    d_heads,
    d_frames,
    entry_r,
    gd,
    gu,
    gq,
    gs,
    go,
    d_up,
    d1,
    d2,
    d3,
    dz,
    u1,
    u2,
    u3,
    uz,
    q1,
    q2,
    q3,
    qz,
    s1,
    s2,
    s3,
    sz,
    o1,
    o2,
    fin_d,
    fin_u,
    fin_q,
    fin_s,
    fin_o,
    vec,
    vec_plane,
    vec_sum,
    vec_z,
    acc,
    lens,
    lens_r,
    send,
    recv,
    load,
    spread,
):
    u, z, x = (lax.axis_index(a) for a in AXES)
    me = 2 * u + x
    peers = plane_peers(u, z, x)
    place = (u, z, x)
    d = entry.shape[1]
    group = n2.shape[0]
    hidden = wide_a.shape[1]
    heads_at = pl.ds(pl.multiple_of(me * 128, 128), 128)
    plane = swap_bits(u)
    away = (z, plane, x)
    stays_away = both(u == z, plane == z)
    own_home = swap_bits(z)
    home = (own_home, u, x)
    stays_home = both(own_home == u, u == z)
    sender = Sender(send, recv, load)
    mine = rows_of(me)
    low, high = 80, 96
    z_devices = (
        (u, flip_low(z), x),
        (u, flip_high(z), x),
        (u, flip_low(flip_high(z)), x),
    )

    barrier = pltpu.get_barrier_semaphore()

    def greet(device):
        pl.semaphore_signal(barrier, inc=1, device_id=device, device_id_type=MESH_ID)

    for device, _ in peers[1:]:
        greet(device)
    for device in z_devices:
        greet(device)

    @pl.when(jnp.logical_not(stays_away))
    def _():
        greet(away)
        greet(home)

    got_x = sender.local(inputs_ref, gd.at[pl.ds(0, TOK)])
    got_s = sender.local(skip_ref, gd.at[pl.ds(TOK, TOK)])
    got_w = [
        sender.local(w_skip_ref.at[pl.ds(i * d, d)], wide_b.at[pl.ds(i * d, d)]) for i in range(2)
    ]
    got_q = [
        sender.local(
            w_qkv_ref.at[:, pl.ds(pl.multiple_of(c * d + me * 128, 128), 128)],
            wide_a.at[:, pl.ds(c * 128, 128)],
        )
        for c in range(3)
    ]
    slots = lengths_ref.shape[1]
    for s in range(slots):
        lens[s : s + 1, :] = jnp.full((1, 128), lengths_ref[0, s].astype(F32), F32)
    lens[slots:8, :] = jnp.zeros((8 - slots, 128), F32)
    got_x.wait()
    got_w[0].wait()
    value = dot_nn(gd[:TOK, :], wide_b[:d, :])
    got_s.wait()
    got_w[1].wait()
    d_mixed[...] = (value + dot_nn(gd[TOK : 2 * TOK, :], wide_b[d : 2 * d, :])).astype(BF)
    pl.semaphore_wait(barrier, jnp.where(stays_away, 10, 12))
    sent_entry = [
        sender.push_or_keep(
            d_mixed.at[pl.ds(a, n)], entry.at[pl.ds(a, n)], away, stays_away
        )
        for a, n in ((0, low), (low, high))
    ]
    entry_left = sender.take(2)
    sent_lens = sender.push_or_keep(lens, lens_r, away, stays_away)
    got_down = sender.local(w_down_ref, wide_b)
    got_out = sender.local(w_out_ref, w_out)

    lane = lax.broadcasted_iota(jnp.int32, (TOK, 128), 1)
    for a in range(4):
        for b in range(2):
            for pair in range(2):
                halves = []
                for s in range(2):
                    block = 4 * (2 * pair + s) + 2 * b + a // 2
                    top = block // (d // 128) * TOK
                    first = block % (d // 128) * 128
                    piece = gd[top : top + TOK, first : first + 128].astype(F32)
                    if a % 2 != s:
                        piece = pltpu.roll(piece, 64, 1)
                    halves.append(piece)
                j = 2 * a + b
                gu[
                    j // 2 * TOK : (j // 2 + 1) * TOK,
                    j % 2 * 256 + pair * 128 : j % 2 * 256 + (pair + 1) * 128,
                ] = jnp.where(lane < 64, halves[0], halves[1]).astype(BF)

    def joined_for(a, b):
        return gu.at[
            pl.ds(pl.multiple_of(a * TOK, 16), TOK), pl.ds(pl.multiple_of(b * 256, 256), 256)
        ]

    def joined_from(a, b):
        first = lax.rem(a, 2) * 512 + b * 256
        return fin_d.at[
            pl.ds(pl.multiple_of(lax.div(a, 2) * TOK, 16), TOK),
            pl.ds(pl.multiple_of(first, 256), 256),
        ]

    own_joined = sender.local(joined_for(u, x), joined_from(u, x))
    got_joined = []
    for device, _ in peers[1:]:
        copy = sender.remote(joined_for(device[0], device[2]), joined_from(u, x), device)
        copy.start()
        got_joined.append(copy)

    sent_lens.wait_recv()
    freqs = jnp.exp(lax.rem(lane, 32).astype(F32) * (-2.0 * math.log(10000.0) / HEAD_DIM))
    front = lax.rem(lane, 64) < 32
    sign = jnp.where(front, -1.0, 1.0)

    def table(i, _):
        rows = rows_of(i)
        at = (lax.broadcasted_iota(jnp.int32, (TOK, 128), 0) + i * TOK).astype(F32)
        spot, segment, end = at, jnp.zeros_like(at), jnp.zeros((1, 128), F32)
        for s in range(slots):
            length = lens_r[s : s + 1, :]
            end = end + length
            past = at >= end
            segment = segment + jnp.where(past, 1.0, 0.0)
            spot = spot - jnp.where(past, length, 0.0)
        angle = spot * freqs
        cos_t[rows, :] = jnp.cos(angle)
        sin_t[rows, :] = jnp.sin(angle) * sign
        seg[rows, :] = segment
        return 0

    lax.fori_loop(0, group // TOK, table, 0)
    at = lax.broadcasted_iota(jnp.int32, (1, group), 1).astype(F32)
    segment_row, end = jnp.zeros((1, group), F32), jnp.zeros((1, 1), F32)
    for s in range(slots):
        end = end + lens_r[s : s + 1, 0:1]
        segment_row = segment_row + jnp.where(at >= end, 1.0, 0.0)
    lse[2:3, :] = segment_row
    for copy in got_q:
        copy.wait()

    def turn(t, rows, way):
        swapped = jnp.where(front, pltpu.roll(t, 96, 1), pltpu.roll(t, 32, 1))
        return t * cos_t[rows, :] + swapped * (way * sin_t[rows, :])

    def project(i):
        first = peers[i][0][0] * (2 * TOK)
        rows = pl.ds(pl.multiple_of(first, 16), 2 * TOK)
        value = dot_nn(n2[rows, :], wide_a[:, :384])
        for h in range(2):
            rows = pl.ds(pl.multiple_of(first + h * TOK, 16), TOK)
            part = value[h * TOK : (h + 1) * TOK]
            q[rows, :] = (
                turn(part[:, :128], rows, 1.0).astype(BF).astype(F32) * HEAD_DIM**-0.5
            ).astype(BF)
            k[rows, :] = turn(part[:, 128:256], rows, 1.0).astype(BF)
            v[rows, :] = part[:, 256:].astype(BF)

    first_a = PlaneGather(sender, n2, peers, 0, low)
    first_b = PlaneGather(sender, n2, peers, low, high)
    for copy, gather, (a, n) in zip(sent_entry, (first_a, first_b), ((0, low), (low, high))):
        copy.wait_recv()
        value = entry[a : a + n, :].astype(F32)
        n2[rows_of(me, a, n), :] = (value * rms_parts(value) * gain_one_ref[...]).astype(BF)
        gather.start()
    sent_cot = sender.push_or_keep(cot_ref, ct.at[rows_of(2 * z + x)], away, stays_away)
    first_a.forward()
    first_b.forward()
    project(0)
    for gather in (first_a, first_b):
        gather.core(0)
        gather.core(1)
    project(2)
    first_a.corner()
    first_b.corner()
    project(4)
    for gather in (first_a, first_b):
        gather.core(2)
        gather.core(3)
    project(6)
    got_up = sender.local(w_up_ref, wide_a)
    kept_normed = sender.local(n2, normed_kept)
    sent_cot.wait_recv()
    gather_cot = PlaneGather(sender, ct, peers)
    gather_cot.start()
    own_joined.wait()
    for copy in got_joined:
        copy.wait_recv()
    for a in range(4):
        to = a % 2 * 2 + a // 2
        for b in range(2):
            sender.push_or_keep(
                joined_from(jnp.int32(a), jnp.int32(b)),
                joined.at[rows_of(2 * z + b)],
                (u, jnp.int32(to), x),
                z == to,
                spread.at[2 * z + b],
            )
    joined_left = sender.take(8)

    pl.run_scoped(
        lambda out_t: forward_heads(q, k, v, seg, segment_row, o, lse, acc, out_t),
        pltpu.VMEM((128, group), F32),
    )
    kept_normed.wait()
    for gather in (first_a, first_b):
        gather.left()
    own_mixed = sender.local(o.at[mine], d_frames.at[0, :, heads_at])
    got_mixed = [
        sender.push(o.at[rows_of(peers[i][1])], d_frames.at[0, :, heads_at], peers[i][0])
        for i in range(1, 8)
    ]
    gather_cot.forward()
    got_down.wait()
    step = d

    def back_feed(c, _):
        cols = pl.ds(pl.multiple_of(c * step, step), step)
        db[rows_of(c), :] = dot_nt(ct[mine, :], wide_b[cols, :]).astype(BF)
        return 0

    lax.fori_loop(0, hidden // step, back_feed, 0)
    own_mixed.wait()
    for copy in got_mixed:
        copy.wait_recv()

    got_out.wait()
    value = entry[...].astype(F32) + dot_nn(d_frames[0], w_out[...])
    middle[...] = value
    n2[mine, :] = (value * rms_parts(value) * gain_two_ref[...]).astype(BF)
    normed_a = PlaneGather(sender, n2, peers, 0, low)
    normed_b = PlaneGather(sender, n2, peers, low, high)
    normed_a.start()
    normed_b.start()

    dq[...] = jnp.zeros_like(dq)
    dk[...] = jnp.zeros_like(dk)

    def add_to(ref, value):
        for j in range(d // 128):
            ref[j * TOK : (j + 1) * TOK, :] += value[:, j * 128 : (j + 1) * 128]

    def side_by_side(ref):
        return jnp.concatenate([ref[j * TOK : (j + 1) * TOK, :] for j in range(d // 128)], axis=1)

    got_up.wait()

    def feed(c, _):
        cols = pl.ds(pl.multiple_of(c * step, step), step)
        up = dot_nn(n2[mine, :], wide_a[:, cols]) + b_up_ref[:, cols]
        active, slope = gelu_pair(up)
        d_up = (db[rows_of(c), :].astype(F32) * slope).astype(BF)
        add_to(dq, dot_nn(active.astype(BF), wide_b[cols, :]))
        add_to(dk, dot_nt(d_up, wide_a[:, cols]))
        sums = jnp.sum(d_up.astype(F32), axis=0, keepdims=True)
        vec[pl.ds(8 + 2 * c, 1), :] = sums[:, : step // 2]
        vec[pl.ds(9 + 2 * c, 1), :] = sums[:, step // 2 :]
        return 0

    half = hidden // step // 2
    lax.fori_loop(0, half, feed, 0)
    gather_cot.corner()
    lax.fori_loop(half, 2 * half, feed, 0)
    normed_a.forward()
    normed_b.forward()
    value = middle[...]
    inverse = rms_parts(value)
    back, g_gain_two = rms_back_rows(value, inverse, gain_two_ref[...], side_by_side(dk))
    grad_out = ct[mine, :].astype(F32)
    d_middle = grad_out + back
    result[...] = (value + side_by_side(dq) + b_down_ref[...]).astype(BF)
    middle[...] = d_middle
    db[mine, :] = d_middle.astype(BF)
    settle(entry_left)
    d_mixed[...] = dot_nt(db[mine, :], w_out[...]).astype(BF)
    own_grad = sender.local(d_mixed.at[:, heads_at], grad.at[mine])
    got_grad = [
        sender.push(
            d_mixed.at[:, pl.ds(pl.multiple_of(peers[i][1] * 128, 128), 128)],
            grad.at[mine],
            peers[i][0],
        )
        for i in range(1, 8)
    ]
    g_b_down = jnp.sum(grad_out, axis=0, keepdims=True)
    for i in range(2):
        part = slice(i * d // 2, (i + 1) * d // 2)
        vec[2 + i : 3 + i, :] = g_gain_two[:, part]
        vec[4 + i : 5 + i, :] = g_b_down[:, part]
    vec[6:8, :] = jnp.zeros((2, d // 2), F32)
    gather_cot.done()

    chunk = hidden // 32
    sum_down = PlaneSum(sender, gd, d1, d2, d3, place)
    sum_up = PlaneSum(sender, gu, u1, u2, u3, place)
    gather_branch = PlaneGather(sender, db, peers)

    def own_units(w_up_own, w_down_own, active):
        starts = [
            pl.multiple_of((2 * s + x) * (4 * chunk) + u * chunk, chunk) for s in range(4)
        ]
        for s, first in enumerate(starts):
            part = slice(s * chunk, (s + 1) * chunk)
            w_up_own[:, part] = wide_a[:, pl.ds(first, chunk)]
            w_down_own[part, :] = wide_b[pl.ds(first, chunk), :]
        bias = jnp.concatenate([b_up_ref[:, pl.ds(first, chunk)] for first in starts], axis=1)

        def units(i):
            rows = pl.ds(pl.multiple_of(peers[i][0][0] * (2 * TOK), 16), 2 * TOK)
            up = dot_nn(n2[rows, :], w_up_own[...]) + bias
            act, slope = gelu_pair(up)
            active[rows, :] = act.astype(BF)
            d_up[rows, :] = (dot_nt(ct[rows, :], w_down_own[...]) * slope).astype(BF)

        units(0)
        normed_a.corner()
        normed_b.corner()
        normed_a.core(0)
        normed_b.core(0)
        normed_a.core(1)
        normed_b.core(1)
        units(2)
        units(4)
        normed_a.core(2)
        normed_b.core(2)
        normed_a.core(3)
        normed_b.core(3)
        units(6)
        normed_a.left()
        normed_b.left()
        gather_branch.start()

        def down_terms(i, _):
            cols = pl.ds(pl.multiple_of(i * 256, 256), 256)
            gd[cols, :] = dot_tn(active[:, cols], ct[...]).astype(BF)
            return 0

        lax.fori_loop(0, 4 * chunk // 256, down_terms, 0)
        sum_down.start()

    pl.run_scoped(
        own_units,
        pltpu.VMEM((d, 4 * chunk), BF),
        pltpu.VMEM((4 * chunk, d), BF),
        pltpu.VMEM((group, 4 * chunk), BF),
    )
    got_normed = sender.local(normed_kept, ct)
    got_qkv = sender.local(w_qkv_ref, wide_a.at[:, pl.ds(0, 3 * d)])
    got_skip = sender.local(w_skip_ref, wide_b.at[pl.ds(0, 2 * d)])
    own_grad.wait()
    for copy in got_grad:
        copy.wait_recv()
    sent_result = sender.push_or_keep(result, result_r, home, stays_home)

    def heads(dv):
        backward_heads(q, k, v, o, grad, seg, lse[2:3, :], lse, dq, dk, dv, acc, gather_branch.forward)

        def turn_back(i, _):
            rows = rows_of(i)
            for c, ref in ((0, dq), (1, dk)):
                t = ref[rows, :].astype(BF).astype(F32)
                d_heads[c, rows, :] = turn(t, rows, -1.0).astype(BF)
            d_heads[2, rows, :] = dv[rows, :].astype(BF)
            return 0

        lax.fori_loop(0, group // TOK, turn_back, 0)

    pl.run_scoped(heads, pltpu.VMEM((group, 128), F32))
    settle(joined_left)
    for copy in got_joined:
        copy.wait_send()
    own_frames = sender.local(d_heads.at[:, mine], d_frames.at[:, :, heads_at])
    got_frames = [
        sender.push(
            d_heads.at[:, rows_of(peers[i][1])], d_frames.at[:, :, heads_at], peers[i][0]
        )
        for i in range(1, 8)
    ]
    gather_branch.corner()

    def up_terms(i, _):
        cols = pl.ds(pl.multiple_of(i * 256, 256), 256)
        gu[cols, :] = dot_tn(n2[:, cols], d_up[...]).astype(BF)
        return 0

    lax.fori_loop(0, d // 256, up_terms, 0)
    sum_up.start()
    got_normed.wait()

    def qkv_terms(i, _):
        cols = pl.ds(pl.multiple_of(i * 256, 256), 256)
        turned = ct[:, cols].T
        for c in range(3):
            gq[cols, c * 128 : (c + 1) * 128] = dot_nn(turned, d_heads[c]).astype(BF)
        return 0

    lax.fori_loop(0, d // 256, qkv_terms, 0)
    sum_qkv = PlaneSum(sender, gq, q1, q2, q3, place)
    sum_qkv.start()
    gather_branch.done()
    go[...] = dot_tn(o[...], db[...]).astype(BF)

    same_high = lax.div(z, 2) == lax.div(u, 2)
    same_low = lax.rem(z, 2) == lax.rem(u, 2)
    owner = z == u
    to_far = sender.remote(go, o1, (u, flip_high(z), x))
    to_near = sender.remote(go, o2, (u, flip_low(z), x))

    @pl.when(jnp.logical_not(same_low))
    def _():
        to_near.start()

    sum_down.middle()

    own_frames.wait()
    for copy in got_frames:
        copy.wait_recv()
    got_qkv.wait()
    d_normed = dot_nt(d_frames[0], wide_a[:, :d])
    d_normed += dot_nt(d_frames[1], wide_a[:, d : 2 * d])
    d_normed += dot_nt(d_frames[2], wide_a[:, 2 * d : 3 * d])
    value = entry[...].astype(F32)
    back, g_gain_one = rms_back_rows(value, rms_parts(value), gain_one_ref[...], d_normed)
    wide_b[rows_of(me, 2 * d), :] = (middle[...] + back).astype(BF)
    entry_a = PlaneGather(sender, wide_b, peers, 2 * d, low)
    entry_b = PlaneGather(sender, wide_b, peers, 2 * d + low, high)
    entry_a.start()
    entry_b.start()

    for i in range(2):
        vec[i : i + 1, :] = g_gain_one[:, i * d // 2 : (i + 1) * d // 2]
    vec_at = pl.ds(pl.multiple_of(me * 16, 16), 16)
    got_vec = [sender.push(vec, vec_plane.at[vec_at], peers[i][0]) for i in range(1, 8)]
    vec_plane[vec_at, :] = vec[...]

    sum_up.middle()
    for s in range(8):
        rows = pl.ds(s * TOK, TOK)
        pltpu.make_async_copy(joined.at[rows], joined.at[rows], spread.at[s]).wait()
    def skip_terms(i):
        p = peers[i][1]
        return dot_tn(joined[rows_of(p), :], wide_b[rows_of(p, 2 * d), :])

    total = skip_terms(0)

    entry_a.forward()
    entry_b.forward()
    sum_qkv.middle()
    total += skip_terms(1)
    total += skip_terms(4)
    entry_a.corner()
    entry_b.corner()
    total += skip_terms(5)
    for copy in entry_a.cores + entry_b.cores:
        copy.wait_recv()
    for i in (2, 3, 6, 7):
        total += skip_terms(i)
    gs[...] = total.astype(BF)
    sum_skip = PlaneSum(sender, gs, s1, s2, s3, place)
    sum_skip.start()

    sent_back = sender.push_or_keep(
        wide_b.at[rows_of(me, 2 * d)], entry_r, home, stays_home
    )
    @pl.when(same_low)
    def _():
        to_near.wait_recv()
        go[...] = (go[...].astype(F32) + o2[...].astype(F32)).astype(BF)

    @pl.when(both(same_low, jnp.logical_not(same_high)))
    def _():
        to_far.start()

    for copy in got_vec:
        copy.wait_recv()
    value = vec_plane[0:16, :]
    for i in range(1, 8):
        value += vec_plane[16 * i : 16 * (i + 1), :]
    vec_sum[...] = value
    vec_at = pl.ds(pl.multiple_of(z * 16, 16), 16)
    got_vec = [sender.push(vec_sum, vec_z.at[vec_at], device) for device in z_devices]
    vec_z[vec_at, :] = vec_sum[...]

    sum_up.end(uz)
    last_up = ColumnGather(sender, uz, fin_u, peers, x)
    sum_down.end(dz)
    last_down = RowGather(sender, dz, fin_d, peers, u)

    sum_skip.middle()

    outs = []
    sent_back.wait_recv()
    got_skip.wait()
    for i, out in enumerate((inputs_out, skip_out)):
        d_frames[i] = dot_nt(entry_r[...], wide_b[i * d : (i + 1) * d, :]).astype(BF)
        outs.append(sender.local(d_frames.at[i], out))
    sum_qkv.end(qz)
    last_qkv = ColumnGather(sender, qz, fin_q, peers, x)

    @pl.when(owner)
    def _():
        to_far.wait_recv()
        fin_o[...] = (go[...].astype(F32) + o1[...].astype(F32)).astype(BF)

    def tell(i, to):
        return pltpu.make_async_remote_copy(
            src_ref=fin_o,
            dst_ref=fin_o,
            send_sem=spread.at[8 + i],
            recv_sem=spread.at[11],
            device_id=peers[to][0],
            device_id_type=MESH_ID,
        )

    tell_core, tell_far, tell_on = tell(0, 2), tell(1, 4), tell(2, 2)

    @pl.when(owner)
    def _():
        tell_far.start()
        tell_core.start()

    last_up.forward()
    last_down.forward()
    sum_skip.end(sz)
    last_skip = RowGather(sender, sz, fin_s, peers, u)
    last_qkv.forward()
    across = u == flip_high(z)

    @pl.when(jnp.logical_not(owner))
    def _():
        tell_core.wait_recv()

    @pl.when(across)
    def _():
        tell_on.start()

    last_up.done()
    for p in range(8):
        for s in range(4):
            first = (2 * s + p % 2) * 4 * chunk + p // 2 * chunk
            outs.append(
                sender.local(
                    fin_u.at[p, :, pl.ds(s * chunk, chunk)], g_up_out.at[:, pl.ds(first, chunk)]
                )
            )
    last_down.done()
    outs.append(sender.local(fin_d, g_down_out))
    for copy in got_vec:
        copy.wait_recv()
    vec_sum_out = vec_z[0:16, :] + vec_z[16:32, :] + vec_z[32:48, :] + vec_z[48:64, :]
    vec_plane[0:16, :] = vec_sum_out
    outs.append(sender.local(vec_plane.at[pl.ds(0, 16)], vector_out))
    sent_result.wait_recv()
    outs.append(sender.local(result_r, result_out))
    outs.append(sender.local(fin_o, g_out_out))
    last_skip.forward()
    last_qkv.done()
    for p in range(8):
        for c in range(3):
            outs.append(
                sender.local(
                    fin_q.at[p, :, pl.ds(c * 128, 128)],
                    g_qkv_out.at[:, pl.ds(c * d + p * 128, 128)],
                )
            )

    @pl.when(owner)
    def _():
        tell_far.wait_send()
        tell_core.wait_send()

    @pl.when(across)
    def _():
        tell_on.wait_send()

    @pl.when(jnp.logical_not(same_low))
    def _():
        to_near.wait_send()

    @pl.when(both(same_low, jnp.logical_not(same_high)))
    def _():
        to_far.wait_send()

    last_skip.done()
    outs.append(sender.local(fin_s, g_skip_out))
    for copy in outs:
        copy.wait()
    entry_a.left()
    entry_b.left()
    sender.finish()


def call_layer(arrays, lengths, vectors):
    d = arrays[0].shape[1]
    hidden = arrays[6].shape[1]
    group = 8 * TOK
    any_space = pl.BlockSpec(memory_space=pl.ANY)
    vmem = pl.BlockSpec(memory_space=pltpu.VMEM)
    smem = pl.BlockSpec(memory_space=pltpu.SMEM)
    block, wide = ((TOK, d), BF), ((group, d), BF)
    head, table, total = ((group, 128), BF), ((group, 128), F32), ((TOK, d), F32)
    unit = hidden // 8

    def sums(rows, columns):
        return [
            ((2, rows, columns), BF),
            ((2, rows, columns), BF),
            ((rows, columns), BF),
            ((rows, columns), BF),
        ]

    outs = [
        block,
        block,
        block,
        ((2 * d // 8, d), BF),
        ((d // 8, 3 * d), BF),
        ((d // 8, d), BF),
        ((d // 8, hidden), BF),
        ((unit, d), BF),
        ((16, 512), F32),
        wide,
    ]
    scratch = [
        ((d, hidden), BF),
        ((hidden, d), BF),
        ((d, d), BF),
        wide,
        wide,
        wide,
        ((group, 256), BF),
        head,
        head,
        head,
        head,
        head,
        ((8, group), F32),
        table,
        table,
        table,
        block,
        total,
        table,
        table,
        block,
        block,
        block,
        ((3, group, 128), BF),
        ((3, TOK, d), BF),
        block,
        ((unit, d), BF),
        ((d, unit), BF),
        ((d, 384), BF),
        ((256, d), BF),
        ((128, d), BF),
        ((group, unit), BF),
        *sums(unit // 4, d),
        *sums(d // 4, unit),
        *sums(d // 4, 384),
        *sums(64, d),
        ((128, d), BF),
        ((128, d), BF),
        ((unit, d), BF),
        ((8, d // 8, unit), BF),
        ((8, d // 8, 384), BF),
        ((256, d), BF),
        ((128, d), BF),
        ((16, 512), F32),
        ((128, 512), F32),
        ((16, 512), F32),
        ((64, 512), F32),
        ((128, group), F32),
        ((8, 128), F32),
        ((8, 128), F32),
    ]
    made = pl.pallas_call(
        layer_kernel,
        in_specs=[smem] + [vmem] * len(vectors) + [any_space] * len(arrays),
        out_specs=[any_space] * len(outs),
        out_shape=[jax.ShapeDtypeStruct(*o) for o in outs],
        scratch_shapes=[pltpu.VMEM(*s) for s in scratch]
        + [pltpu.SemaphoreType.DMA((160,))] * 3
        + [pltpu.SemaphoreType.DMA((12,))],
        compiler_params=pltpu.CompilerParams(
            vmem_limit_bytes=60 * 2**20 + 2**18, has_side_effects=True, collective_id=0
        ),
        name="layer",
    )(lengths, *vectors, *arrays)
    return made[:9]


def widen_kernel(*refs):
    n = 9
    ins, outs = refs[:n], refs[n:]
    for i in range(8):
        outs[i][...] = ins[i][...].astype(outs[i].dtype)
    vectors = ins[8]
    for out, row in zip(outs[8:], (0, 2, 4, 8)):
        for part in range(out.shape[1] // 512):
            out[:, part * 512 : (part + 1) * 512] = vectors[row + part : row + part + 1, :]


def call_widen(made):
    steps = 4
    whole = [pl.BlockSpec(a.shape, lambda i: (0, 0)) for a in made]
    parts = [
        pl.BlockSpec((a.shape[0] // steps, a.shape[1]), lambda i: (i, 0)) for a in made[3:8]
    ]
    d, hidden = made[5].shape[1], made[6].shape[1]
    ends = [(1, d), (1, d), (1, d), (1, hidden)]
    outs = pl.pallas_call(
        widen_kernel,
        grid=(steps,),
        in_specs=whole[:3] + parts + whole[8:],
        out_specs=whole[:3] + parts + [pl.BlockSpec(e, lambda i: (0, 0)) for e in ends],
        out_shape=[jax.ShapeDtypeStruct(a.shape, BF) for a in made[:3]]
        + [jax.ShapeDtypeStruct(a.shape, F32) for a in made[3:8]]
        + [jax.ShapeDtypeStruct(e, F32) for e in ends],
        name="widen",
    )(*made)
    one, two, down, up = (v[0] for v in outs[8:])
    return (*outs[:8], one, two, up, down)


def local(
    sizes,
    inputs,
    skip_in,
    lengths,
    cotangent,
    w_skip,
    gain_one,
    w_qkv,
    w_out,
    gain_two,
    w_up,
    b_up,
    w_down,
    b_down,
):
    n_u, n_z, n_x = sizes
    frames, d = inputs.shape
    hidden = w_up.shape[1]
    parts = n_u * n_x
    group = frames * parts
    u, z, x = (lax.axis_index(a) for a in AXES)
    me = u * n_x + x
    width = d // parts

    def line(a, b, c):
        return (a * n_z + b) * n_x + c

    def permute(v, to):
        pairs = [
            (line(a, b, c), line(*to(a, b, c)))
            for a in range(n_u)
            for b in range(n_z)
            for c in range(n_x)
        ]
        return lax.ppermute(v, AXES, pairs)

    def plane_of(a):
        return (a % 2) * (n_u // 2) + a // 2

    group_of = {plane_of(a): a for a in range(n_u)}

    def away(v):
        return permute(v, lambda a, b, c: (b, plane_of(a), c))

    def home(v):
        return permute(v, lambda a, b, c: (group_of[b], a, c))

    def swap_plane(v, bit):
        def to(a, b, c):
            other = (a * n_x + c) ^ bit
            return other // n_x, b, other % n_x

        return permute(v, to)

    plane_bits = [1 << i for i in range(parts.bit_length() - 1)]
    if n_x == 2 and n_u == 4:
        orders = ([1, 4, 2], [4, 1, 2])
    else:
        orders = (plane_bits, plane_bits)
    cut = frames // 32 * 16

    def gather_plane(v):
        pieces = []
        for piece, order in zip((v[:cut], v[cut:]), orders):
            for bit in order:
                piece = jnp.concatenate([piece, swap_plane(piece, bit)], axis=0)
            pieces.append(piece)
        return jnp.concatenate(pieces, axis=0)

    def gather_order(v):
        pieces = []
        for start, size, order in ((0, cut, orders[0]), (cut, frames - cut, orders[1])):
            offsets = [0]
            for bit in order:
                offsets = offsets + [o ^ bit for o in offsets]
            for o in offsets:
                pieces.append(
                    lax.dynamic_slice_in_dim(v, (me ^ o) * frames + start, size, axis=0)
                )
        return jnp.concatenate(pieces, axis=0)

    z_bits = n_z.bit_length() - 1

    def reduce_z(v):
        rest = v.shape[1:]
        v = v.reshape((2,) * z_bits + (v.shape[0] // n_z,) + rest)
        for bit in range(z_bits):
            axis = z_bits - 1 - bit
            own = (z >> bit) & 1
            keep = lax.dynamic_index_in_dim(v, own, axis, keepdims=False)
            give = lax.dynamic_index_in_dim(v, 1 - own, axis, keepdims=False)
            got = permute(
                give.astype(BF), lambda a, b, c, bit=bit: (a, b ^ (1 << bit), c)
            )
            v = keep.astype(F32) + got.astype(F32)
            if bit < z_bits - 1:
                v = v.astype(BF)
        return v.astype(BF)

    def finish_columns(v):
        if n_x == 2:
            v = v.reshape((2, v.shape[0] // 2) + v.shape[1:])
            keep = lax.dynamic_index_in_dim(v, x, 0, keepdims=False)
            give = lax.dynamic_index_in_dim(v, 1 - x, 0, keepdims=False)
            got = permute(give, lambda a, b, c: (a, b, 1 - c))
            both = jnp.where(x == 0, jnp.stack([keep, got]), jnp.stack([got, keep]))
        else:
            both = v[None]
        every = lax.all_gather(both, "u", axis=0)
        return every.reshape((parts,) + both.shape[1:])

    def sum_all(v):
        total = n_u * n_z * n_x
        for i in range(total.bit_length() - 1):
            bit = 1 << i
            pairs = [(n, n ^ bit) for n in range(total)]
            v = v + lax.ppermute(v, AXES, pairs)
        return v

    entry_home = dot_nn(inputs, w_skip[:d]) + dot_nn(skip_in, w_skip[d:])
    entry = away(entry_home.astype(BF)).astype(F32)
    group_lengths = away(lengths)[0]
    grad_low = away(cotangent)
    inputs_away = away(inputs)
    skip_away = away(skip_in)

    segment, places = frame_segments(group_lengths, jnp.arange(group, dtype=jnp.int32))
    own_places = lax.dynamic_slice_in_dim(places, me * frames, frames)
    tables = rotary_tables(own_places)
    col, row = segment[:, None], segment[None, :]

    inverse_one = rms_parts(entry)
    normed_one = (entry * inverse_one * gain_one).astype(BF)
    qkv = dot_nn(normed_one, w_qkv)
    query = (rotate(qkv[:, :d], tables, 1.0)).astype(BF) * BF(HEAD_DIM**-0.5)
    keys = rotate(qkv[:, d : 2 * d], tables, 1.0).astype(BF)
    values = qkv[:, 2 * d :].astype(BF)

    def to_heads(*arrays):
        n = len(arrays)
        v = jnp.stack([a.reshape(frames, parts, width) for a in arrays], axis=2)
        v = lax.all_to_all(
            v.reshape(frames, parts * n * width), PLANE, split_axis=1, concat_axis=0, tiled=True
        )
        return [v[:, i * width : (i + 1) * width] for i in range(n)]

    def to_frames(*arrays):
        n = len(arrays)
        v = jnp.concatenate(arrays, axis=1)
        v = lax.all_to_all(v, PLANE, split_axis=0, concat_axis=1, tiled=True)
        v = v.reshape(frames, parts, n, width)
        return [v[:, :, i].reshape(frames, d) for i in range(n)]

    head_query, head_keys, head_values = to_heads(query, keys, values)
    head_mixed, lse = call_forward(head_query, head_keys, head_values, col, row)
    (mixed,) = to_frames(head_mixed)

    middle = entry + dot_nn(mixed, w_out)
    inverse_two = rms_parts(middle)
    normed_two = (middle * inverse_two * gain_two).astype(BF)
    up = dot_nn(normed_two, w_up) + b_up
    d_active = dot_nt(grad_low, w_down)
    active, slope = gelu_both(up)
    d_up = (d_active * slope).astype(BF)
    result_away = (middle + dot_nn(active.astype(BF), w_down) + b_down).astype(BF)
    result = home(result_away)
    d_normed_two = dot_nt(d_up, w_up)
    middle_part, g_gain_two = rms_back(middle, inverse_two, gain_two, d_normed_two)
    d_middle = grad_low.astype(F32) + middle_part
    d_branch = d_middle.astype(BF)
    d_mixed = dot_nt(d_branch, w_out).astype(BF)
    (head_grad,) = to_heads(d_mixed)
    dq, dk, dv = call_backward(
        head_query, head_keys, head_values, head_mixed, head_grad, col, row, lse
    )

    chunk = hidden // (n_z * parts)
    w_up_own = lax.dynamic_slice(
        w_up.reshape(d, n_z, n_x, n_u, chunk), (0, 0, x, u, 0), (d, n_z, 1, 1, chunk)
    ).reshape(d, n_z * chunk)
    w_down_own = lax.dynamic_slice(
        w_down.reshape(n_z, n_x, n_u, chunk, d), (0, x, u, 0, 0), (n_z, 1, 1, chunk, d)
    ).reshape(n_z * chunk, d)
    b_up_own = lax.dynamic_slice(
        b_up.reshape(n_z, n_x, n_u, chunk), (0, x, u, 0), (n_z, 1, 1, chunk)
    ).reshape(n_z * chunk)
    plane_grad = gather_plane(grad_low)
    plane_normed = gather_plane(normed_two)
    up_own = dot_nn(plane_normed, w_up_own) + b_up_own
    active_own, slope_own = gelu_both(up_own)
    d_up_own = (dot_nt(plane_grad, w_down_own) * slope_own).astype(BF)
    g_down = dot_tn(active_own.astype(BF), plane_grad)
    g_up = dot_tn(plane_normed, d_up_own)
    down_z = reduce_z(g_down.astype(BF))
    up_z = reduce_z(g_up.astype(BF))
    out_down = lax.all_gather(down_z, "u", axis=0, tiled=True).astype(F32)
    out_up = finish_columns(up_z)
    out_up = (
        out_up.reshape(n_u, n_x, -1, n_z, chunk).transpose(2, 3, 1, 0, 4).reshape(-1, hidden)
    ).astype(F32)

    plane_mixed = gather_plane(mixed)
    own_branch = gather_order(
        lax.all_to_all(d_branch, PLANE, split_axis=1, concat_axis=0, tiled=True)
    )
    g_out = dot_tn(plane_mixed, own_branch)
    out_out = (
        finish_columns(reduce_z(g_out.astype(BF))).transpose(1, 0, 2).reshape(-1, d).astype(F32)
    )

    low = [a.astype(BF) for a in (dq, dk, dv)]
    frame_query, frame_keys, frame_values = to_frames(*low)
    d_qkv = jnp.concatenate(
        [
            rotate(frame_query.astype(F32), tables, -1.0).astype(BF),
            rotate(frame_keys.astype(F32), tables, -1.0).astype(BF),
            frame_values,
        ],
        axis=1,
    )
    d_normed_one = dot_nt(d_qkv, w_qkv)
    entry_part, g_gain_one = rms_back(entry, inverse_one, gain_one, d_normed_one)
    d_entry = (d_middle + entry_part).astype(BF)
    d_entry_home = home(d_entry)
    d_joined = dot_nt(d_entry_home, w_skip)
    d_inputs = d_joined[:, :d].astype(BF)
    d_skip = d_joined[:, d:].astype(BF)

    group_tables = rotary_tables(places)
    head_d_qkv = jnp.concatenate(
        [
            rotate(low[0].astype(F32), group_tables, -1.0).astype(BF),
            rotate(low[1].astype(F32), group_tables, -1.0).astype(BF),
            low[2],
        ],
        axis=1,
    )
    plane_first = gather_plane(normed_one)
    g_qkv = dot_tn(plane_first, gather_order(head_d_qkv))
    plane_inputs = gather_plane(inputs_away)
    plane_skip = gather_plane(skip_away)
    own_entry = gather_order(
        lax.all_to_all(d_entry, PLANE, split_axis=1, concat_axis=0, tiled=True)
    )
    g_skip = jnp.concatenate([dot_tn(plane_inputs, own_entry), dot_tn(plane_skip, own_entry)])
    out_qkv = finish_columns(reduce_z(g_qkv.astype(BF)))
    out_qkv = (
        out_qkv.reshape(parts, -1, 3, width).transpose(1, 2, 0, 3).reshape(-1, 3 * d).astype(F32)
    )
    out_skip = (
        finish_columns(reduce_z(g_skip.astype(BF))).transpose(1, 0, 2).reshape(-1, d).astype(F32)
    )

    early = sum_all(
        jnp.concatenate(
            [
                g_gain_two,
                jnp.sum(d_up.astype(F32), axis=0),
                jnp.sum(cotangent.astype(F32), axis=0),
            ]
        )
    )
    total_gain_one = sum_all(g_gain_one)
    return (
        result,
        d_inputs,
        d_skip,
        out_skip,
        total_gain_one,
        out_qkv,
        out_out,
        early[:d],
        out_up,
        early[d : d + hidden],
        out_down,
        early[d + hidden :],
    )


def local_fast(
    sizes,
    inputs,
    skip_in,
    lengths,
    cotangent,
    w_skip,
    gain_one,
    w_qkv,
    w_out,
    gain_two,
    w_up,
    b_up,
    w_down,
    b_down,
):
    made = call_layer(
        (inputs, skip_in, cotangent, w_skip, w_qkv, w_out, w_up, w_down),
        lengths,
        (gain_one[None], gain_two[None], b_up[None], b_down[None]),
    )
    (
        result,
        d_inputs,
        d_skip,
        g_skip,
        g_qkv,
        g_out,
        g_up,
        g_down,
        total_one,
        total_two,
        total_up,
        total_down,
    ) = call_widen(made)
    return (
        result,
        d_inputs,
        d_skip,
        g_skip,
        total_one,
        g_qkv,
        g_out,
        total_two,
        g_up,
        total_up,
        g_down,
        total_down,
    )


def solution(mesh):
    n_u, n_s = mesh.shape["utt"], mesh.shape["seq"]
    sizes = (n_u, n_u, n_s // n_u)
    program = local_fast if sizes == (4, 4, 2) else local
    inner = Mesh(mesh.devices.reshape(sizes), AXES)
    rows, seq = P(AXES, None), P(("z", "x"), None)
    in_specs = (rows, rows, P("u", None), rows) + (P(),) * 9
    out_specs = (rows, rows, rows, seq, P(), seq, seq, P(), seq, P(), seq, P())
    return jax.shard_map(
        functools.partial(program, sizes),
        mesh=inner,
        in_specs=in_specs,
        out_specs=out_specs,
        check_vma=False,
    )
```
